32 devices in a mesh: seq: 8 (over z, core), grp: 4 (over y, x).
Axes of the slice: x: 2, y: 2, z: 4, core: 2. Of those that a mesh axis runs over, the one named last changes fastest.
Arguments:
- inputs: bfloat16 [4, 4096, 576], P('grp', 'seq'), may hold values from -6 to 6
- lengths: int32 [4], P('grp'), may hold values from 2049 to 4096, as said below
- attn_gain: float32 [576], replicated, may hold values from 0.5 to 1.5
- w_query: bfloat16 [576, 576], replicated, may hold values from -0.25 to 0.25
- w_key: bfloat16 [576, 192], replicated, may hold values from -0.25 to 0.25
- w_value: bfloat16 [576, 192], replicated, may hold values from -0.25 to 0.25
- w_out: bfloat16 [576, 576], replicated, may hold values from -6 to 6
- ffn_gain: float32 [576], replicated, may hold values from 0.5 to 1.5
- w_gate: bfloat16 [576, 1536], replicated, may hold values from -0.25 to 0.25
- w_up: bfloat16 [576, 1536], replicated, may hold values from -0.25 to 0.25
- w_down: bfloat16 [1536, 576], replicated, may hold values from -0.15625 to 0.15625
- cotangent: bfloat16 [4, 4096, 576], P('grp', 'seq'), may hold values from -6 to 6
Outputs:
- outputs: bfloat16 [4, 4096, 576], P('grp', 'seq')
- d_inputs: bfloat16 [4, 4096, 576], P('grp', 'seq')
- d_attn_gain: float32 [576], replicated
- d_query: float32 [576, 576], replicated
- d_key: float32 [576, 192], replicated
- d_value: float32 [576, 192], replicated
- d_out: float32 [576, 576], replicated
- d_ffn_gain: float32 [576], replicated
- d_gate: float32 [576, 1536], replicated
- d_up: float32 [576, 1536], replicated
- d_down: float32 [1536, 576], replicated
The draws below stay inside these ranges and needn't reach their ends.
Inputs may be any that keep to these rules, and one draw needn't show every extreme that they name: `lengths`: some sequence fills all 4096 slots and another holds exactly 2049 tokens.
All inputs are finite; a program needn't handle non-finite values.
Results may differ from the reference program's by a relative error of at most 0.018.
Values may be sent and summed in bfloat16 or wider, within the bound.
No kernel may reach another device: no remote copies, remote signals or barrier semaphores. Data moves between devices by JAX's collectives and lax.ppermute only.
A program may use at most 128 MiB of HBM per device.

```python
import math
import jax
import jax.numpy as jnp
from jax import lax

D = 576
KV_HEADS = 3
HEAD_DIM = 64
FF = 1536
REP = 3
KVD = 192
LEN = 4096
SEQS = 4


def draw_lengths(key, part):
    key = jax.random.fold_in(key, 7)
    cut_key, full_key = jax.random.split(key)
    half_len = LEN // 2
    shortfall = jax.random.randint(cut_key, (SEQS,), 0, half_len)
    chosen = jax.random.randint(full_key, (), 0, SEQS)
    slots = jnp.arange(SEQS)
    shortfall = jnp.where(slots == chosen, 0, shortfall)
    shortfall = jnp.where(slots == (chosen + 1) % SEQS, half_len - 1, shortfall)
    return (LEN - shortfall).astype(jnp.int32)


def level_of(stream_key, shape, cuts, least, largest):
    level = 1.0
    for position, blocks in cuts:
        heights = jax.random.uniform(jax.random.fold_in(jax.random.fold_in(stream_key, 6), position), (blocks,), jnp.float32, least / len(cuts), largest / len(cuts))
        level = level * jnp.repeat(jnp.exp(heights), shape[position] // blocks).reshape((-1,) + (1,) * (len(shape) - 1 - position))
    return level


def bell_draw(key, extent, width, reach, cuts=(), held_as=jnp.bfloat16):
    array = jax.random.normal(key, extent, jnp.float32) * width
    if len(cuts) > 0:
        array = level_of(key, extent, cuts, -0.22, 0.18) * array
    return jnp.clip(array, min=-reach, max=reach).astype(held_as)


def setup_inputs(seed: int = 0) -> dict:
    arg_keys = jax.random.split(jax.random.key(seed), 13)
    inputs = bell_draw(arg_keys[0], (SEQS, LEN, D), 1.0, 6.0, ((0, 4), (1, 8)))
    lengths = draw_lengths(jax.random.fold_in(arg_keys[12], 71), 0)
    attn_gain = jnp.clip(1.0 + 0.1 * jax.random.normal(arg_keys[2], (D,), jnp.float32), 0.5, 1.5)
    w_query = bell_draw(arg_keys[3], (D, D), D ** -0.5, 0.25)
    w_key = bell_draw(arg_keys[4], (D, KVD), D ** -0.5, 0.25)
    w_value = bell_draw(arg_keys[5], (D, KVD), D ** -0.5, 0.25)
    w_out = bell_draw(arg_keys[6], (D, D), (max(D * 8 // LEN, 1)) ** -0.5, 6.0)
    ffn_gain = jnp.clip(1.0 + 0.1 * jax.random.normal(arg_keys[7], (D,), jnp.float32), 0.5, 1.5)
    w_gate = bell_draw(arg_keys[8], (D, FF), D ** -0.5, 0.25)
    w_up = bell_draw(arg_keys[9], (D, FF), D ** -0.5, 0.25)
    w_down = bell_draw(arg_keys[10], (FF, D), FF ** -0.5, 0.15625)
    cotangent = bell_draw(arg_keys[11], (SEQS, LEN, D), 1.0, 6.0, ((0, 4), (1, 8)))
    return {"inputs": inputs, "lengths": lengths, "attn_gain": attn_gain, "w_query": w_query, "w_key": w_key, "w_value": w_value, "w_out": w_out, "ffn_gain": ffn_gain, "w_gate": w_gate, "w_up": w_up, "w_down": w_down, "cotangent": cotangent}


epsilon = 1e-05
rope_base = 100000.0
neg_big = -1e+30

@jax.custom_vjp
def low(v):
    return lax.optimization_barrier(v.astype(jnp.bfloat16)).astype(jnp.float32)

@jax.custom_vjp
def low_back(v):
    return v

def low_keep(v):
    return (low(v), None)

def low_pass(kept, grad):
    return (grad,)

def back_keep(v):
    return (v, None)

def back_low(kept, grad):
    return (low(grad),)
low.defvjp(low_keep, low_pass)
low_back.defvjp(back_keep, back_low)

def matmul(left, right):
    return jnp.dot(left, right, precision=lax.Precision.HIGHEST, preferred_element_type=jnp.float32)

def angles_for(positions):
    half_dim = HEAD_DIM // 2
    frequencies = 1.0 / rope_base ** (jnp.arange(half_dim, dtype=jnp.float32) * 2.0 / HEAD_DIM)
    angles = positions.astype(jnp.float32)[:, None] * frequencies[None, :]
    return (jnp.cos(angles), jnp.sin(angles))

def rotate(values, cos_table, sine_table):
    half_dim = values.shape[-1] // 2
    table_shape = (cos_table.shape[0],) + (1,) * (values.ndim - 2) + (half_dim,)
    cos_table = cos_table.reshape(table_shape)
    sine_table = sine_table.reshape(table_shape)
    first_half = values[..., :half_dim]
    second_half = values[..., half_dim:]
    return jnp.concatenate([first_half * cos_table - second_half * sine_table, second_half * cos_table + first_half * sine_table], axis=-1)

def rms_norm(values, gain_vec):
    scaling = lax.rsqrt(lax.optimization_barrier(jnp.mean(values * values, axis=-1, keepdims=True)) + epsilon)
    return values * scaling * gain_vec

def forward(inputs, length, params):
    attn_gain, w_query, w_key, w_value, w_out, ffn_gain, w_gate, w_up, w_down = params
    positions = jnp.arange(LEN, dtype=jnp.int32)
    cos_table, sine_table = angles_for(positions)
    normed = low(rms_norm(inputs, attn_gain))
    query_proj = low_back(matmul(normed, w_query)).reshape(LEN, KV_HEADS, REP, HEAD_DIM)
    key_proj = low_back(matmul(normed, w_key)).reshape(LEN, KV_HEADS, HEAD_DIM)
    value_low = low(low_back(matmul(normed, w_value))).reshape(LEN, KV_HEADS, HEAD_DIM)
    query_rot = low(rotate(query_proj, cos_table, sine_table) * HEAD_DIM ** (-0.5))
    key_rot = low(rotate(key_proj, cos_table, sine_table))
    tile_rows = math.gcd(LEN, 512)
    query_tiles = query_rot.reshape(LEN // tile_rows, tile_rows, KV_HEADS, REP, HEAD_DIM)
    tile_starts = jnp.arange(LEN // tile_rows, dtype=jnp.int32) * tile_rows
    key_pos = jnp.arange(LEN, dtype=jnp.int32)

    def attend(query_tile, begin_at):
        query_pos = begin_at + jnp.arange(tile_rows, dtype=jnp.int32)
        scores = low_back(jnp.einsum('qngd,knd->ngqk', query_tile, key_rot, precision=lax.Precision.HIGHEST, preferred_element_type=jnp.float32))
        visible = (key_pos[None, :] <= query_pos[:, None]) & (key_pos[None, :] < length)
        masked = jnp.where(visible, scores, neg_big)
        row_max = lax.optimization_barrier(jnp.max(masked, axis=-1, keepdims=True))
        weights = jnp.where(visible, jnp.exp(masked - row_max), 0.0)
        probabilities = weights / lax.optimization_barrier(jnp.sum(weights, axis=-1, keepdims=True))
        return jnp.einsum('ngqk,knd->qngd', low(probabilities), value_low, precision=lax.Precision.HIGHEST, preferred_element_type=jnp.float32)
    checked = jax.checkpoint(attend)

    def attend_pair(bundle):
        return checked(bundle[0], bundle[1])
    attended = lax.map(attend_pair, (query_tiles, tile_starts))
    mixed_low = low(low_back(attended.reshape(LEN, D)))
    residual = inputs + low_back(matmul(mixed_low, w_out))
    normed_two = low(rms_norm(residual, ffn_gain))
    gate_pre = low_back(matmul(normed_two, w_gate))
    upward = low_back(matmul(normed_two, w_up))
    hidden = low(gate_pre * jax.nn.sigmoid(gate_pre) * upward)
    return residual + matmul(hidden, w_down)

def reference(inputs, lengths, attn_gain, w_query, w_key, w_value, w_out, ffn_gain, w_gate, w_up, w_down, cotangent):
    params = (attn_gain.astype(jnp.float32), w_query.astype(jnp.float32), w_key.astype(jnp.float32), w_value.astype(jnp.float32), w_out.astype(jnp.float32), ffn_gain.astype(jnp.float32), w_gate.astype(jnp.float32), w_up.astype(jnp.float32), w_down.astype(jnp.float32))

    def per_sequence(totals, bundle):
        seq_inputs, seq_length, seq_cot = bundle

        def layer(first_arg, *weight_list):
            return forward(first_arg, seq_length, weight_list)
        layer_out, pull = jax.vjp(layer, seq_inputs.astype(jnp.float32), *params)
        gradients = pull(seq_cot.astype(jnp.float32))
        totals = tuple((summed + addend for summed, addend in zip(totals, gradients[1:])))
        return (totals, (layer_out.astype(jnp.bfloat16), gradients[0].astype(jnp.bfloat16)))
    zero_grads = tuple((jnp.zeros(element.shape, jnp.float32) for element in params))
    totals, (layer_out, d_inputs) = lax.scan(per_sequence, zero_grads, (inputs, lengths, cotangent))
    return (layer_out, d_inputs, totals[0], totals[1], totals[2], totals[3], totals[4], totals[5], totals[6], totals[7], totals[8])
```

```python
import functools
import math

import jax
import jax.numpy as jnp
import numpy as np
from jax import lax
from jax.experimental import pallas as pl
from jax.experimental.pallas import tpu as pltpu
from jax.sharding import PartitionSpec as P

D = 576
KV_HEADS = 3
HEAD_DIM = 64
REP = 3
HEADS = KV_HEADS * REP
KVD = 192
FF = 1536
CHUNK = 512
STACK = 2048
HALF = HEAD_DIM // 2

epsilon = 1e-05
rope_base = 100000.0
neg_big = -1e30
log2e = math.log2(math.e)
ln2 = math.log(2.0)

F32 = jnp.float32
BF16 = jnp.bfloat16
VMEM_LIMIT = 60 * 2**20


def mm(left, right, left_dim, right_dim):
    return lax.dot_general(
        left, right, (((left_dim,), (right_dim,)), ((), ())), preferred_element_type=F32
    )


def params():
    return pltpu.CompilerParams(vmem_limit_bytes=VMEM_LIMIT)


def whole(shape):
    return pl.BlockSpec(shape, lambda *_: (0,) * len(shape))


def cost(flops, nbytes, exps=0):
    return pl.CostEstimate(flops=int(flops), bytes_accessed=int(nbytes), transcendentals=int(exps))


def rope_tables(length):
    steps = np.arange(HALF, dtype=np.float32)
    freqs = (1.0 / np.float32(rope_base) ** (steps * np.float32(2.0) / np.float32(HEAD_DIM))).astype(
        np.float32
    )
    angles = np.arange(length, dtype=np.float32)[None, :] * freqs[:, None]
    return np.cos(angles).astype(np.float32), np.sin(angles).astype(np.float32)


def rotated(rows, cos, sin, scale, sign):
    parts = []
    for start in range(0, rows.shape[0], HEAD_DIM):
        one = rows[start : start + HALF]
        two = rows[start + HALF : start + HEAD_DIM]
        parts.append((one * cos - sign * (two * sin)) * scale)
        parts.append((two * cos + sign * (one * sin)) * scale)
    return jnp.concatenate(parts, 0)


def first_kernel(sc, x_ref, gain_ref, wq_ref, wk_ref, wv_ref, cos_ref, sin_ref, n_ref, q_ref, kv_ref):
    x = x_ref[...].astype(F32)
    scale = lax.rsqrt(jnp.mean(x * x, axis=1, keepdims=True) + epsilon)
    normed = (x * scale * gain_ref[...]).astype(BF16)
    normed_t = normed.T
    n_ref[...] = normed_t
    cos = cos_ref[...]
    sin = sin_ref[...]
    key = mm(wk_ref[...].T, normed_t, 1, 0)
    kv_ref[:KVD, :] = rotated(key, cos, sin, 1.0, 1.0).astype(BF16)
    kv_ref[KVD:, :] = mm(wv_ref[...].T, normed_t, 1, 0).astype(BF16)
    query = mm(wq_ref[...].T, normed_t, 1, 0)
    q_ref[...] = rotated(query, cos, sin, HEAD_DIM**-0.5 * log2e, 1.0).astype(BF16)


def first(sc, x, gain, wq, wk, wv, cos, sin):
    rows = x.shape[0]
    return pl.pallas_call(
        first_kernel,
        grid_spec=pltpu.PrefetchScalarGridSpec(
            num_scalar_prefetch=1,
            grid=(1,),
            in_specs=[
                whole(x.shape),
                whole(gain.shape),
                whole(wq.shape),
                whole(wk.shape),
                whole(wv.shape),
                pl.BlockSpec((HALF, rows), lambda i, sc: (0, sc[0])),
                pl.BlockSpec((HALF, rows), lambda i, sc: (0, sc[0])),
            ],
            out_specs=[whole((D, rows)), whole((D, rows)), whole((2 * KVD, rows))],
        ),
        out_shape=[
            jax.ShapeDtypeStruct((D, rows), BF16),
            jax.ShapeDtypeStruct((D, rows), BF16),
            jax.ShapeDtypeStruct((2 * KVD, rows), BF16),
        ],
        compiler_params=params(),
        cost_estimate=cost(2 * rows * D * (D + 2 * KVD), 4 * 2**20),
        name="first",
    )(sc, x, gain, wq, wk, wv, cos, sin)


def block_facts(sc, rank, which, rows):
    mine = sc[0]
    block = mine - 2 * rank if which == 0 else (mine ^ 1) - 2 * rank
    length = sc[1]
    start = block * rows
    active = (block >= 0) & (block <= mine) & (start < length)
    partial = (block == mine) | (start + rows > length)
    pos = mine * rows + lax.broadcasted_iota(jnp.int32, (1, rows), 1)
    bound = jnp.minimum(pos, length - 1) - start
    return active, partial, bound


def masked_scores(scores, bound):
    rows = lax.broadcasted_iota(jnp.int32, scores.shape, 0)
    return jnp.where(rows <= bound, scores, neg_big)


def forward_block(hidden_keys, bound, kv_ref, q_ref, m_ref, l_ref, acc_ref):
    rows = q_ref.shape[1]
    keys = kv_ref[:KVD, :].T
    ones = jnp.ones((8, rows), BF16)

    def score(head):
        kv = head // REP
        scores = mm(
            keys[:, kv * HEAD_DIM : (kv + 1) * HEAD_DIM],
            q_ref[head * HEAD_DIM : (head + 1) * HEAD_DIM, :],
            1,
            0,
        )
        if hidden_keys:
            scores = masked_scores(scores, bound)
        return scores, jnp.max(scores, axis=0, keepdims=True)

    def weigh(head, scores, top):
        kv = head // REP
        old = m_ref[head : head + 1, :]
        new = jnp.maximum(old, top)
        weights = jnp.exp2(scores - new).astype(BF16)
        values = jnp.concatenate(
            [kv_ref[KVD + kv * HEAD_DIM : KVD + (kv + 1) * HEAD_DIM, :], ones], 0
        )
        return new, jnp.exp2(old - new), mm(values, weights, 1, 0)

    def store(head, new, fade, out):
        rows_of = slice(head * HEAD_DIM, (head + 1) * HEAD_DIM)
        m_ref[head : head + 1, :] = new
        l_ref[head : head + 1, :] = l_ref[head : head + 1, :] * fade + out[HEAD_DIM : HEAD_DIM + 1]
        acc_ref[rows_of, :] = acc_ref[rows_of, :] * fade + out[:HEAD_DIM]

    ahead = score(0)
    held = None
    for head in range(HEADS):
        current = ahead
        if head + 1 < HEADS:
            ahead = score(head + 1)
        result = weigh(head, *current)
        if held is not None:
            store(*held)
        held = (head,) + result
    store(*held)


def forward_kernel(sc, q_ref, a_ref, b_ref, *refs, rank, fresh):
    rows = q_ref.shape[1]
    which = pl.program_id(0)
    m_ref, l_ref, acc_ref, kv_ref = refs[-4:]

    @pl.when(which == 0)
    def _():
        if fresh:
            m_ref[...] = jnp.full_like(m_ref, neg_big)
            l_ref[...] = jnp.zeros_like(l_ref)
            acc_ref[...] = jnp.zeros_like(acc_ref)
        else:
            m_ref[...] = refs[0][...]
            l_ref[...] = refs[1][...]
            acc_ref[...] = refs[2][...]
        kv_ref[...] = a_ref[...]

    @pl.when(which == 1)
    def _():
        kv_ref[...] = b_ref[...]

    first_facts = block_facts(sc, rank, 0, rows)
    second_facts = block_facts(sc, rank, 1, rows)
    active, partial, bound = [
        jnp.where(which == 0, one, two) for one, two in zip(first_facts, second_facts)
    ]

    @pl.when(active & jnp.logical_not(partial))
    def _():
        forward_block(False, bound, kv_ref, q_ref, m_ref, l_ref, acc_ref)

    @pl.when(active & partial)
    def _():
        forward_block(True, bound, kv_ref, q_ref, m_ref, l_ref, acc_ref)


def forward(sc, q, a, b, state, rank):
    rows = q.shape[1]
    state = () if state is None else tuple(state)
    return pl.pallas_call(
        functools.partial(forward_kernel, rank=rank, fresh=not state),
        grid_spec=pltpu.PrefetchScalarGridSpec(
            num_scalar_prefetch=1,
            grid=(2,),
            in_specs=[whole(q.shape), whole(a.shape), whole(b.shape)]
            + [whole(part.shape) for part in state],
            out_specs=[whole((16, rows)), whole((16, rows)), whole((D, rows))],
            scratch_shapes=[pltpu.VMEM(a.shape, BF16)],
        ),
        out_shape=[
            jax.ShapeDtypeStruct((16, rows), F32),
            jax.ShapeDtypeStruct((16, rows), F32),
            jax.ShapeDtypeStruct((D, rows), F32),
        ],
        compiler_params=params(),
        cost_estimate=cost(2 * 16 * rows * rows * D, 4 * 2**20, 2 * HEADS * rows * rows),
        name=f"forward_{rank}",
    )(sc, q, a, b, *state)


def backward_block(hidden_keys, bound, kv_ref, q_ref, do_ref, lse_ref, delta_ref, dq_ref, out_ref):
    keys = kv_ref[:KVD, :].T
    values = kv_ref[KVD:, :].T
    for kv in range(KV_HEADS):
        lanes = slice(kv * HEAD_DIM, (kv + 1) * HEAD_DIM)
        d_key = None
        d_value = None
        for rep in range(REP):
            head = kv * REP + rep
            rows_of = slice(head * HEAD_DIM, (head + 1) * HEAD_DIM)
            query = q_ref[rows_of, :]
            d_out = do_ref[rows_of, :]
            scores = mm(keys[:, lanes], query, 1, 0)
            if hidden_keys:
                scores = masked_scores(scores, bound)
            d_probs = mm(values[:, lanes], d_out, 1, 0)
            probs = jnp.exp2(scores - lse_ref[head : head + 1, :])
            d_scores = (probs * (d_probs - delta_ref[head : head + 1, :])).astype(BF16)
            value_term = mm(probs.astype(BF16), d_out, 1, 1)
            key_term = mm(d_scores, query, 1, 1)
            d_value = value_term if d_value is None else d_value + value_term
            d_key = key_term if d_key is None else d_key + key_term
            dq_ref[rows_of, :] = dq_ref[rows_of, :] + mm(
                kv_ref[kv * HEAD_DIM : (kv + 1) * HEAD_DIM, :], d_scores, 1, 0
            )
        out_ref[kv] = jnp.concatenate([d_key, d_value], 1).astype(BF16)


def backward_kernel(
    sc, q_ref, do_ref, lse_ref, delta_ref, a_ref, b_ref, *refs, rank, fresh
):
    rows = q_ref.shape[1]
    which = pl.program_id(0)
    dq_ref, ga_ref, gb_ref, kv_ref, out_ref = refs[-5:]

    @pl.when(which == 0)
    def _():
        if fresh:
            dq_ref[...] = jnp.zeros_like(dq_ref)
        else:
            dq_ref[...] = refs[0][...]
        kv_ref[...] = b_ref[...]

    @pl.when(which == 1)
    def _():
        kv_ref[...] = a_ref[...]

    first_facts = block_facts(sc, rank, 1, rows)
    second_facts = block_facts(sc, rank, 0, rows)
    active, partial, bound = [
        jnp.where(which == 0, one, two) for one, two in zip(first_facts, second_facts)
    ]
    rest = (kv_ref, q_ref, do_ref, lse_ref, delta_ref, dq_ref, out_ref)

    @pl.when(active & jnp.logical_not(partial))
    def _():
        backward_block(False, bound, *rest)

    @pl.when(active & partial)
    def _():
        backward_block(True, bound, *rest)

    @pl.when(jnp.logical_not(active))
    def _():
        out_ref[...] = jnp.zeros_like(out_ref)

    @pl.when(which == 0)
    def _():
        gb_ref[...] = out_ref[...]

    @pl.when(which == 1)
    def _():
        ga_ref[...] = out_ref[...]


def backward(sc, q, d_out, lse, delta, a, b, dq, rank):
    rows = q.shape[1]
    state = () if dq is None else (dq,)
    grads = (KV_HEADS, rows, 2 * HEAD_DIM)
    return pl.pallas_call(
        functools.partial(backward_kernel, rank=rank, fresh=not state),
        grid_spec=pltpu.PrefetchScalarGridSpec(
            num_scalar_prefetch=1,
            grid=(2,),
            in_specs=[whole(part.shape) for part in (q, d_out, lse, delta, a, b) + state],
            out_specs=[whole((D, rows)), whole(grads), whole(grads)],
            scratch_shapes=[pltpu.VMEM(a.shape, BF16), pltpu.VMEM(grads, BF16)],
        ),
        out_shape=[
            jax.ShapeDtypeStruct((D, rows), F32),
            jax.ShapeDtypeStruct(grads, BF16),
            jax.ShapeDtypeStruct(grads, BF16),
        ],
        compiler_params=params(),
        cost_estimate=cost(2 * 40 * rows * rows * D, 5 * 2**20, 2 * HEADS * rows * rows),
        name=f"backward_{rank}",
    )(sc, q, d_out, lse, delta, a, b, *state)


def store_rows(out_ref, table, chunk, base, values):
    pieces = out_ref.shape[1]
    rows = out_ref.shape[2]
    for start in range(0, values.shape[0], rows):
        piece = (base + start) // rows
        out_ref[chunk, table[chunk * pieces + piece], :, : values.shape[1]] = values[
            start : start + rows
        ].astype(BF16)


def middle_kernel(
    table,
    acc_ref,
    m_ref,
    l_ref,
    x_ref,
    cot_ref,
    gain_ref,
    wo_ref,
    wg_ref,
    wu_ref,
    wd_ref,
    y_ref,
    do_ref,
    lse_ref,
    delta_ref,
    dh_ref,
    grads_ref,
    mixed_ref,
    h_ref,
    n_ref,
    nt_ref,
    ct_ref,
    out_ref,
    dn_ref,
):
    chunk = pl.program_id(0)

    @pl.when(chunk == 0)
    def _():
        for head in range(HEADS):
            rows_of = slice(head * HEAD_DIM, (head + 1) * HEAD_DIM)
            mixed_ref[rows_of, :] = acc_ref[rows_of, :] * (1.0 / l_ref[head : head + 1, :])
        lse_ref[:HEADS, :] = m_ref[:HEADS, :] + jnp.log2(l_ref[:HEADS, :])
        mixed_low = mixed_ref[...].astype(BF16)
        h = x_ref[...].astype(F32) + mm(mixed_low.T, wo_ref[...], 1, 0)
        h_ref[...] = h
        scale = lax.rsqrt(jnp.mean(h * h, axis=1, keepdims=True) + epsilon)
        normed = (h * scale * gain_ref[...]).astype(BF16)
        n_ref[...] = normed
        nt_ref[...] = normed.T
        ct_ref[...] = cot_ref[...].T
        out_ref[...] = h

    normed = n_ref[...]
    cot = cot_ref[...]
    gate = mm(normed, wg_ref[...], 1, 0)
    up = mm(normed, wu_ref[...], 1, 0)
    d_hidden = mm(cot, wd_ref[...], 1, 1)
    sig = 1.0 / (1.0 + jnp.exp2(gate * -log2e))
    silu = gate * sig
    hidden = (silu * up).astype(BF16)
    d_gate = (d_hidden * up * (sig * (1.0 + gate * (1.0 - sig)))).astype(BF16)
    d_up = (d_hidden * silu).astype(BF16)
    out_ref[...] += mm(hidden, wd_ref[...], 1, 0)
    d_normed = mm(d_gate, wg_ref[...], 1, 1) + mm(d_up, wu_ref[...], 1, 1)

    @pl.when(chunk == 0)
    def _():
        dn_ref[...] = d_normed

    @pl.when(chunk != 0)
    def _():
        dn_ref[...] += d_normed

    store_rows(grads_ref, table, chunk, 0, mm(nt_ref[...], d_gate, 1, 0))
    store_rows(grads_ref, table, chunk, D, mm(nt_ref[...], d_up, 1, 0))
    store_rows(grads_ref, table, chunk, 2 * D, mm(ct_ref[...], hidden, 1, 0))

    @pl.when(chunk == pl.num_programs(0) - 1)
    def _():
        y_ref[...] = out_ref[...].astype(BF16)
        h = h_ref[...]
        scale = lax.rsqrt(jnp.mean(h * h, axis=1, keepdims=True) + epsilon)
        unit = h * scale
        dn = dn_ref[...]
        gain_row = jnp.sum(dn * unit, axis=0, keepdims=True)
        scaled = dn * gain_ref[...]
        dh = cot_ref[...].astype(F32) + scale * (
            scaled - unit * jnp.mean(scaled * unit, axis=1, keepdims=True)
        )
        dh_ref[...] = dh
        dh_low = dh.astype(BF16)
        mixed = mixed_ref[...]
        d_mixed = mm(wo_ref[...], dh_low, 1, 1).astype(BF16)
        do_ref[...] = d_mixed
        for head in range(HEADS):
            rows_of = slice(head * HEAD_DIM, (head + 1) * HEAD_DIM)
            delta_ref[head : head + 1, :] = jnp.sum(
                d_mixed[rows_of].astype(F32) * mixed[rows_of], axis=0, keepdims=True
            )
        d_wo = mm(mixed.astype(BF16), dh_low, 1, 0)
        third = D // 3
        tail = STACK - 3 * D - third
        for k in range(3):
            part = d_wo[k * third : (k + 1) * third]
            store_rows(grads_ref, table, k, 3 * D, part[:, :CHUNK])
            lanes = part[:, CHUNK:]
            left = lanes[:tail]
            right = jnp.concatenate(
                [lanes[tail:], jnp.zeros((2 * tail - third, D - CHUNK), F32)], 0
            )
            gain_part = (
                gain_row[:, : CHUNK - 128]
                if k == 0
                else jnp.concatenate(
                    [gain_row[:, CHUNK - 128 :], jnp.zeros((1, 2 * (CHUNK - 128) - D), F32)], 1
                )
            )
            store_rows(
                grads_ref,
                table,
                k,
                3 * D + third,
                jnp.concatenate(
                    [left, right, jnp.broadcast_to(gain_part, (tail, CHUNK - 128))], 1
                ),
            )


def middle(table, acc, m, l, x, cot, gain, wo, wg, wu, wd):
    rows = x.shape[0]
    pieces = table.shape[0] // (FF // CHUNK)
    grads = (FF // CHUNK, pieces, STACK // pieces, CHUNK)
    cols = pl.BlockSpec((D, CHUNK), lambda i, t: (0, i))
    return pl.pallas_call(
        middle_kernel,
        grid_spec=pltpu.PrefetchScalarGridSpec(
            num_scalar_prefetch=1,
            grid=(FF // CHUNK,),
            in_specs=[
                whole(acc.shape),
                whole(m.shape),
                whole(l.shape),
                whole(x.shape),
                whole(cot.shape),
                whole(gain.shape),
                whole(wo.shape),
                cols,
                cols,
                pl.BlockSpec((CHUNK, D), lambda i, t: (i, 0)),
            ],
            out_specs=[
                whole((rows, D)),
                whole((D, rows)),
                whole((16, rows)),
                whole((16, rows)),
                whole((rows, D)),
                whole(grads),
            ],
            scratch_shapes=[
                pltpu.VMEM((D, rows), F32),
                pltpu.VMEM((rows, D), F32),
                pltpu.VMEM((rows, D), BF16),
                pltpu.VMEM((D, rows), BF16),
                pltpu.VMEM((D, rows), BF16),
                pltpu.VMEM((rows, D), F32),
                pltpu.VMEM((rows, D), F32),
            ],
        ),
        out_shape=[
            jax.ShapeDtypeStruct((rows, D), BF16),
            jax.ShapeDtypeStruct((D, rows), BF16),
            jax.ShapeDtypeStruct((16, rows), F32),
            jax.ShapeDtypeStruct((16, rows), F32),
            jax.ShapeDtypeStruct((rows, D), F32),
            jax.ShapeDtypeStruct(grads, BF16),
        ],
        compiler_params=params(),
        cost_estimate=cost(18 * rows * D * FF, 24 * 2**20, rows * FF),
        name="middle",
    )(table, acc, m, l, x, cot, gain, wo, wg, wu, wd)


def last_kernel(
    sc,
    dq_ref,
    dkv_ref,
    n_ref,
    x_ref,
    dh_ref,
    gain_ref,
    wq_ref,
    wk_ref,
    wv_ref,
    cos_ref,
    sin_ref,
    dx_ref,
    grads_ref,
):
    cos = cos_ref[...]
    sin = sin_ref[...]
    d_query = rotated(dq_ref[...], cos, sin, HEAD_DIM**-0.5, -1.0).astype(BF16)
    turned = [dkv_ref[kv].astype(F32).T for kv in range(KV_HEADS)]
    d_key = rotated(
        jnp.concatenate([part[:HEAD_DIM] for part in turned], 0), cos, sin, ln2, -1.0
    ).astype(BF16)
    d_value = jnp.concatenate([part[HEAD_DIM:] for part in turned], 0).astype(BF16)
    dn_t = (
        mm(wq_ref[...], d_query, 1, 0)
        + mm(wk_ref[...], d_key, 1, 0)
        + mm(wv_ref[...], d_value, 1, 0)
    )
    dn = dn_t.T
    x = x_ref[...].astype(F32)
    scale = lax.rsqrt(jnp.mean(x * x, axis=1, keepdims=True) + epsilon)
    unit = x * scale
    product = dn * unit
    scaled = dn * gain_ref[...]
    dx_ref[...] = (
        dh_ref[...] + scale * (scaled - unit * jnp.mean(scaled * unit, axis=1, keepdims=True))
    ).astype(BF16)
    rows = x.shape[0]
    whole_grad = mm(n_ref[...], jnp.concatenate([d_query, d_key, d_value], 0), 1, 1)
    gain_col = jnp.broadcast_to(
        jnp.sum(product, axis=0, keepdims=True), (8, D)
    ).T
    width = D + 2 * KVD
    padded = jnp.concatenate([whole_grad, jnp.broadcast_to(gain_col[:, :1], (D, 64))], 1).astype(BF16)
    pieces, piece_rows, lanes = grads_ref.shape
    across = (width + 64) // lanes
    for piece in range(pieces):
        top = (piece // across) * piece_rows
        left = (piece % across) * lanes
        count = min(piece_rows, D - top)
        where = sc[2 + piece]
        if count < piece_rows:
            grads_ref[where] = jnp.zeros((piece_rows, lanes), BF16)
        if count > 0:
            grads_ref[where, :count] = padded[top : top + count, left : left + lanes]


def last_shape(pieces):
    across = 8
    down = max(pieces // across, 1)
    rows = -(-D // down)
    return (pieces, -(-rows // 16) * 16, 128)


def last(sc, dq, dkv, n, x, dh, gain, wq, wk, wv, cos, sin, pieces):
    rows = x.shape[0]
    grads = last_shape(pieces)
    table = pl.BlockSpec((HALF, rows), lambda i, sc: (0, sc[0]))
    return pl.pallas_call(
        last_kernel,
        grid_spec=pltpu.PrefetchScalarGridSpec(
            num_scalar_prefetch=1,
            grid=(1,),
            in_specs=[
                whole(part.shape) for part in (dq, dkv, n, x, dh, gain, wq, wk, wv)
            ]
            + [table, table],
            out_specs=[whole((rows, D)), whole(grads)],
        ),
        out_shape=[
            jax.ShapeDtypeStruct((rows, D), BF16),
            jax.ShapeDtypeStruct(grads, BF16),
        ],
        compiler_params=params(),
        cost_estimate=cost(4 * rows * D * (D + 2 * KVD), 8 * 2**20),
        name="last",
    )(sc, dq, dkv, n, x, dh, gain, wq, wk, wv, cos, sin)


def unpack_big_kernel(table, *refs):
    ins = refs[:3]
    gate_ref, up_ref, down_ref, wo_ref, gain_ref, turn_ref = refs[3:]
    pieces, rows, _ = ins[0].shape
    third = D // 3
    tail = STACK - 3 * D - third

    def load(chunk, base, count, width):
        parts = [
            ins[chunk][table[chunk * pieces + (base + start) // rows], :, :width]
            for start in range(0, count, rows)
        ]
        return jnp.concatenate(parts, 0) if len(parts) > 1 else parts[0]

    for k in range(3):
        cols = slice(k * CHUNK, (k + 1) * CHUNK)
        for start in range(0, D, rows):
            gate_ref[start : start + rows, cols] = load(k, start, rows, CHUNK).astype(F32)
            up_ref[start : start + rows, cols] = load(k, D + start, rows, CHUNK).astype(F32)
        for start in range(0, D, rows):
            turn_ref[start : start + rows, :] = load(k, 2 * D + start, rows, CHUNK)
        down_ref[cols, :] = turn_ref[...].astype(F32).T
        wo_ref[k * third : (k + 1) * third, :CHUNK] = load(k, 3 * D, third, CHUNK).astype(F32)
        rest = load(k, 3 * D + third, tail, CHUNK).astype(F32)
        wo_ref[k * third : k * third + tail, CHUNK:] = rest[:, : D - CHUNK]
        wo_ref[k * third + tail : (k + 1) * third, CHUNK:] = rest[
            : third - tail, D - CHUNK : 2 * (D - CHUNK)
        ]
        if k == 0:
            gain_ref[:, : CHUNK - 128] = rest[:1, 128:]
        if k == 1:
            gain_ref[:, CHUNK - 128 :] = rest[:1, 128 : 128 + D - (CHUNK - 128)]


def unpack_big(table, chains):
    shapes = [(D, FF), (D, FF), (FF, D), (D, D), (1, D)]
    return pl.pallas_call(
        unpack_big_kernel,
        grid_spec=pltpu.PrefetchScalarGridSpec(
            num_scalar_prefetch=1,
            grid=(1,),
            in_specs=[whole(part.shape) for part in chains],
            out_specs=[whole(shape) for shape in shapes],
            scratch_shapes=[pltpu.VMEM((D, CHUNK), BF16)],
        ),
        out_shape=[jax.ShapeDtypeStruct(shape, F32) for shape in shapes],
        compiler_params=params(),
        cost_estimate=cost(0, 20 * 2**20),
        name="unpack_big",
    )(table, *chains)


def unpack_small_kernel(sc, in_ref, q_ref, k_ref, v_ref, gain_ref):
    pieces, rows, lanes = in_ref.shape
    across = 8
    columns = []
    for col in range(across):
        parts = []
        for row in range(pieces // across):
            count = min(rows, D - row * rows)
            if count > 0:
                parts.append(in_ref[sc[2 + row * across + col], :count].astype(F32))
        columns.append(jnp.concatenate(parts, 0) if len(parts) > 1 else parts[0])
    full = jnp.concatenate(columns, 1)
    q_ref[...] = full[:, :D]
    k_ref[...] = full[:, D : D + KVD]
    v_ref[...] = full[:, D + KVD : D + 2 * KVD]
    gain_ref[...] = columns[-1].T[64:65, :]


def unpack_small(sc, grads):
    shapes = [(D, D), (D, KVD), (D, KVD), (1, D)]
    return pl.pallas_call(
        unpack_small_kernel,
        grid_spec=pltpu.PrefetchScalarGridSpec(
            num_scalar_prefetch=1,
            grid=(1,),
            in_specs=[whole(grads.shape)],
            out_specs=[whole(shape) for shape in shapes],
        ),
        out_shape=[jax.ShapeDtypeStruct(shape, F32) for shape in shapes],
        compiler_params=params(),
        cost_estimate=cost(0, 4 * 2**20),
        name="unpack_small",
    )(sc, grads)


def plus(*parts):
    total = parts[0].astype(F32)
    for part in parts[1:]:
        total = total + part.astype(F32)
    return total.astype(BF16)


def swap(values, axis, size, flip):
    return lax.ppermute(values, axis, [(i, i ^ flip) for i in range(size)])


def halving_sum(values, order):
    for step in order:
        half = values.shape[0] // 2
        values = plus(values[:half], swap(values[half:], *step))
    return values


def doubling_gather(values, order):
    for step in reversed(order):
        values = jnp.concatenate([values, swap(values, *step)], 0)
    return values


def direct_sum(values, axis, size, unit):
    share = values.shape[0] // size
    pieces = [values[i * share : (i + 1) * share] for i in range(size)]
    return plus(
        pieces[0], *[swap(pieces[i], axis, size * unit, i * unit) for i in range(1, size)]
    )


def direct_gather(values, axis, size, unit):
    return jnp.concatenate(
        [values] + [swap(values, axis, size * unit, i * unit) for i in range(1, size)], 0
    )


def spread_bits(value, places):
    count = len(places)
    total = 0
    for t, place in enumerate(places):
        total = total | (((value >> place) & 1) << (count - 1 - t))
    return total


def build(seq_size, grp_size):
    count = seq_size * grp_size
    chips = seq_size // 2
    seq_bits = seq_size.bit_length() - 1
    grp_bits = grp_size.bit_length() - 1
    core = ("seq", seq_size, 1)
    chip_steps = [("seq", seq_size, 1 << bit) for bit in range(1, seq_bits)]
    grp_steps = [("grp", grp_size, 1 << bit) for bit in range(grp_bits)]
    places = {("seq", 1 << bit): bit for bit in range(seq_bits)}
    places.update({("grp", 1 << bit): seq_bits + bit for bit in range(grp_bits)})
    orders = [
        [core] + grp_steps + chip_steps,
        [core] + grp_steps[1:] + grp_steps[:1] + chip_steps,
        [core] + chip_steps[:1] + grp_steps + chip_steps[1:],
    ]
    spots = [[places[(axis, flip)] for axis, _, flip in order] for order in orders]
    small_spots = (
        [0]
        + [seq_bits + bit for bit in reversed(range(grp_bits))]
        + list(reversed(range(1, seq_bits)))
    )
    fixed_big = np.array(
        [[spread_bits(p, spot) for p in range(count)] for spot in spots], np.int32
    )
    fixed_small = np.array([spread_bits(p, small_spots) for p in range(count)], np.int32)

    def shards(
        inputs,
        lengths,
        attn_gain,
        w_query,
        w_key,
        w_value,
        w_out,
        ffn_gain,
        w_gate,
        w_up,
        w_down,
        cotangent,
    ):
        rows = inputs.shape[1]
        mine = lax.axis_index("seq")
        linear = lax.axis_index("grp") * seq_size + mine
        big_table = jnp.concatenate(
            [jnp.asarray(fixed_big[k]) ^ spread_bits(linear, spots[k]) for k in range(3)]
        ).astype(jnp.int32)
        sc = jnp.concatenate(
            [
                jnp.stack([mine.astype(jnp.int32), lengths[0]]),
                jnp.asarray(fixed_small) ^ spread_bits(linear, small_spots),
            ]
        ).astype(jnp.int32)
        cos_np, sin_np = rope_tables(rows * seq_size)
        cos = jnp.asarray(cos_np)
        sin = jnp.asarray(sin_np)
        x = inputs[0]
        cot = cotangent[0]
        gain_one = attn_gain[None]
        gain_two = ffn_gain[None]

        up = [(i, i + 2) for i in range(seq_size - 2)]
        down = [(i + 2, i) for i in range(seq_size - 2)]
        normed, query, own = first(sc, x, gain_one, w_query, w_key, w_value, cos, sin)
        blocks = [own]
        for _ in range(1, chips):
            blocks.append(lax.ppermute(blocks[-1], "seq", up))
        pairs = [(block, swap(block, *core)) for block in blocks]
        state = None
        for rank, (a, b) in enumerate(pairs):
            state = forward(sc, query, a, b, state, rank)
        m, l, acc = state
        outputs, d_mixed, lse, delta, d_resid, grads = middle(
            big_table, acc, m, l, x, cot, gain_two, w_out, w_gate, w_up, w_down
        )
        chains = [
            doubling_gather(halving_sum(grads[k], orders[k]), orders[k]) for k in range(3)
        ]

        dq = None
        passed = None
        for rank in reversed(range(chips)):
            a, b = pairs[rank]
            dq, grad_a, grad_b = backward(sc, query, d_mixed, lse, delta, a, b, dq, rank)
            terms = [grad_a, swap(grad_b, *core)]
            if passed is not None:
                terms.append(lax.ppermute(passed, "seq", down))
            passed = plus(*terms)

        d_inputs, small = last(
            sc,
            dq,
            passed,
            normed,
            x,
            d_resid,
            gain_one,
            w_query,
            w_key,
            w_value,
            cos,
            sin,
            count,
        )
        small = halving_sum(small, [core])
        small = direct_sum(small, "grp", grp_size, 1)
        small = direct_sum(small, "seq", chips, 2)
        small = direct_gather(small, "seq", chips, 2)
        small = direct_gather(small, "grp", grp_size, 1)
        small = doubling_gather(small, [core])
        d_query, d_key, d_value, d_attn_gain = unpack_small(sc, small)
        d_gate, d_up, d_down, d_out, d_ffn_gain = unpack_big(big_table, chains)
        return (
            outputs[None],
            d_inputs[None],
            d_attn_gain[0],
            d_query,
            d_key,
            d_value,
            d_out,
            d_ffn_gain[0],
            d_gate,
            d_up,
            d_down,
        )

    return shards


def solution(mesh):
    tokens = P("grp", "seq", None)
    return jax.shard_map(
        build(mesh.shape["seq"], mesh.shape["grp"]),
        mesh=mesh,
        in_specs=(tokens, P("grp")) + (P(),) * 9 + (tokens,),
        out_specs=(tokens, tokens) + (P(),) * 9,
        check_vma=False,
    )
```

```python
import functools
import math

import jax
import jax.numpy as jnp
import numpy as np
from jax import lax
from jax.experimental import pallas as pl
from jax.experimental.pallas import tpu as pltpu
from jax.sharding import PartitionSpec as P

D = 576
KV_HEADS = 3
HEAD_DIM = 64
REP = 3
HEADS = KV_HEADS * REP
KVD = 192
FF = 1536
CHUNK = 512
STACK = 2048
HALF = HEAD_DIM // 2

epsilon = 1e-05
rope_base = 100000.0
neg_big = -1e30
log2e = math.log2(math.e)
ln2 = math.log(2.0)

F32 = jnp.float32
BF16 = jnp.bfloat16
VMEM_LIMIT = 60 * 2**20


def mm(left, right, left_dim, right_dim):
    return lax.dot_general(
        left, right, (((left_dim,), (right_dim,)), ((), ())), preferred_element_type=F32
    )


def params():
    return pltpu.CompilerParams(vmem_limit_bytes=VMEM_LIMIT)


def whole(shape):
    return pl.BlockSpec(shape, lambda *_: (0,) * len(shape))


def cost(flops, nbytes, exps=0):
    return pl.CostEstimate(flops=int(flops), bytes_accessed=int(nbytes), transcendentals=int(exps))


def rope_tables(length):
    steps = np.arange(HALF, dtype=np.float32)
    freqs = (1.0 / np.float32(rope_base) ** (steps * np.float32(2.0) / np.float32(HEAD_DIM))).astype(
        np.float32
    )
    angles = np.arange(length, dtype=np.float32)[None, :] * freqs[:, None]
    return np.cos(angles).astype(np.float32), np.sin(angles).astype(np.float32)


def rotated(rows, cos, sin, scale, sign):
    parts = []
    for start in range(0, rows.shape[0], HEAD_DIM):
        one = rows[start : start + HALF]
        two = rows[start + HALF : start + HEAD_DIM]
        parts.append((one * cos - sign * (two * sin)) * scale)
        parts.append((two * cos + sign * (one * sin)) * scale)
    return jnp.concatenate(parts, 0)


def column(vector):
    return jnp.broadcast_to(vector[None], (8, vector.shape[0])).T[:, :1]


def first_kernel(sc, x_ref, gain_ref, wq_ref, wk_ref, wv_ref, cos_ref, sin_ref, n_ref, q_ref, kv_ref):
    x = x_ref[...].astype(F32)
    scale = lax.rsqrt(jnp.mean(x * x, axis=0, keepdims=True) + epsilon)
    normed = (x * scale * column(gain_ref[...])).astype(BF16)
    n_ref[...] = normed
    cos = cos_ref[...]
    sin = sin_ref[...]
    key = mm(wk_ref[...], normed, 1, 0)
    kv_ref[:KVD, :] = rotated(key, cos, sin, 1.0, 1.0).astype(BF16)
    kv_ref[KVD:, :] = mm(wv_ref[...], normed, 1, 0).astype(BF16)
    query = mm(wq_ref[...].T, normed, 1, 0)
    q_ref[...] = rotated(query, cos, sin, HEAD_DIM**-0.5 * log2e, 1.0).astype(BF16)


def first(sc, x, gain, wq, wk, wv, cos, sin):
    rows = x.shape[1]
    return pl.pallas_call(
        first_kernel,
        grid_spec=pltpu.PrefetchScalarGridSpec(
            num_scalar_prefetch=1,
            grid=(1,),
            in_specs=[
                whole(x.shape),
                whole(gain.shape),
                whole(wq.shape),
                whole(wk.shape),
                whole(wv.shape),
                pl.BlockSpec((HALF, rows), lambda i, sc: (0, sc[0])),
                pl.BlockSpec((HALF, rows), lambda i, sc: (0, sc[0])),
            ],
            out_specs=[whole((D, rows)), whole((D, rows)), whole((2 * KVD, rows))],
        ),
        out_shape=[
            jax.ShapeDtypeStruct((D, rows), BF16),
            jax.ShapeDtypeStruct((D, rows), BF16),
            jax.ShapeDtypeStruct((2 * KVD, rows), BF16),
        ],
        compiler_params=params(),
        cost_estimate=cost(2 * rows * D * (D + 2 * KVD), 4 * 2**20),
        name="first",
    )(sc, x, gain, wq, wk, wv, cos, sin)


def block_facts(sc, rank, which, rows):
    mine = sc[0]
    block = mine - 2 * rank if which == 0 else (mine ^ 1) - 2 * rank
    length = sc[1]
    start = block * rows
    active = (block >= 0) & (block <= mine) & (start < length)
    partial = (block == mine) | (start + rows > length)
    pos = mine * rows + lax.broadcasted_iota(jnp.int32, (1, rows), 1)
    bound = jnp.minimum(pos, length - 1) - start
    return active, partial, bound


def masked_scores(scores, bound):
    rows = lax.broadcasted_iota(jnp.int32, scores.shape, 0)
    return jnp.where(rows <= bound, scores, neg_big)


def forward_block(hidden_keys, bound, kv_ref, q_ref, m_ref, l_ref, acc_ref):
    rows = q_ref.shape[1]
    keys = kv_ref[:KVD, :].T
    ones = jnp.ones((8, rows), BF16)

    def score(head):
        kv = head // REP
        scores = mm(
            keys[:, kv * HEAD_DIM : (kv + 1) * HEAD_DIM],
            q_ref[head * HEAD_DIM : (head + 1) * HEAD_DIM, :],
            1,
            0,
        )
        if hidden_keys:
            scores = masked_scores(scores, bound)
        return scores, jnp.max(scores, axis=0, keepdims=True)

    def weigh(head, scores, top):
        kv = head // REP
        old = m_ref[head : head + 1, :]
        new = jnp.maximum(old, top)
        weights = jnp.exp2(scores - new).astype(BF16)
        values = jnp.concatenate(
            [kv_ref[KVD + kv * HEAD_DIM : KVD + (kv + 1) * HEAD_DIM, :], ones], 0
        )
        return new, jnp.exp2(old - new), mm(values, weights, 1, 0)

    def store(head, new, fade, out):
        rows_of = slice(head * HEAD_DIM, (head + 1) * HEAD_DIM)
        m_ref[head : head + 1, :] = new
        l_ref[head : head + 1, :] = l_ref[head : head + 1, :] * fade + out[HEAD_DIM : HEAD_DIM + 1]
        acc_ref[rows_of, :] = acc_ref[rows_of, :] * fade + out[:HEAD_DIM]

    ahead = score(0)
    held = None
    for head in range(HEADS):
        current = ahead
        if head + 1 < HEADS:
            ahead = score(head + 1)
        result = weigh(head, *current)
        if held is not None:
            store(*held)
        held = (head,) + result
    store(*held)


def forward_kernel(sc, q_ref, a_ref, b_ref, *refs, rank, fresh):
    rows = q_ref.shape[1]
    which = pl.program_id(0)
    m_ref, l_ref, acc_ref, kv_ref = refs[-4:]

    @pl.when(which == 0)
    def _():
        if fresh:
            m_ref[...] = jnp.full_like(m_ref, neg_big)
            l_ref[...] = jnp.zeros_like(l_ref)
            acc_ref[...] = jnp.zeros_like(acc_ref)
        else:
            m_ref[...] = refs[0][...]
            l_ref[...] = refs[1][...]
            acc_ref[...] = refs[2][...]
        kv_ref[...] = a_ref[...]

    @pl.when(which == 1)
    def _():
        kv_ref[...] = b_ref[...]

    first_facts = block_facts(sc, rank, 0, rows)
    second_facts = block_facts(sc, rank, 1, rows)
    active, partial, bound = [
        jnp.where(which == 0, one, two) for one, two in zip(first_facts, second_facts)
    ]

    @pl.when(active & jnp.logical_not(partial))
    def _():
        forward_block(False, bound, kv_ref, q_ref, m_ref, l_ref, acc_ref)

    @pl.when(active & partial)
    def _():
        forward_block(True, bound, kv_ref, q_ref, m_ref, l_ref, acc_ref)


def forward(sc, q, a, b, state, rank):
    rows = q.shape[1]
    state = () if state is None else tuple(state)
    return pl.pallas_call(
        functools.partial(forward_kernel, rank=rank, fresh=not state),
        grid_spec=pltpu.PrefetchScalarGridSpec(
            num_scalar_prefetch=1,
            grid=(2,),
            in_specs=[whole(q.shape), whole(a.shape), whole(b.shape)]
            + [whole(part.shape) for part in state],
            out_specs=[whole((16, rows)), whole((16, rows)), whole((D, rows))],
            scratch_shapes=[pltpu.VMEM(a.shape, BF16)],
        ),
        out_shape=[
            jax.ShapeDtypeStruct((16, rows), F32),
            jax.ShapeDtypeStruct((16, rows), F32),
            jax.ShapeDtypeStruct((D, rows), F32),
        ],
        compiler_params=params(),
        cost_estimate=cost(2 * 16 * rows * rows * D, 4 * 2**20, 2 * HEADS * rows * rows),
        name=f"forward_{rank}",
    )(sc, q, a, b, *state)


def backward_block(hidden_keys, bound, kv_ref, q_ref, do_ref, lse_ref, delta_ref, dq_ref, out_ref):
    keys = kv_ref[:KVD, :].T
    values = kv_ref[KVD:, :].T
    for kv in range(KV_HEADS):
        lanes = slice(kv * HEAD_DIM, (kv + 1) * HEAD_DIM)
        d_key = None
        d_value = None
        for rep in range(REP):
            head = kv * REP + rep
            rows_of = slice(head * HEAD_DIM, (head + 1) * HEAD_DIM)
            query = q_ref[rows_of, :]
            d_out = do_ref[rows_of, :]
            scores = mm(keys[:, lanes], query, 1, 0)
            if hidden_keys:
                scores = masked_scores(scores, bound)
            d_probs = mm(values[:, lanes], d_out, 1, 0)
            probs = jnp.exp2(scores - lse_ref[head : head + 1, :])
            d_scores = (probs * (d_probs - delta_ref[head : head + 1, :])).astype(BF16)
            value_term = mm(probs.astype(BF16), d_out, 1, 1)
            key_term = mm(d_scores, query, 1, 1)
            d_value = value_term if d_value is None else d_value + value_term
            d_key = key_term if d_key is None else d_key + key_term
            dq_ref[rows_of, :] = dq_ref[rows_of, :] + mm(
                kv_ref[kv * HEAD_DIM : (kv + 1) * HEAD_DIM, :], d_scores, 1, 0
            )
        out_ref[kv] = jnp.concatenate([d_key, d_value], 1).astype(BF16)


def backward_kernel(
    sc, q_ref, do_ref, lse_ref, delta_ref, a_ref, b_ref, *refs, rank, fresh
):
    rows = q_ref.shape[1]
    which = pl.program_id(0)
    dq_ref, ga_ref, gb_ref, kv_ref, out_ref = refs[-5:]

    @pl.when(which == 0)
    def _():
        if fresh:
            dq_ref[...] = jnp.zeros_like(dq_ref)
        else:
            dq_ref[...] = refs[0][...]
        kv_ref[...] = b_ref[...]

    @pl.when(which == 1)
    def _():
        kv_ref[...] = a_ref[...]

    first_facts = block_facts(sc, rank, 1, rows)
    second_facts = block_facts(sc, rank, 0, rows)
    active, partial, bound = [
        jnp.where(which == 0, one, two) for one, two in zip(first_facts, second_facts)
    ]
    rest = (kv_ref, q_ref, do_ref, lse_ref, delta_ref, dq_ref, out_ref)

    @pl.when(active & jnp.logical_not(partial))
    def _():
        backward_block(False, bound, *rest)

    @pl.when(active & partial)
    def _():
        backward_block(True, bound, *rest)

    @pl.when(jnp.logical_not(active))
    def _():
        out_ref[...] = jnp.zeros_like(out_ref)

    @pl.when(which == 0)
    def _():
        gb_ref[...] = out_ref[...]

    @pl.when(which == 1)
    def _():
        ga_ref[...] = out_ref[...]


def backward(sc, q, d_out, lse, delta, a, b, dq, rank):
    rows = q.shape[1]
    state = () if dq is None else (dq,)
    grads = (KV_HEADS, rows, 2 * HEAD_DIM)
    return pl.pallas_call(
        functools.partial(backward_kernel, rank=rank, fresh=not state),
        grid_spec=pltpu.PrefetchScalarGridSpec(
            num_scalar_prefetch=1,
            grid=(2,),
            in_specs=[whole(part.shape) for part in (q, d_out, lse, delta, a, b) + state],
            out_specs=[whole((D, rows)), whole(grads), whole(grads)],
            scratch_shapes=[pltpu.VMEM(a.shape, BF16), pltpu.VMEM(grads, BF16)],
        ),
        out_shape=[
            jax.ShapeDtypeStruct((D, rows), F32),
            jax.ShapeDtypeStruct(grads, BF16),
            jax.ShapeDtypeStruct(grads, BF16),
        ],
        compiler_params=params(),
        cost_estimate=cost(2 * 40 * rows * rows * D, 5 * 2**20, 2 * HEADS * rows * rows),
        name=f"backward_{rank}",
    )(sc, q, d_out, lse, delta, a, b, *state)


def store_pieces(sc, keep_ref, send_ref, stack, piece_of):
    low = (sc[2] & 1) == 0
    for pair in range(keep_ref.shape[0]):
        where = pair ^ lax.shift_right_logical(sc[2], 1)
        even = piece_of(stack, 2 * pair)
        odd = piece_of(stack, 2 * pair + 1)
        keep_ref[where] = jnp.where(low, even, odd)
        send_ref[where] = jnp.where(low, odd, even)


def load_pair(sc, keep_ref, got_ref, pair):
    low = (sc[2] & 1) == 0
    where = pair ^ lax.shift_right_logical(sc[2], 1)
    one = keep_ref[where]
    two = got_ref[where]
    return jnp.where(low, one, two), jnp.where(low, two, one)


def middle_kernel(
    sc,
    acc_ref,
    m_ref,
    l_ref,
    x_ref,
    cot_ref,
    gain_ref,
    wo_ref,
    wg_ref,
    wu_ref,
    wd_ref,
    y_ref,
    do_ref,
    lse_ref,
    delta_ref,
    dh_ref,
    keep_ref,
    send_ref,
    mixed_ref,
    stack_ref,
    hid_ref,
    dg_ref,
    du_ref,
):
    for head in range(HEADS):
        rows_of = slice(head * HEAD_DIM, (head + 1) * HEAD_DIM)
        mixed_ref[rows_of, :] = acc_ref[rows_of, :] * (1.0 / l_ref[head : head + 1, :])
    lse_ref[:HEADS, :] = m_ref[:HEADS, :] + jnp.log2(l_ref[:HEADS, :])
    gain = column(gain_ref[...])
    cot_t = cot_ref[...]
    cot = cot_t.T
    mixed_low = mixed_ref[...].astype(BF16)
    h = x_ref[...].astype(F32) + mm(wo_ref[...].T, mixed_low, 1, 0)
    scale = lax.rsqrt(jnp.mean(h * h, axis=0, keepdims=True) + epsilon)
    normed_t = (h * scale * gain).astype(BF16)
    normed = normed_t.T

    def start(chunk):
        cols = slice(chunk * CHUNK, (chunk + 1) * CHUNK)
        return (
            mm(normed, wg_ref[:, cols], 1, 0),
            mm(normed, wu_ref[:, cols], 1, 0),
            mm(cot, wd_ref[:, cols], 1, 0),
        )

    chunks = FF // CHUNK
    ahead = start(0)
    for chunk in range(chunks):
        gate, up, d_hidden = ahead
        if chunk + 1 < chunks:
            ahead = start(chunk + 1)
        cols = slice(chunk * CHUNK, (chunk + 1) * CHUNK)
        sig = 1.0 / (1.0 + jnp.exp2(gate * -log2e))
        silu = gate * sig
        hidden = (silu * up).astype(BF16)
        d_gate = (d_hidden * up * (sig * (1.0 + gate * (1.0 - sig)))).astype(BF16)
        d_up = (d_hidden * silu).astype(BF16)
        hid_ref[:, cols] = hidden
        dg_ref[:, cols] = d_gate
        du_ref[:, cols] = d_up
        stack_ref[:D, cols] = mm(normed_t, d_gate, 1, 0).astype(BF16)
        stack_ref[D : 2 * D, cols] = mm(normed_t, d_up, 1, 0).astype(BF16)
        stack_ref[2 * D : 3 * D, cols] = mm(cot_t, hidden, 1, 0).astype(BF16)
    y_ref[...] = (h + mm(wd_ref[...], hid_ref[...], 1, 1)).astype(BF16)
    dn = mm(wg_ref[...], dg_ref[...], 1, 1) + mm(wu_ref[...], du_ref[...], 1, 1)
    unit = h * scale
    gain_sum = jnp.sum(dn * unit, axis=1, keepdims=True)
    scaled = dn * gain
    dh = cot_t.astype(F32) + scale * (
        scaled - unit * jnp.mean(scaled * unit, axis=0, keepdims=True)
    )
    dh_ref[...] = dh
    dh_low = dh.astype(BF16)
    mixed = mixed_ref[...]
    d_mixed = mm(wo_ref[...], dh_low, 1, 0).astype(BF16)
    do_ref[...] = d_mixed
    for head in range(HEADS):
        rows_of = slice(head * HEAD_DIM, (head + 1) * HEAD_DIM)
        delta_ref[head : head + 1, :] = jnp.sum(
            d_mixed[rows_of].astype(F32) * mixed[rows_of], axis=0, keepdims=True
        )
    d_wo = mm(mixed_low, dh_low, 1, 1).astype(BF16)
    gain_row = jnp.broadcast_to(gain_sum, (D, 128)).T[:16].astype(BF16)
    third = D // 3
    base = 3 * D + third
    tail = STACK - base
    room = CHUNK - 128
    for k in range(3):
        left = k * CHUNK
        part = d_wo[k * third : (k + 1) * third]
        stack_ref[3 * D : base, left : left + CHUNK] = part[:, :CHUNK]
        lanes = part[:, CHUNK:]
        right = jnp.concatenate([lanes[tail:], jnp.zeros((2 * tail - third, D - CHUNK), BF16)], 0)
        stack_ref[base:, left : left + 128] = jnp.concatenate([lanes[:tail], right], 1)
        stack_ref[base:, left + 128 : left + CHUNK] = jnp.zeros((tail, room), BF16)
    stack_ref[base : base + 16, 128:CHUNK] = gain_row[:, :room]
    stack_ref[base : base + 16, CHUNK + 128 : CHUNK + 128 + D - room] = gain_row[:, room:]
    rows = keep_ref.shape[1]
    store_pieces(
        sc, keep_ref, send_ref, stack_ref, lambda ref, p: ref[p * rows : (p + 1) * rows, :]
    )


def middle(sc, acc, m, l, x, cot, gain, wo, wg, wu, wd, pieces):
    rows = x.shape[1]
    half = (pieces // 2, STACK // pieces, FF)
    args = (acc, m, l, x, cot, gain, wo, wg, wu, wd)
    outs = [
        ((D, rows), BF16),
        ((D, rows), BF16),
        ((16, rows), F32),
        ((16, rows), F32),
        ((D, rows), F32),
        (half, BF16),
        (half, BF16),
    ]
    return pl.pallas_call(
        middle_kernel,
        grid_spec=pltpu.PrefetchScalarGridSpec(
            num_scalar_prefetch=1,
            grid=(1,),
            in_specs=[whole(part.shape) for part in args],
            out_specs=[whole(shape) for shape, _ in outs],
            scratch_shapes=[
                pltpu.VMEM((D, rows), F32),
                pltpu.VMEM((STACK, FF), BF16),
                pltpu.VMEM((rows, FF), BF16),
                pltpu.VMEM((rows, FF), BF16),
                pltpu.VMEM((rows, FF), BF16),
            ],
        ),
        out_shape=[jax.ShapeDtypeStruct(*out) for out in outs],
        compiler_params=params(),
        cost_estimate=cost(18 * rows * D * FF, 24 * 2**20, rows * FF),
        name="middle",
    )(sc, *args)


def last_kernel(
    sc,
    dq_ref,
    dkv_ref,
    n_ref,
    x_ref,
    dh_ref,
    gain_ref,
    wq_ref,
    wk_ref,
    wv_ref,
    cos_ref,
    sin_ref,
    dx_ref,
    keep_ref,
    send_ref,
):
    cos = cos_ref[...]
    sin = sin_ref[...]
    rows = x_ref.shape[1]
    d_query = rotated(dq_ref[...], cos, sin, HEAD_DIM**-0.5, -1.0).astype(BF16)
    turned = [dkv_ref[kv].astype(F32).T for kv in range(KV_HEADS)]
    d_key = rotated(
        jnp.concatenate([part[:HEAD_DIM] for part in turned], 0), cos, sin, ln2, -1.0
    ).astype(BF16)
    d_value = jnp.concatenate([part[HEAD_DIM:] for part in turned], 0).astype(BF16)
    dn = (
        mm(wq_ref[...], d_query, 1, 0)
        + mm(wk_ref[...], d_key, 0, 0)
        + mm(wv_ref[...], d_value, 0, 0)
    )
    x = x_ref[...].astype(F32)
    scale = lax.rsqrt(jnp.mean(x * x, axis=0, keepdims=True) + epsilon)
    unit = x * scale
    scaled = dn * column(gain_ref[...])
    dx_ref[...] = (
        dh_ref[...] + scale * (scaled - unit * jnp.mean(scaled * unit, axis=0, keepdims=True))
    ).astype(BF16)
    pad = 64
    joined = jnp.concatenate([d_query, jnp.zeros((pad, rows), BF16), d_key, d_value], 0)
    grad = mm(n_ref[...], joined, 1, 1)
    gain_sum = jnp.sum(dn * unit, axis=1, keepdims=True)
    spot = D // 128
    lane = lax.broadcasted_iota(jnp.int32, (D, 128), 1)
    mixed = jnp.where(
        lane < D - spot * 128, grad[:, spot * 128 : (spot + 1) * 128], gain_sum
    )
    tiles = [
        (mixed if i == spot else grad[:, i * 128 : (i + 1) * 128]).astype(BF16) for i in range(8)
    ]
    piece_rows = keep_ref.shape[1]

    def piece_of(parts, piece):
        top = (piece // 8) * piece_rows
        count = max(min(piece_rows, D - top), 0)
        empty = jnp.zeros((piece_rows - count, 128), BF16)
        if count == 0:
            return empty
        part = parts[piece % 8][top : top + count]
        return jnp.concatenate([part, empty], 0) if count < piece_rows else part

    store_pieces(sc, keep_ref, send_ref, tiles, piece_of)


def last(sc, dq, dkv, n, x, dh, gain, wq, wk, wv, cos, sin, pieces):
    rows = x.shape[1]
    piece_rows = -(-D // max(pieces // 8, 1))
    half = (pieces // 2, -(-piece_rows // 16) * 16, 128)
    table = pl.BlockSpec((HALF, rows), lambda i, sc: (0, sc[0]))
    return pl.pallas_call(
        last_kernel,
        grid_spec=pltpu.PrefetchScalarGridSpec(
            num_scalar_prefetch=1,
            grid=(1,),
            in_specs=[whole(part.shape) for part in (dq, dkv, n, x, dh, gain, wq, wk, wv)]
            + [table, table],
            out_specs=[whole((D, rows)), whole(half), whole(half)],
        ),
        out_shape=[
            jax.ShapeDtypeStruct((D, rows), BF16),
            jax.ShapeDtypeStruct(half, BF16),
            jax.ShapeDtypeStruct(half, BF16),
        ],
        compiler_params=params(),
        cost_estimate=cost(4 * rows * D * (D + 2 * KVD), 8 * 2**20),
        name="last",
    )(sc, dq, dkv, n, x, dh, gain, wq, wk, wv, cos, sin)


def unpack_big_kernel(sc, keep_ref, got_ref, gate_ref, up_ref, down_ref, wo_ref, gain_ref):
    pairs, rows, _ = keep_ref.shape
    third = D // 3
    base = 3 * D + third
    tail = STACK - base
    room = CHUNK - 128
    rest = []
    for pair in range(pairs):
        for side, part in enumerate(load_pair(sc, keep_ref, got_ref, pair)):
            part = part.astype(F32)
            top = (2 * pair + side) * rows
            if top < 3 * D:
                ref = (gate_ref, up_ref, down_ref)[top // D]
                ref[top % D : top % D + rows, :] = part
            elif top < base:
                for k in range(3):
                    at = k * third + top - 3 * D
                    wo_ref[at : at + rows, :CHUNK] = part[:, k * CHUNK : (k + 1) * CHUNK]
            else:
                rest.append(part)
    rest = jnp.concatenate(rest, 0)
    for k in range(3):
        lanes = rest[:, k * CHUNK : k * CHUNK + 128]
        top = k * third
        wo_ref[top : top + tail, CHUNK:] = lanes[:, : D - CHUNK]
        wo_ref[top + tail : top + third, CHUNK:] = lanes[: third - tail, D - CHUNK :]
    gain_ref[...] = jnp.concatenate(
        [rest[0, 128:CHUNK], rest[0, CHUNK + 128 : CHUNK + 128 + D - room]], 0
    )


def unpack_big(sc, keep, got):
    shapes = [(D, FF), (D, FF), (D, FF), (D, D), (D,)]
    return pl.pallas_call(
        unpack_big_kernel,
        grid_spec=pltpu.PrefetchScalarGridSpec(
            num_scalar_prefetch=1,
            grid=(1,),
            in_specs=[whole(keep.shape), whole(got.shape)],
            out_specs=[whole(shape) for shape in shapes],
        ),
        out_shape=[jax.ShapeDtypeStruct(shape, F32) for shape in shapes],
        compiler_params=params(),
        cost_estimate=cost(0, 20 * 2**20),
        name="unpack_big",
    )(sc, keep, got)


def unpack_small_kernel(sc, keep_ref, got_ref, q_ref, k_ref, v_ref, gain_ref):
    pairs, rows, _ = keep_ref.shape
    columns = [[] for _ in range(8)]
    for pair in range(pairs):
        for side, part in enumerate(load_pair(sc, keep_ref, got_ref, pair)):
            piece = 2 * pair + side
            count = min(rows, D - (piece // 8) * rows)
            if count > 0:
                columns[piece % 8].append(part[:count].astype(F32))
    full = [jnp.concatenate(parts, 0) if len(parts) > 1 else parts[0] for parts in columns]
    spot = D // 128
    for i in range(spot):
        q_ref[:, i * 128 : (i + 1) * 128] = full[i]
    q_ref[:, spot * 128 :] = full[spot][:, : D - spot * 128]
    gain_ref[...] = full[spot].T[D - spot * 128]
    key_value = jnp.concatenate(full[spot + 1 :], 1).T
    k_ref[...] = key_value[:KVD]
    v_ref[...] = key_value[KVD:]


def unpack_small(sc, keep, got):
    shapes = [(D, D), (KVD, D), (KVD, D), (D,)]
    return pl.pallas_call(
        unpack_small_kernel,
        grid_spec=pltpu.PrefetchScalarGridSpec(
            num_scalar_prefetch=1,
            grid=(1,),
            in_specs=[whole(keep.shape), whole(got.shape)],
            out_specs=[whole(shape) for shape in shapes],
        ),
        out_shape=[jax.ShapeDtypeStruct(shape, F32) for shape in shapes],
        compiler_params=params(),
        cost_estimate=cost(0, 4 * 2**20),
        name="unpack_small",
    )(sc, keep, got)


def plus(*parts):
    total = parts[0].astype(F32)
    for part in parts[1:]:
        total = total + part.astype(F32)
    return total.astype(BF16)


def swap(values, axis, size, flip):
    return lax.ppermute(values, axis, [(i, i ^ flip) for i in range(size)])


def direct_sum(values, axis, size, unit):
    share = values.shape[0] // size
    pieces = [values[i * share : (i + 1) * share] for i in range(size)]
    return plus(
        pieces[0], *[swap(pieces[i], axis, size * unit, i * unit) for i in range(1, size)]
    )


def direct_gather(values, axis, size, unit):
    return jnp.concatenate(
        [values] + [swap(values, axis, size * unit, i * unit) for i in range(1, size)], 0
    )


def after(value, *others):
    return lax.optimization_barrier((value,) + others)[0]


def build(seq_size, grp_size):
    count = seq_size * grp_size
    chips = seq_size // 2
    core = ("seq", seq_size, 1)

    def shards(
        inputs,
        lengths,
        attn_gain,
        w_query,
        w_key,
        w_value,
        w_out,
        ffn_gain,
        w_gate,
        w_up,
        w_down,
        cotangent,
    ):
        rows = inputs.shape[1]
        mine = lax.axis_index("seq")
        sc = jnp.stack(
            [mine, lengths[0], lax.axis_index("grp") * seq_size + mine]
        ).astype(jnp.int32)
        cos_np, sin_np = rope_tables(rows * seq_size)
        cos = jnp.asarray(cos_np)
        sin = jnp.asarray(sin_np)
        x = inputs[0].T
        cot = cotangent[0].T
        wk = w_key.T
        wv = w_value.T
        wd = w_down.T

        up = [(i, i + 2) for i in range(seq_size - 2)]
        down = [(i + 2, i) for i in range(seq_size - 2)]
        normed, query, own = first(sc, x, attn_gain, w_query, wk, wv, cos, sin)
        pairs = []
        state = None
        block = own
        for rank in range(chips):
            pair = (block, swap(block, *core))
            if rank + 1 < chips:
                block = lax.ppermute(block, "seq", up)
            pairs.append(pair)
            state = forward(sc, query, *pair, state, rank)
            if rank + 2 < chips:
                block = after(block, state[0])
        m, l, acc = state
        outputs, d_mixed, lse, delta, d_resid, keep, send = middle(
            sc, acc, m, l, x, cot, ffn_gain, w_out, w_gate, w_up, wd, count
        )

        sums = [
            lambda big: plus(big, swap(send, *core)),
            lambda big: direct_sum(big, "grp", grp_size, 1),
            lambda big: direct_sum(big, "seq", chips, 2),
        ]
        waits = {chips - 2: 0, 0: 1}
        big = keep
        dq = None
        passed = None
        for rank in reversed(range(chips)):
            if rank in waits:
                big = sums[waits[rank]](big)
                dq = after(dq, big)
            dq, grad_a, grad_b = backward(
                sc, query, d_mixed, lse, delta, *pairs[rank], dq, rank
            )
            terms = [grad_a, swap(grad_b, *core)]
            if passed is not None:
                terms.append(lax.ppermute(passed, "seq", down))
            passed = plus(*terms)
        big = sums[2](big)

        d_inputs, small, small_send = last(
            sc, dq, passed, normed, x, d_resid, attn_gain, w_query, wk, wv, cos, sin, count
        )
        small = plus(small, swap(small_send, *core))
        small = direct_sum(small, "grp", grp_size, 1)
        small = direct_sum(small, "seq", chips, 2)
        small = direct_gather(small, "seq", chips, 2)
        small = direct_gather(small, "grp", grp_size, 1)
        d_query, d_key, d_value, d_attn_gain = unpack_small(sc, small, swap(small, *core))

        big = direct_gather(big, "seq", chips, 2)
        big = direct_gather(big, "grp", grp_size, 1)
        d_gate, d_up, d_down, d_out, d_ffn_gain = unpack_big(sc, big, swap(big, *core))
        return (
            outputs.T[None],
            d_inputs.T[None],
            d_attn_gain,
            d_query,
            d_key.T,
            d_value.T,
            d_out,
            d_ffn_gain,
            d_gate,
            d_up,
            d_down.T,
        )

    return shards


def solution(mesh):
    tokens = P("grp", "seq", None)
    return jax.shard_map(
        build(mesh.shape["seq"], mesh.shape["grp"]),
        mesh=mesh,
        in_specs=(tokens, P("grp")) + (P(),) * 9 + (tokens,),
        out_specs=(tokens, tokens) + (P(),) * 9,
        check_vma=False,
    )
```

```python
import functools
import math

import jax
import jax.numpy as jnp
import numpy as np
from jax import lax
from jax.experimental import pallas as pl
from jax.experimental.pallas import tpu as pltpu
from jax.sharding import PartitionSpec as P

D = 576
KV_HEADS = 3
HEAD_DIM = 64
REP = 3
HEADS = KV_HEADS * REP
KVD = 192
FF = 1536
CHUNK = 512
STACK = 2048
PART = 384
HALF = HEAD_DIM // 2

epsilon = 1e-05
rope_base = 100000.0
neg_big = -1e30
log2e = math.log2(math.e)
ln2 = math.log(2.0)

F32 = jnp.float32
BF16 = jnp.bfloat16
VMEM_LIMIT = 60 * 2**20


def mm(left, right, left_dim, right_dim):
    return lax.dot_general(
        left, right, (((left_dim,), (right_dim,)), ((), ())), preferred_element_type=F32
    )


def params():
    return pltpu.CompilerParams(vmem_limit_bytes=VMEM_LIMIT)


def whole(shape):
    return pl.BlockSpec(shape, lambda *_: (0,) * len(shape))


def cost():
    return pl.CostEstimate(flops=10**8, bytes_accessed=2**17, transcendentals=0)


def rope_tables(length):
    steps = np.arange(HALF, dtype=np.float32)
    freqs = (1.0 / np.float32(rope_base) ** (steps * np.float32(2.0) / np.float32(HEAD_DIM))).astype(
        np.float32
    )
    angles = np.arange(length, dtype=np.float32)[None, :] * freqs[:, None]
    return np.cos(angles).astype(np.float32), np.sin(angles).astype(np.float32)


def rotated(rows, cos, sin, scale, sign):
    parts = []
    for start in range(0, rows.shape[0], HEAD_DIM):
        one = rows[start : start + HALF]
        two = rows[start + HALF : start + HEAD_DIM]
        parts.append((one * cos - sign * (two * sin)) * scale)
        parts.append((two * cos + sign * (one * sin)) * scale)
    return jnp.concatenate(parts, 0)


def column(vector):
    return jnp.broadcast_to(vector[None], (8, vector.shape[0])).T[:, :1]


def first_kernel(sc, x_ref, gain_ref, wq_ref, wk_ref, wv_ref, cos_ref, sin_ref, n_ref, q_ref, kv_ref):
    x = x_ref[...].astype(F32)
    scale = lax.rsqrt(jnp.mean(x * x, axis=0, keepdims=True) + epsilon)
    normed = (x * scale * column(gain_ref[...])).astype(BF16)
    n_ref[...] = normed
    cos = cos_ref[...]
    sin = sin_ref[...]
    key = mm(wk_ref[...], normed, 1, 0)
    kv_ref[:KVD, :] = rotated(key, cos, sin, 1.0, 1.0).astype(BF16)
    kv_ref[KVD:, :] = mm(wv_ref[...], normed, 1, 0).astype(BF16)
    query = mm(wq_ref[...].T, normed, 1, 0)
    q_ref[...] = rotated(query, cos, sin, HEAD_DIM**-0.5 * log2e, 1.0).astype(BF16)


def first(sc, x, gain, wq, wk, wv, cos, sin):
    rows = x.shape[1]
    return pl.pallas_call(
        first_kernel,
        grid_spec=pltpu.PrefetchScalarGridSpec(
            num_scalar_prefetch=1,
            grid=(1,),
            in_specs=[
                whole(x.shape),
                whole(gain.shape),
                whole(wq.shape),
                whole(wk.shape),
                whole(wv.shape),
                pl.BlockSpec((HALF, rows), lambda i, sc: (0, sc[0])),
                pl.BlockSpec((HALF, rows), lambda i, sc: (0, sc[0])),
            ],
            out_specs=[whole((D, rows)), whole((D, rows)), whole((2 * KVD, rows))],
        ),
        out_shape=[
            jax.ShapeDtypeStruct((D, rows), BF16),
            jax.ShapeDtypeStruct((D, rows), BF16),
            jax.ShapeDtypeStruct((2 * KVD, rows), BF16),
        ],
        compiler_params=params(),
        cost_estimate=cost(),
        name="first",
    )(sc, x, gain, wq, wk, wv, cos, sin)


def block_facts(sc, rank, which, rows):
    mine = sc[0]
    block = mine - 2 * rank if which == 0 else (mine ^ 1) - 2 * rank
    length = sc[1]
    start = block * rows
    active = (block >= 0) & (block <= mine) & (start < length)
    partial = (block == mine) | (start + rows > length)
    pos = mine * rows + lax.broadcasted_iota(jnp.int32, (1, rows), 1)
    bound = jnp.minimum(pos, length - 1) - start
    return active, partial, bound


def masked_scores(scores, bound):
    rows = lax.broadcasted_iota(jnp.int32, scores.shape, 0)
    return jnp.where(rows <= bound, scores, neg_big)


def forward_block(hidden_keys, bound, kv_ref, q_ref, m_ref, l_ref, acc_ref):
    rows = q_ref.shape[1]
    keys = kv_ref[:KVD, :].T
    ones = jnp.ones((8, rows), BF16)

    def score(head):
        kv = head // REP
        scores = mm(
            keys[:, kv * HEAD_DIM : (kv + 1) * HEAD_DIM],
            q_ref[head * HEAD_DIM : (head + 1) * HEAD_DIM, :],
            1,
            0,
        )
        if hidden_keys:
            scores = masked_scores(scores, bound)
        return scores, jnp.max(scores, axis=0, keepdims=True)

    def weigh(head, scores, top):
        kv = head // REP
        old = m_ref[head : head + 1, :]
        new = jnp.maximum(old, top)
        weights = jnp.exp2(scores - new).astype(BF16)
        values = jnp.concatenate(
            [kv_ref[KVD + kv * HEAD_DIM : KVD + (kv + 1) * HEAD_DIM, :], ones], 0
        )
        return new, jnp.exp2(old - new), mm(values, weights, 1, 0)

    def store(head, new, fade, out):
        rows_of = slice(head * HEAD_DIM, (head + 1) * HEAD_DIM)
        m_ref[head : head + 1, :] = new
        l_ref[head : head + 1, :] = l_ref[head : head + 1, :] * fade + out[HEAD_DIM : HEAD_DIM + 1]
        acc_ref[rows_of, :] = acc_ref[rows_of, :] * fade + out[:HEAD_DIM]

    ahead = score(0)
    held = None
    for head in range(HEADS):
        current = ahead
        if head + 1 < HEADS:
            ahead = score(head + 1)
        result = weigh(head, *current)
        if held is not None:
            store(*held)
        held = (head,) + result
    store(*held)


def forward_kernel(sc, q_ref, a_ref, b_ref, *refs, rank, fresh):
    rows = q_ref.shape[1]
    which = pl.program_id(0)
    m_ref, l_ref, acc_ref, kv_ref = refs[-4:]

    @pl.when(which == 0)
    def _():
        if fresh:
            m_ref[...] = jnp.full_like(m_ref, neg_big)
            l_ref[...] = jnp.zeros_like(l_ref)
            acc_ref[...] = jnp.zeros_like(acc_ref)
        else:
            m_ref[...] = refs[0][...]
            l_ref[...] = refs[1][...]
            acc_ref[...] = refs[2][...]
        kv_ref[...] = a_ref[...]

    @pl.when(which == 1)
    def _():
        kv_ref[...] = b_ref[...]

    first_facts = block_facts(sc, rank, 0, rows)
    second_facts = block_facts(sc, rank, 1, rows)
    active, partial, bound = [
        jnp.where(which == 0, one, two) for one, two in zip(first_facts, second_facts)
    ]

    @pl.when(active & jnp.logical_not(partial))
    def _():
        forward_block(False, bound, kv_ref, q_ref, m_ref, l_ref, acc_ref)

    @pl.when(active & partial)
    def _():
        forward_block(True, bound, kv_ref, q_ref, m_ref, l_ref, acc_ref)


def forward(sc, q, a, b, state, rank):
    rows = q.shape[1]
    state = () if state is None else tuple(state)
    return pl.pallas_call(
        functools.partial(forward_kernel, rank=rank, fresh=not state),
        grid_spec=pltpu.PrefetchScalarGridSpec(
            num_scalar_prefetch=1,
            grid=(2,),
            in_specs=[whole(q.shape), whole(a.shape), whole(b.shape)]
            + [whole(part.shape) for part in state],
            out_specs=[whole((16, rows)), whole((16, rows)), whole((D, rows))],
            scratch_shapes=[pltpu.VMEM(a.shape, BF16)],
        ),
        out_shape=[
            jax.ShapeDtypeStruct((16, rows), F32),
            jax.ShapeDtypeStruct((16, rows), F32),
            jax.ShapeDtypeStruct((D, rows), F32),
        ],
        compiler_params=params(),
        cost_estimate=cost(),
        name=f"forward_{rank}",
    )(sc, q, a, b, *state)


def backward_block(hidden_keys, bound, kv_ref, q_ref, do_ref, lse_ref, delta_ref, dq_ref, out_ref):
    keys = kv_ref[:KVD, :].T
    values = kv_ref[KVD:, :].T
    for kv in range(KV_HEADS):
        lanes = slice(kv * HEAD_DIM, (kv + 1) * HEAD_DIM)
        d_key = None
        d_value = None
        for rep in range(REP):
            head = kv * REP + rep
            rows_of = slice(head * HEAD_DIM, (head + 1) * HEAD_DIM)
            query = q_ref[rows_of, :]
            d_out = do_ref[rows_of, :]
            scores = mm(keys[:, lanes], query, 1, 0)
            if hidden_keys:
                scores = masked_scores(scores, bound)
            d_probs = mm(values[:, lanes], d_out, 1, 0)
            probs = jnp.exp2(scores - lse_ref[head : head + 1, :])
            d_scores = (probs * (d_probs - delta_ref[head : head + 1, :])).astype(BF16)
            value_term = mm(probs.astype(BF16), d_out, 1, 1)
            key_term = mm(d_scores, query, 1, 1)
            d_value = value_term if d_value is None else d_value + value_term
            d_key = key_term if d_key is None else d_key + key_term
            dq_ref[rows_of, :] = dq_ref[rows_of, :] + mm(
                kv_ref[kv * HEAD_DIM : (kv + 1) * HEAD_DIM, :], d_scores, 1, 0
            )
        out_ref[kv] = jnp.concatenate([d_key, d_value], 1).astype(BF16)


def backward_kernel(
    sc, q_ref, do_ref, lse_ref, delta_ref, a_ref, b_ref, *refs, rank, fresh
):
    rows = q_ref.shape[1]
    which = pl.program_id(0)
    dq_ref, ga_ref, gb_ref, kv_ref, out_ref = refs[-5:]

    @pl.when(which == 0)
    def _():
        if fresh:
            dq_ref[...] = jnp.zeros_like(dq_ref)
        else:
            dq_ref[...] = refs[0][...]
        kv_ref[...] = b_ref[...]

    @pl.when(which == 1)
    def _():
        kv_ref[...] = a_ref[...]

    first_facts = block_facts(sc, rank, 1, rows)
    second_facts = block_facts(sc, rank, 0, rows)
    active, partial, bound = [
        jnp.where(which == 0, one, two) for one, two in zip(first_facts, second_facts)
    ]
    rest = (kv_ref, q_ref, do_ref, lse_ref, delta_ref, dq_ref, out_ref)

    @pl.when(active & jnp.logical_not(partial))
    def _():
        backward_block(False, bound, *rest)

    @pl.when(active & partial)
    def _():
        backward_block(True, bound, *rest)

    @pl.when(jnp.logical_not(active))
    def _():
        out_ref[...] = jnp.zeros_like(out_ref)

    @pl.when(which == 0)
    def _():
        gb_ref[...] = out_ref[...]

    @pl.when(which == 1)
    def _():
        ga_ref[...] = out_ref[...]


def backward(sc, q, d_out, lse, delta, a, b, dq, rank):
    rows = q.shape[1]
    state = () if dq is None else (dq,)
    grads = (KV_HEADS, rows, 2 * HEAD_DIM)
    return pl.pallas_call(
        functools.partial(backward_kernel, rank=rank, fresh=not state),
        grid_spec=pltpu.PrefetchScalarGridSpec(
            num_scalar_prefetch=1,
            grid=(2,),
            in_specs=[whole(part.shape) for part in (q, d_out, lse, delta, a, b) + state],
            out_specs=[whole((D, rows)), whole(grads), whole(grads)],
            scratch_shapes=[pltpu.VMEM(a.shape, BF16), pltpu.VMEM(grads, BF16)],
        ),
        out_shape=[
            jax.ShapeDtypeStruct((D, rows), F32),
            jax.ShapeDtypeStruct(grads, BF16),
            jax.ShapeDtypeStruct(grads, BF16),
        ],
        compiler_params=params(),
        cost_estimate=cost(),
        name=f"backward_{rank}",
    )(sc, q, d_out, lse, delta, a, b, *state)


def store_pieces(sc, spot, keep_ref, send_ref, piece_of):
    low = (sc[0] & 1) == 0
    for pair in range(keep_ref.shape[0]):
        even = piece_of(2 * pair)
        odd = piece_of(2 * pair + 1)
        keep_ref[pair ^ spot] = jnp.where(low, even, odd)
        send_ref[pair ^ spot] = jnp.where(low, odd, even)


def load_pair(sc, spot, keep_ref, got_ref, pair):
    low = (sc[0] & 1) == 0
    one = keep_ref[pair ^ spot]
    two = got_ref[pair ^ spot]
    return jnp.where(low, one, two), jnp.where(low, two, one)


def middle_kernel(
    sc,
    acc_ref,
    m_ref,
    l_ref,
    x_ref,
    cot_ref,
    gain_ref,
    wo_ref,
    wg_ref,
    wu_ref,
    wd_ref,
    y_ref,
    do_ref,
    lse_ref,
    delta_ref,
    dh_ref,
    keep_ref,
    send_ref,
    mixed_ref,
    stack_ref,
    hid_ref,
    dg_ref,
    du_ref,
):
    for head in range(HEADS):
        rows_of = slice(head * HEAD_DIM, (head + 1) * HEAD_DIM)
        mixed_ref[rows_of, :] = acc_ref[rows_of, :] * (1.0 / l_ref[head : head + 1, :])
    lse_ref[:HEADS, :] = m_ref[:HEADS, :] + jnp.log2(l_ref[:HEADS, :])
    gain = column(gain_ref[...])
    cot_t = cot_ref[...]
    cot = cot_t.T
    mixed_low = mixed_ref[...].astype(BF16)
    h = x_ref[...].astype(F32) + mm(wo_ref[...].T, mixed_low, 1, 0)
    scale = lax.rsqrt(jnp.mean(h * h, axis=0, keepdims=True) + epsilon)
    normed_t = (h * scale * gain).astype(BF16)
    normed = normed_t.T

    def start(chunk):
        cols = slice(chunk * CHUNK, (chunk + 1) * CHUNK)
        return (
            mm(normed, wg_ref[:, cols], 1, 0),
            mm(normed, wu_ref[:, cols], 1, 0),
            mm(cot, wd_ref[:, cols], 1, 0),
        )

    chunks = FF // CHUNK
    ahead = start(0)
    for chunk in range(chunks):
        gate, up, d_hidden = ahead
        if chunk + 1 < chunks:
            ahead = start(chunk + 1)
        cols = slice(chunk * CHUNK, (chunk + 1) * CHUNK)
        sig = 1.0 / (1.0 + jnp.exp2(gate * -log2e))
        silu = gate * sig
        hidden = (silu * up).astype(BF16)
        d_gate = (d_hidden * up * (sig * (1.0 + gate * (1.0 - sig)))).astype(BF16)
        d_up = (d_hidden * silu).astype(BF16)
        hid_ref[:, cols] = hidden
        dg_ref[:, cols] = d_gate
        du_ref[:, cols] = d_up
        stack_ref[:D, cols] = mm(normed_t, d_gate, 1, 0).astype(BF16)
        stack_ref[D : 2 * D, cols] = mm(normed_t, d_up, 1, 0).astype(BF16)
        stack_ref[2 * D : 3 * D, cols] = mm(cot_t, hidden, 1, 0).astype(BF16)
    y_ref[...] = (h + mm(wd_ref[...], hid_ref[...], 1, 1)).astype(BF16)
    dn = mm(wg_ref[...], dg_ref[...], 1, 1) + mm(wu_ref[...], du_ref[...], 1, 1)
    unit = h * scale
    gain_sum = jnp.sum(dn * unit, axis=1, keepdims=True)
    scaled = dn * gain
    dh = cot_t.astype(F32) + scale * (
        scaled - unit * jnp.mean(scaled * unit, axis=0, keepdims=True)
    )
    dh_ref[...] = dh
    dh_low = dh.astype(BF16)
    mixed = mixed_ref[...]
    d_mixed = mm(wo_ref[...], dh_low, 1, 0).astype(BF16)
    do_ref[...] = d_mixed
    for head in range(HEADS):
        rows_of = slice(head * HEAD_DIM, (head + 1) * HEAD_DIM)
        delta_ref[head : head + 1, :] = jnp.sum(
            d_mixed[rows_of].astype(F32) * mixed[rows_of], axis=0, keepdims=True
        )
    d_wo = mm(mixed_low, dh_low, 1, 1).astype(BF16)
    gain_row = jnp.broadcast_to(gain_sum, (D, 128)).T[:16].astype(BF16)
    quarter = D // 4
    base = 3 * D
    for k in range(4):
        cols = slice(k * PART, (k + 1) * PART)
        part = d_wo[k * quarter : (k + 1) * quarter]
        stack_ref[base : base + quarter, cols] = part[:, :PART]
        stack_ref[base + quarter : base + 2 * quarter, cols] = jnp.concatenate(
            [part[:, PART:], jnp.zeros((quarter, 2 * PART - D), BF16)], 1
        )
        stack_ref[base + 2 * quarter :, cols] = jnp.zeros((STACK - base - 2 * quarter, PART), BF16)
    stack_ref[base + 2 * quarter : base + 2 * quarter + 16, :D] = gain_row
    rows = keep_ref.shape[1]
    store_pieces(sc, sc[2], keep_ref, send_ref, lambda p: stack_ref[p * rows : (p + 1) * rows, :])


def middle(sc, acc, m, l, x, cot, gain, wo, wg, wu, wd, pieces):
    rows = x.shape[1]
    half = (pieces // 2, STACK // pieces, FF)
    args = (acc, m, l, x, cot, gain, wo, wg, wu, wd)
    outs = [
        ((D, rows), BF16),
        ((D, rows), BF16),
        ((16, rows), F32),
        ((16, rows), F32),
        ((D, rows), F32),
        (half, BF16),
        (half, BF16),
    ]
    return pl.pallas_call(
        middle_kernel,
        grid_spec=pltpu.PrefetchScalarGridSpec(
            num_scalar_prefetch=1,
            grid=(1,),
            in_specs=[whole(part.shape) for part in args],
            out_specs=[whole(shape) for shape, _ in outs],
            scratch_shapes=[
                pltpu.VMEM((D, rows), F32),
                pltpu.VMEM((STACK, FF), BF16),
                pltpu.VMEM((rows, FF), BF16),
                pltpu.VMEM((rows, FF), BF16),
                pltpu.VMEM((rows, FF), BF16),
            ],
        ),
        out_shape=[jax.ShapeDtypeStruct(*out) for out in outs],
        compiler_params=params(),
        cost_estimate=cost(),
        name="middle",
    )(sc, *args)


def last_kernel(
    sc,
    dq_ref,
    dkv_ref,
    n_ref,
    x_ref,
    dh_ref,
    gain_ref,
    wq_ref,
    wk_ref,
    wv_ref,
    cos_ref,
    sin_ref,
    dx_ref,
    keep_ref,
    send_ref,
):
    cos = cos_ref[...]
    sin = sin_ref[...]
    rows = x_ref.shape[1]
    d_query = rotated(dq_ref[...], cos, sin, HEAD_DIM**-0.5, -1.0).astype(BF16)
    turned = [dkv_ref[kv].astype(F32).T for kv in range(KV_HEADS)]
    d_key = rotated(
        jnp.concatenate([part[:HEAD_DIM] for part in turned], 0), cos, sin, ln2, -1.0
    ).astype(BF16)
    d_value = jnp.concatenate([part[HEAD_DIM:] for part in turned], 0).astype(BF16)
    dn = (
        mm(wq_ref[...], d_query, 1, 0)
        + mm(wk_ref[...], d_key, 0, 0)
        + mm(wv_ref[...], d_value, 0, 0)
    )
    x = x_ref[...].astype(F32)
    scale = lax.rsqrt(jnp.mean(x * x, axis=0, keepdims=True) + epsilon)
    unit = x * scale
    scaled = dn * column(gain_ref[...])
    dx_ref[...] = (
        dh_ref[...] + scale * (scaled - unit * jnp.mean(scaled * unit, axis=0, keepdims=True))
    ).astype(BF16)
    pad = 64
    joined = jnp.concatenate([d_query, jnp.zeros((pad, rows), BF16), d_key, d_value], 0)
    grad = mm(n_ref[...], joined, 1, 1)
    gain_sum = jnp.sum(dn * unit, axis=1, keepdims=True)
    spot = D // 128
    lane = lax.broadcasted_iota(jnp.int32, (D, 128), 1)
    mixed = jnp.where(
        lane < D - spot * 128, grad[:, spot * 128 : (spot + 1) * 128], gain_sum
    )
    tiles = [
        (mixed if i == spot else grad[:, i * 128 : (i + 1) * 128]).astype(BF16) for i in range(8)
    ]
    piece_rows = keep_ref.shape[1]

    def piece_of(piece):
        top = (piece // 8) * piece_rows
        count = max(min(piece_rows, D - top), 0)
        empty = jnp.zeros((piece_rows - count, 128), BF16)
        if count == 0:
            return empty
        part = tiles[piece % 8][top : top + count]
        return jnp.concatenate([part, empty], 0) if count < piece_rows else part

    store_pieces(sc, sc[3], keep_ref, send_ref, piece_of)


def last(sc, dq, dkv, n, x, dh, gain, wq, wk, wv, cos, sin, pieces):
    rows = x.shape[1]
    piece_rows = -(-D // max(pieces // 8, 1))
    half = (pieces // 2, -(-piece_rows // 16) * 16, 128)
    table = pl.BlockSpec((HALF, rows), lambda i, sc: (0, sc[0]))
    return pl.pallas_call(
        last_kernel,
        grid_spec=pltpu.PrefetchScalarGridSpec(
            num_scalar_prefetch=1,
            grid=(1,),
            in_specs=[whole(part.shape) for part in (dq, dkv, n, x, dh, gain, wq, wk, wv)]
            + [table, table],
            out_specs=[whole((D, rows)), whole(half), whole(half)],
        ),
        out_shape=[
            jax.ShapeDtypeStruct((D, rows), BF16),
            jax.ShapeDtypeStruct(half, BF16),
            jax.ShapeDtypeStruct(half, BF16),
        ],
        compiler_params=params(),
        cost_estimate=cost(),
        name="last",
    )(sc, dq, dkv, n, x, dh, gain, wq, wk, wv, cos, sin)


def unpack_big_kernel(sc, keep_ref, got_ref, gate_ref, up_ref, down_ref, wo_ref, gain_ref):
    step = pl.program_id(0)
    pairs, rows, _ = keep_ref.shape
    quarter = D // 4
    refs = (gate_ref, up_ref, down_ref)
    rest = []
    for pair in range(pairs):
        for side, part in enumerate(load_pair(sc, sc[2], keep_ref, got_ref, pair)):
            part = part.astype(F32)
            top = (2 * pair + side) * rows
            if top < 3 * D:
                refs[top // D][top % D : top % D + rows, :] = part
            else:
                rest.append(part)
    rest = jnp.concatenate(rest, 0)
    wo_ref[:, :PART] = rest[:quarter]
    wo_ref[:, PART:] = rest[quarter : 2 * quarter, : D - PART]
    row = rest[2 * quarter : 2 * quarter + 1]

    @pl.when(step == 0)
    def _():
        gain_ref[:, :PART] = row

    @pl.when(step == 1)
    def _():
        gain_ref[:, PART:] = row[:, : D - PART]


def unpack_big(sc, keep, got):
    shapes = [(D, FF), (D, FF), (D, FF), (D, D), (1, D)]
    cols = pl.BlockSpec((D, PART), lambda i, sc: (0, i))
    part = pl.BlockSpec(keep.shape[:2] + (PART,), lambda i, sc: (0, 0, i))
    return pl.pallas_call(
        unpack_big_kernel,
        grid_spec=pltpu.PrefetchScalarGridSpec(
            num_scalar_prefetch=1,
            grid=(FF // PART,),
            in_specs=[part, part],
            out_specs=[
                cols,
                cols,
                cols,
                pl.BlockSpec((D // 4, D), lambda i, sc: (i, 0)),
                whole((1, D)),
            ],
        ),
        out_shape=[jax.ShapeDtypeStruct(shape, F32) for shape in shapes],
        compiler_params=params(),
        cost_estimate=cost(),
        name="unpack_big",
    )(sc, keep, got)


def unpack_small_kernel(sc, keep_ref, got_ref, q_ref, k_ref, v_ref, gain_ref):
    pairs, rows, _ = keep_ref.shape
    columns = [[] for _ in range(8)]
    for pair in range(pairs):
        for side, part in enumerate(load_pair(sc, sc[3], keep_ref, got_ref, pair)):
            piece = 2 * pair + side
            count = min(rows, D - (piece // 8) * rows)
            if count > 0:
                columns[piece % 8].append(part[:count].astype(F32))
    full = [jnp.concatenate(parts, 0) if len(parts) > 1 else parts[0] for parts in columns]
    spot = D // 128
    for i in range(spot):
        q_ref[:, i * 128 : (i + 1) * 128] = full[i]
    q_ref[:, spot * 128 :] = full[spot][:, : D - spot * 128]
    gain_ref[...] = full[spot].T[D - spot * 128]
    key_value = jnp.concatenate(full[spot + 1 :], 1).T
    k_ref[...] = key_value[:KVD]
    v_ref[...] = key_value[KVD:]


def unpack_small(sc, keep, got):
    shapes = [(D, D), (KVD, D), (KVD, D), (D,)]
    return pl.pallas_call(
        unpack_small_kernel,
        grid_spec=pltpu.PrefetchScalarGridSpec(
            num_scalar_prefetch=1,
            grid=(1,),
            in_specs=[whole(keep.shape), whole(got.shape)],
            out_specs=[whole(shape) for shape in shapes],
        ),
        out_shape=[jax.ShapeDtypeStruct(shape, F32) for shape in shapes],
        compiler_params=params(),
        cost_estimate=cost(),
        name="unpack_small",
    )(sc, keep, got)


def plus(*parts):
    total = parts[0].astype(F32)
    for part in parts[1:]:
        total = total + part.astype(F32)
    return total.astype(BF16)


def swap(values, axis, size, flip):
    return lax.ppermute(values, axis, [(i, i ^ flip) for i in range(size)])


def direct_sum(values, axis, size, unit):
    share = values.shape[0] // size
    pieces = [values[i * share : (i + 1) * share] for i in range(size)]
    return plus(
        pieces[0], *[swap(pieces[i], axis, size * unit, i * unit) for i in range(1, size)]
    )


def direct_gather(values, axis, size, unit, gate=None):
    others = [swap(values, axis, size * unit, i * unit) for i in range(1, size)]
    if gate is not None:
        others = [after(other, gate) for other in others]
    return jnp.concatenate([values] + others, 0)


def after(value, *others):
    return lax.optimization_barrier((value,) + others)[0]


def build(seq_size, grp_size):
    count = seq_size * grp_size
    chips = seq_size // 2
    core = ("seq", seq_size, 1)

    def shards(
        inputs,
        lengths,
        attn_gain,
        w_query,
        w_key,
        w_value,
        w_out,
        ffn_gain,
        w_gate,
        w_up,
        w_down,
        cotangent,
    ):
        rows = inputs.shape[1]
        mine = lax.axis_index("seq")
        group = lax.axis_index("grp")
        sc = jnp.stack([mine, lengths[0], group * chips + mine // 2, group]).astype(jnp.int32)
        cos_np, sin_np = rope_tables(rows * seq_size)
        cos = jnp.asarray(cos_np)
        sin = jnp.asarray(sin_np)
        x = inputs[0].T
        cot = cotangent[0].T
        wk = w_key.T
        wv = w_value.T
        wd = w_down.T

        up = [(i, i + 2) for i in range(seq_size - 2)]
        down = [(i + 2, i) for i in range(seq_size - 2)]
        normed, query, own = first(sc, x, attn_gain, w_query, wk, wv, cos, sin)
        pairs = []
        state = None
        block = own
        for rank in range(chips):
            mate = swap(block if state is None else after(block, state[0]), *core)
            pairs.append((block, mate))
            if rank + 1 < chips:
                block = lax.ppermute(block, "seq", up)
            state = forward(sc, query, *pairs[-1], state, rank)
        m, l, acc = state
        outputs, d_mixed, lse, delta, d_resid, big, send = middle(
            sc, acc, m, l, x, cot, ffn_gain, w_out, w_gate, w_up, wd, count
        )
        over_grp = ("grp", grp_size, 1)
        over_chip = ("seq", chips, 2)

        dq = None
        passed = None
        for rank in reversed(range(chips)):
            if rank == chips - 2:
                big = plus(big, swap(send, *core))
                dq = after(dq, big)
            if rank == 0:
                big = direct_sum(big, *over_grp)
                dq = after(dq, big)
            dq, grad_a, grad_b = backward(
                sc, query, d_mixed, lse, delta, *pairs[rank], dq, rank
            )
            terms = [grad_a, swap(grad_b, *core)]
            if passed is not None:
                terms.append(lax.ppermute(passed, "seq", down))
            passed = plus(*terms)
        big = direct_sum(big, *over_chip)
        dq = after(dq, big)

        d_inputs, small, small_send = last(
            sc, dq, passed, normed, x, d_resid, attn_gain, w_query, wk, wv, cos, sin, 2 * grp_size
        )
        big = direct_gather(big, *over_chip)
        small = plus(small, swap(small_send, *core))
        grp_flips = [1 << bit for bit in range(grp_size.bit_length() - 1)]
        for flip in reversed(grp_flips):
            half = small.shape[0] // 2
            small = plus(small[:half], swap(small[half:], "grp", grp_size, flip))
        for bit in range(chips.bit_length() - 1):
            small = plus(small, swap(small, "seq", seq_size, 2 << bit))
        big = direct_gather(big, *over_grp, gate=small)
        for flip in grp_flips:
            small = jnp.concatenate([small, swap(small, "grp", grp_size, flip)], 0)
        d_query, d_key, d_value, d_attn_gain = unpack_small(sc, small, swap(small, *core))
        d_gate, d_up, d_down, d_out, d_ffn_gain = unpack_big(sc, big, swap(big, *core))
        return (
            outputs.T[None],
            d_inputs.T[None],
            d_attn_gain,
            d_query,
            d_key.T,
            d_value.T,
            d_out,
            d_ffn_gain.reshape(D),
            d_gate,
            d_up,
            d_down.T,
        )

    return shards


def solution(mesh):
    tokens = P("grp", "seq", None)
    return jax.shard_map(
        build(mesh.shape["seq"], mesh.shape["grp"]),
        mesh=mesh,
        in_specs=(tokens, P("grp")) + (P(),) * 9 + (tokens,),
        out_specs=(tokens, tokens) + (P(),) * 9,
        check_vma=False,
    )
```

```python
import functools
import math

import jax
import jax.numpy as jnp
import numpy as np
from jax import lax
from jax.experimental import pallas as pl
from jax.experimental.pallas import tpu as pltpu
from jax.sharding import PartitionSpec as P

D = 576
KV_HEADS = 3
HEAD_DIM = 64
REP = 3
HEADS = KV_HEADS * REP
KVD = 192
FF = 1536
CHUNK = 512
STACK = 2048
PART = 384
HALF = HEAD_DIM // 2

epsilon = 1e-05
rope_base = 100000.0
neg_big = -1e30
log2e = math.log2(math.e)
ln2 = math.log(2.0)

F32 = jnp.float32
BF16 = jnp.bfloat16


def mm(left, right, left_dim, right_dim):
    return lax.dot_general(
        left, right, (((left_dim,), (right_dim,)), ((), ())), preferred_element_type=F32
    )


def params(mebibytes):
    return pltpu.CompilerParams(vmem_limit_bytes=mebibytes * 2**20)


def whole(shape):
    return pl.BlockSpec(shape, lambda *_: (0,) * len(shape))


def cost():
    return pl.CostEstimate(flops=10**8, bytes_accessed=2**17, transcendentals=0)


def rope_tables(length):
    steps = np.arange(HALF, dtype=np.float32)
    freqs = (1.0 / np.float32(rope_base) ** (steps * np.float32(2.0) / np.float32(HEAD_DIM))).astype(
        np.float32
    )
    angles = np.arange(length, dtype=np.float32)[None, :] * freqs[:, None]
    return np.cos(angles).astype(np.float32), np.sin(angles).astype(np.float32)


def rotated(rows, cos, sin, scale, sign):
    parts = []
    for start in range(0, rows.shape[0], HEAD_DIM):
        one = rows[start : start + HALF]
        two = rows[start + HALF : start + HEAD_DIM]
        parts.append((one * cos - sign * (two * sin)) * scale)
        parts.append((two * cos + sign * (one * sin)) * scale)
    return jnp.concatenate(parts, 0)


def column(vector):
    return jnp.broadcast_to(vector[None], (8, vector.shape[0])).T[:, :1]


def first_kernel(sc, x_ref, gain_ref, wq_ref, wk_ref, wv_ref, cos_ref, sin_ref, n_ref, q_ref, kv_ref):
    x = x_ref[...].astype(F32)
    scale = lax.rsqrt(jnp.mean(x * x, axis=0, keepdims=True) + epsilon)
    normed = (x * scale * column(gain_ref[...])).astype(BF16)
    n_ref[...] = normed
    cos = cos_ref[...]
    sin = sin_ref[...]
    key = mm(wk_ref[...], normed, 1, 0)
    kv_ref[:KVD, :] = rotated(key, cos, sin, 1.0, 1.0).astype(BF16)
    kv_ref[KVD:, :] = mm(wv_ref[...], normed, 1, 0).astype(BF16)
    query = mm(wq_ref[...].T, normed, 1, 0)
    q_ref[...] = rotated(query, cos, sin, HEAD_DIM**-0.5 * log2e, 1.0).astype(BF16)


def first(sc, x, gain, wq, wk, wv, cos, sin):
    rows = x.shape[1]
    return pl.pallas_call(
        first_kernel,
        grid_spec=pltpu.PrefetchScalarGridSpec(
            num_scalar_prefetch=1,
            grid=(1,),
            in_specs=[
                whole(x.shape),
                whole(gain.shape),
                whole(wq.shape),
                whole(wk.shape),
                whole(wv.shape),
                pl.BlockSpec((HALF, rows), lambda i, sc: (0, sc[0])),
                pl.BlockSpec((HALF, rows), lambda i, sc: (0, sc[0])),
            ],
            out_specs=[whole((D, rows)), whole((D, rows)), whole((2 * KVD, rows))],
        ),
        out_shape=[
            jax.ShapeDtypeStruct((D, rows), BF16),
            jax.ShapeDtypeStruct((D, rows), BF16),
            jax.ShapeDtypeStruct((2 * KVD, rows), BF16),
        ],
        compiler_params=params(16),
        cost_estimate=cost(),
        name="first",
    )(sc, x, gain, wq, wk, wv, cos, sin)


def block_facts(sc, rank, which, rows):
    mine = sc[0]
    block = mine - 2 * rank if which == 0 else (mine ^ 1) - 2 * rank
    length = sc[1]
    start = block * rows
    active = (block >= 0) & (block <= mine) & (start < length)
    partial = (block == mine) | (start + rows > length)
    pos = mine * rows + lax.broadcasted_iota(jnp.int32, (1, rows), 1)
    bound = jnp.minimum(pos, length - 1) - start
    return active, partial, bound


def masked_scores(scores, bound):
    rows = lax.broadcasted_iota(jnp.int32, scores.shape, 0)
    return jnp.where(rows <= bound, scores, neg_big)


def forward_block(hidden_keys, bound, kv_ref, q_ref, m_ref, l_ref, acc_ref):
    rows = q_ref.shape[1]
    keys = kv_ref[:KVD, :].T
    ones = jnp.ones((8, rows), BF16)

    def score(head):
        kv = head // REP
        scores = mm(
            keys[:, kv * HEAD_DIM : (kv + 1) * HEAD_DIM],
            q_ref[head * HEAD_DIM : (head + 1) * HEAD_DIM, :],
            1,
            0,
        )
        if hidden_keys:
            scores = masked_scores(scores, bound)
        return scores, jnp.max(scores, axis=0, keepdims=True)

    def weigh(head, scores, top):
        kv = head // REP
        old = m_ref[head : head + 1, :]
        new = jnp.maximum(old, top)
        weights = jnp.exp2(scores - new).astype(BF16)
        values = jnp.concatenate(
            [kv_ref[KVD + kv * HEAD_DIM : KVD + (kv + 1) * HEAD_DIM, :], ones], 0
        )
        return new, jnp.exp2(old - new), mm(values, weights, 1, 0)

    def store(head, new, fade, out):
        rows_of = slice(head * HEAD_DIM, (head + 1) * HEAD_DIM)
        m_ref[head : head + 1, :] = new
        l_ref[head : head + 1, :] = l_ref[head : head + 1, :] * fade + out[HEAD_DIM : HEAD_DIM + 1]
        acc_ref[rows_of, :] = acc_ref[rows_of, :] * fade + out[:HEAD_DIM]

    ahead = score(0)
    held = None
    for head in range(HEADS):
        current = ahead
        if head + 1 < HEADS:
            ahead = score(head + 1)
        result = weigh(head, *current)
        if held is not None:
            store(*held)
        held = (head,) + result
    store(*held)


def forward_kernel(sc, q_ref, a_ref, b_ref, *refs, rank, fresh):
    rows = q_ref.shape[1]
    which = pl.program_id(0)
    m_ref, l_ref, acc_ref, kv_ref = refs[-4:]

    @pl.when(which == 0)
    def _():
        if fresh:
            m_ref[...] = jnp.full_like(m_ref, neg_big)
            l_ref[...] = jnp.zeros_like(l_ref)
            acc_ref[...] = jnp.zeros_like(acc_ref)
        else:
            m_ref[...] = refs[0][...]
            l_ref[...] = refs[1][...]
            acc_ref[...] = refs[2][...]
        kv_ref[...] = a_ref[...]

    @pl.when(which == 1)
    def _():
        kv_ref[...] = b_ref[...]

    first_facts = block_facts(sc, rank, 0, rows)
    second_facts = block_facts(sc, rank, 1, rows)
    active, partial, bound = [
        jnp.where(which == 0, one, two) for one, two in zip(first_facts, second_facts)
    ]

    @pl.when(active & jnp.logical_not(partial))
    def _():
        forward_block(False, bound, kv_ref, q_ref, m_ref, l_ref, acc_ref)

    @pl.when(active & partial)
    def _():
        forward_block(True, bound, kv_ref, q_ref, m_ref, l_ref, acc_ref)


def forward(sc, q, a, b, state, rank):
    rows = q.shape[1]
    state = () if state is None else tuple(state)
    return pl.pallas_call(
        functools.partial(forward_kernel, rank=rank, fresh=not state),
        grid_spec=pltpu.PrefetchScalarGridSpec(
            num_scalar_prefetch=1,
            grid=(2,),
            in_specs=[whole(q.shape), whole(a.shape), whole(b.shape)]
            + [whole(part.shape) for part in state],
            out_specs=[whole((16, rows)), whole((16, rows)), whole((D, rows))],
            scratch_shapes=[pltpu.VMEM(a.shape, BF16)],
        ),
        out_shape=[
            jax.ShapeDtypeStruct((16, rows), F32),
            jax.ShapeDtypeStruct((16, rows), F32),
            jax.ShapeDtypeStruct((D, rows), F32),
        ],
        compiler_params=params(20),
        cost_estimate=cost(),
        name=f"forward_{rank}",
    )(sc, q, a, b, *state)


def backward_block(hidden_keys, bound, kv_ref, q_ref, do_ref, lse_ref, delta_ref, dq_ref, out_ref):
    keys = kv_ref[:KVD, :].T
    values = kv_ref[KVD:, :].T

    def start(head):
        kv = head // REP
        lanes = slice(kv * HEAD_DIM, (kv + 1) * HEAD_DIM)
        rows_of = slice(head * HEAD_DIM, (head + 1) * HEAD_DIM)
        scores = mm(keys[:, lanes], q_ref[rows_of, :], 1, 0)
        if hidden_keys:
            scores = masked_scores(scores, bound)
        return scores, mm(values[:, lanes], do_ref[rows_of, :], 1, 0)

    ahead = start(0)
    for head in range(HEADS):
        kv = head // REP
        rows_of = slice(head * HEAD_DIM, (head + 1) * HEAD_DIM)
        scores, d_probs = ahead
        if head + 1 < HEADS:
            ahead = start(head + 1)
        probs = jnp.exp2(scores - lse_ref[head : head + 1, :])
        d_scores = (probs * (d_probs - delta_ref[head : head + 1, :])).astype(BF16)
        value_term = mm(probs.astype(BF16), do_ref[rows_of, :], 1, 1)
        key_term = mm(d_scores, q_ref[rows_of, :], 1, 1)
        first_rep = head % REP == 0
        d_value = value_term if first_rep else d_value + value_term
        d_key = key_term if first_rep else d_key + key_term
        dq_ref[rows_of, :] = dq_ref[rows_of, :] + mm(
            kv_ref[kv * HEAD_DIM : (kv + 1) * HEAD_DIM, :], d_scores, 1, 0
        )
        if head % REP == REP - 1:
            out_ref[kv] = jnp.concatenate([d_key, d_value], 1).astype(BF16)


def backward_kernel(sc, q_ref, do_ref, lse_ref, delta_ref, kv_ref, *refs, rank, which):
    dq_ref, out_ref = refs[-2:]
    dq_ref[...] = refs[0][...] if len(refs) == 3 else jnp.zeros_like(dq_ref)
    active, partial, bound = block_facts(sc, rank, which, q_ref.shape[1])
    rest = (kv_ref, q_ref, do_ref, lse_ref, delta_ref, dq_ref, out_ref)

    @pl.when(active & jnp.logical_not(partial))
    def _():
        backward_block(False, bound, *rest)

    @pl.when(active & partial)
    def _():
        backward_block(True, bound, *rest)

    @pl.when(jnp.logical_not(active))
    def _():
        out_ref[...] = jnp.zeros_like(out_ref)


def backward(sc, q, d_out, lse, delta, kv, dq, rank, which):
    rows = q.shape[1]
    args = (q, d_out, lse, delta, kv) + (() if dq is None else (dq,))
    grads = (KV_HEADS, rows, 2 * HEAD_DIM)
    return pl.pallas_call(
        functools.partial(backward_kernel, rank=rank, which=which),
        grid_spec=pltpu.PrefetchScalarGridSpec(
            num_scalar_prefetch=1,
            grid=(1,),
            in_specs=[whole(part.shape) for part in args],
            out_specs=[whole((D, rows)), whole(grads)],
        ),
        out_shape=[
            jax.ShapeDtypeStruct((D, rows), F32),
            jax.ShapeDtypeStruct(grads, BF16),
        ],
        compiler_params=params(20),
        cost_estimate=cost(),
        name=f"backward_{rank}_{which}",
    )(sc, *args)


def store_pieces(sc, order, spot, keep_ref, send_ref, piece_of):
    low = (sc[0] & 1) == 0
    for pair in range(keep_ref.shape[0]):
        even = piece_of(2 * pair)
        odd = piece_of(2 * pair + 1)
        keep_ref[order[pair] ^ spot] = jnp.where(low, even, odd)
        send_ref[order[pair] ^ spot] = jnp.where(low, odd, even)


def load_pair(sc, order, spot, keep_ref, got_ref, pair):
    low = (sc[0] & 1) == 0
    one = keep_ref[order[pair] ^ spot]
    two = got_ref[order[pair] ^ spot]
    return jnp.where(low, one, two), jnp.where(low, two, one)


def middle_kernel(
    sc,
    acc_ref,
    m_ref,
    l_ref,
    x_ref,
    cot_ref,
    gain_ref,
    wo_ref,
    wg_ref,
    wu_ref,
    wd_ref,
    y_ref,
    do_ref,
    lse_ref,
    delta_ref,
    dh_ref,
    keep_ref,
    send_ref,
    keep_b_ref,
    send_b_ref,
    mixed_ref,
    stack_ref,
    hid_ref,
    dg_ref,
    du_ref,
    *,
    orders,
):
    for head in range(HEADS):
        rows_of = slice(head * HEAD_DIM, (head + 1) * HEAD_DIM)
        mixed_ref[rows_of, :] = acc_ref[rows_of, :] * (1.0 / l_ref[head : head + 1, :])
    lse_ref[:HEADS, :] = m_ref[:HEADS, :] + jnp.log2(l_ref[:HEADS, :])
    gain = column(gain_ref[...])
    cot_t = cot_ref[...]
    cot = cot_t.T
    mixed_low = mixed_ref[...].astype(BF16)
    h = x_ref[...].astype(F32) + mm(wo_ref[...].T, mixed_low, 1, 0)
    scale = lax.rsqrt(jnp.mean(h * h, axis=0, keepdims=True) + epsilon)
    normed_t = (h * scale * gain).astype(BF16)
    normed = normed_t.T

    def start(chunk):
        cols = slice(chunk * CHUNK, (chunk + 1) * CHUNK)
        return (
            mm(normed, wg_ref[:, cols], 1, 0),
            mm(normed, wu_ref[:, cols], 1, 0),
            mm(cot, wd_ref[:, cols], 1, 0),
        )

    chunks = FF // CHUNK
    ahead = start(0)
    for chunk in range(chunks):
        gate, up, d_hidden = ahead
        if chunk + 1 < chunks:
            ahead = start(chunk + 1)
        cols = slice(chunk * CHUNK, (chunk + 1) * CHUNK)
        sig = 1.0 / (1.0 + jnp.exp2(gate * -log2e))
        silu = gate * sig
        hidden = (silu * up).astype(BF16)
        d_gate = (d_hidden * up * (sig * (1.0 + gate * (1.0 - sig)))).astype(BF16)
        d_up = (d_hidden * silu).astype(BF16)
        hid_ref[:, cols] = hidden
        dg_ref[:, cols] = d_gate
        du_ref[:, cols] = d_up
        stack_ref[:D, cols] = mm(normed_t, d_gate, 1, 0).astype(BF16)
        stack_ref[D : 2 * D, cols] = mm(normed_t, d_up, 1, 0).astype(BF16)
        stack_ref[2 * D : 3 * D, cols] = mm(cot_t, hidden, 1, 0).astype(BF16)
    y_ref[...] = (h + mm(wd_ref[...], hid_ref[...], 1, 1)).astype(BF16)
    dn = mm(wg_ref[...], dg_ref[...], 1, 1) + mm(wu_ref[...], du_ref[...], 1, 1)
    unit = h * scale
    gain_sum = jnp.sum(dn * unit, axis=1, keepdims=True)
    scaled = dn * gain
    dh = cot_t.astype(F32) + scale * (
        scaled - unit * jnp.mean(scaled * unit, axis=0, keepdims=True)
    )
    dh_ref[...] = dh
    dh_low = dh.astype(BF16)
    mixed = mixed_ref[...]
    d_mixed = mm(wo_ref[...], dh_low, 1, 0).astype(BF16)
    do_ref[...] = d_mixed
    for head in range(HEADS):
        rows_of = slice(head * HEAD_DIM, (head + 1) * HEAD_DIM)
        delta_ref[head : head + 1, :] = jnp.sum(
            d_mixed[rows_of].astype(F32) * mixed[rows_of], axis=0, keepdims=True
        )
    d_wo = mm(mixed_low, dh_low, 1, 1).astype(BF16)
    gain_row = jnp.broadcast_to(gain_sum, (D, 128)).T[:16].astype(BF16)
    quarter = D // 4
    base = 3 * D
    for k in range(4):
        cols = slice(k * PART, (k + 1) * PART)
        part = d_wo[k * quarter : (k + 1) * quarter]
        stack_ref[base : base + quarter, cols] = part[:, :PART]
        stack_ref[base + quarter : base + 2 * quarter, cols] = jnp.concatenate(
            [part[:, PART:], jnp.zeros((quarter, 2 * PART - D), BF16)], 1
        )
        stack_ref[base + 2 * quarter :, cols] = jnp.zeros((STACK - base - 2 * quarter, PART), BF16)
    stack_ref[base + 2 * quarter : base + 2 * quarter + 16, :D] = gain_row
    rows = keep_ref.shape[1]
    half = FF // 2
    store_pieces(
        sc, orders[0], sc[2], keep_ref, send_ref, lambda p: stack_ref[p * rows : (p + 1) * rows, :half]
    )
    store_pieces(
        sc, orders[1], sc[3], keep_b_ref, send_b_ref, lambda p: stack_ref[p * rows : (p + 1) * rows, half:]
    )


def middle(sc, acc, m, l, x, cot, gain, wo, wg, wu, wd, orders):
    rows = x.shape[1]
    pairs = len(orders[0])
    half = (pairs, STACK // (2 * pairs), FF // 2)
    args = (acc, m, l, x, cot, gain, wo, wg, wu, wd)
    outs = [
        ((D, rows), BF16),
        ((D, rows), BF16),
        ((16, rows), F32),
        ((16, rows), F32),
        ((D, rows), F32),
        (half, BF16),
        (half, BF16),
        (half, BF16),
        (half, BF16),
    ]
    return pl.pallas_call(
        functools.partial(middle_kernel, orders=orders),
        grid_spec=pltpu.PrefetchScalarGridSpec(
            num_scalar_prefetch=1,
            grid=(1,),
            in_specs=[whole(part.shape) for part in args],
            out_specs=[whole(shape) for shape, _ in outs],
            scratch_shapes=[
                pltpu.VMEM((D, rows), F32),
                pltpu.VMEM((STACK, FF), BF16),
                pltpu.VMEM((rows, FF), BF16),
                pltpu.VMEM((rows, FF), BF16),
                pltpu.VMEM((rows, FF), BF16),
            ],
        ),
        out_shape=[jax.ShapeDtypeStruct(*out) for out in outs],
        compiler_params=params(48),
        cost_estimate=cost(),
        name="middle",
    )(sc, *args)


def last_kernel(
    sc,
    dq_ref,
    dkv_ref,
    n_ref,
    x_ref,
    dh_ref,
    gain_ref,
    wq_ref,
    wk_ref,
    wv_ref,
    cos_ref,
    sin_ref,
    dx_ref,
    keep_ref,
    send_ref,
):
    cos = cos_ref[...]
    sin = sin_ref[...]
    rows = x_ref.shape[1]
    d_query = rotated(dq_ref[...], cos, sin, HEAD_DIM**-0.5, -1.0).astype(BF16)
    turned = [dkv_ref[kv].astype(F32).T for kv in range(KV_HEADS)]
    d_key = rotated(
        jnp.concatenate([part[:HEAD_DIM] for part in turned], 0), cos, sin, ln2, -1.0
    ).astype(BF16)
    d_value = jnp.concatenate([part[HEAD_DIM:] for part in turned], 0).astype(BF16)
    dn = (
        mm(wq_ref[...], d_query, 1, 0)
        + mm(wk_ref[...], d_key, 0, 0)
        + mm(wv_ref[...], d_value, 0, 0)
    )
    x = x_ref[...].astype(F32)
    scale = lax.rsqrt(jnp.mean(x * x, axis=0, keepdims=True) + epsilon)
    unit = x * scale
    scaled = dn * column(gain_ref[...])
    dx_ref[...] = (
        dh_ref[...] + scale * (scaled - unit * jnp.mean(scaled * unit, axis=0, keepdims=True))
    ).astype(BF16)
    pad = 64
    joined = jnp.concatenate([d_query, jnp.zeros((pad, rows), BF16), d_key, d_value], 0)
    grad = mm(n_ref[...], joined, 1, 1)
    gain_sum = jnp.sum(dn * unit, axis=1, keepdims=True)
    spot = D // 128
    lane = lax.broadcasted_iota(jnp.int32, (D, 128), 1)
    mixed = jnp.where(
        lane < D - spot * 128, grad[:, spot * 128 : (spot + 1) * 128], gain_sum
    )
    tiles = [
        (mixed if i == spot else grad[:, i * 128 : (i + 1) * 128]).astype(BF16) for i in range(8)
    ]
    piece_rows = keep_ref.shape[1]

    def piece_of(piece):
        top = (piece // 8) * piece_rows
        count = max(min(piece_rows, D - top), 0)
        empty = jnp.zeros((piece_rows - count, 128), BF16)
        if count == 0:
            return empty
        part = tiles[piece % 8][top : top + count]
        return jnp.concatenate([part, empty], 0) if count < piece_rows else part

    store_pieces(sc, range(keep_ref.shape[0]), sc[4], keep_ref, send_ref, piece_of)


def last(sc, dq, dkv, n, x, dh, gain, wq, wk, wv, cos, sin, pieces):
    rows = x.shape[1]
    piece_rows = -(-D // max(pieces // 8, 1))
    half = (pieces // 2, -(-piece_rows // 16) * 16, 128)
    table = pl.BlockSpec((HALF, rows), lambda i, sc: (0, sc[0]))
    return pl.pallas_call(
        last_kernel,
        grid_spec=pltpu.PrefetchScalarGridSpec(
            num_scalar_prefetch=1,
            grid=(1,),
            in_specs=[whole(part.shape) for part in (dq, dkv, n, x, dh, gain, wq, wk, wv)]
            + [table, table],
            out_specs=[whole((D, rows)), whole(half), whole(half)],
        ),
        out_shape=[
            jax.ShapeDtypeStruct((D, rows), BF16),
            jax.ShapeDtypeStruct(half, BF16),
            jax.ShapeDtypeStruct(half, BF16),
        ],
        compiler_params=params(24),
        cost_estimate=cost(),
        name="last",
    )(sc, dq, dkv, n, x, dh, gain, wq, wk, wv, cos, sin)


def unpack_big_kernel(
    sc, keep_ref, got_ref, keep_b_ref, got_b_ref, gate_ref, up_ref, down_ref, wo_ref, gain_ref, *, orders
):
    step = pl.program_id(0)
    quarter = D // 4
    refs = (gate_ref, up_ref, down_ref)

    def unpack(one_ref, two_ref, order, spot):
        pairs, rows, _ = one_ref.shape
        rest = []
        for pair in range(pairs):
            for side, part in enumerate(load_pair(sc, order, spot, one_ref, two_ref, pair)):
                part = part.astype(F32)
                top = (2 * pair + side) * rows
                if top < 3 * D:
                    refs[top // D][top % D : top % D + rows, :] = part
                else:
                    rest.append(part)
        rest = jnp.concatenate(rest, 0)
        wo_ref[:, :PART] = rest[:quarter]
        wo_ref[:, PART:] = rest[quarter : 2 * quarter, : D - PART]
        return rest[2 * quarter : 2 * quarter + 1]

    @pl.when(step < 2)
    def _():
        row = unpack(keep_ref, got_ref, orders[0], sc[2])

        @pl.when(step == 0)
        def _():
            gain_ref[:, :PART] = row

        @pl.when(step == 1)
        def _():
            gain_ref[:, PART:] = row[:, : D - PART]

    @pl.when(step >= 2)
    def _():
        unpack(keep_b_ref, got_b_ref, orders[1], sc[3])


def unpack_big(sc, keep, got, keep_b, got_b, orders):
    shapes = [(D, FF), (D, FF), (D, FF), (D, D), (1, D)]
    cols = pl.BlockSpec((D, PART), lambda i, sc: (0, i))
    block = keep.shape[:2] + (PART,)
    early = pl.BlockSpec(block, lambda i, sc: (0, 0, jnp.minimum(i, 1)))
    late = pl.BlockSpec(block, lambda i, sc: (0, 0, jnp.maximum(i - 2, 0)))
    return pl.pallas_call(
        functools.partial(unpack_big_kernel, orders=orders),
        grid_spec=pltpu.PrefetchScalarGridSpec(
            num_scalar_prefetch=1,
            grid=(FF // PART,),
            in_specs=[early, early, late, late],
            out_specs=[
                cols,
                cols,
                cols,
                pl.BlockSpec((D // 4, D), lambda i, sc: (i, 0)),
                whole((1, D)),
            ],
        ),
        out_shape=[jax.ShapeDtypeStruct(shape, F32) for shape in shapes],
        compiler_params=params(32),
        cost_estimate=cost(),
        name="unpack_big",
    )(sc, keep, got, keep_b, got_b)


def unpack_small_kernel(sc, keep_ref, got_ref, q_ref, k_ref, v_ref, gain_ref):
    pairs, rows, _ = keep_ref.shape
    columns = [[] for _ in range(8)]
    for pair in range(pairs):
        for side, part in enumerate(load_pair(sc, range(pairs), sc[4], keep_ref, got_ref, pair)):
            piece = 2 * pair + side
            count = min(rows, D - (piece // 8) * rows)
            if count > 0:
                columns[piece % 8].append(part[:count].astype(F32))
    full = [jnp.concatenate(parts, 0) if len(parts) > 1 else parts[0] for parts in columns]
    spot = D // 128
    for i in range(spot):
        q_ref[:, i * 128 : (i + 1) * 128] = full[i]
    q_ref[:, spot * 128 :] = full[spot][:, : D - spot * 128]
    gain_ref[...] = full[spot].T[D - spot * 128]
    key_value = jnp.concatenate(full[spot + 1 :], 1).T
    k_ref[...] = key_value[:KVD]
    v_ref[...] = key_value[KVD:]


def unpack_small(sc, keep, got):
    shapes = [(D, D), (KVD, D), (KVD, D), (D,)]
    return pl.pallas_call(
        unpack_small_kernel,
        grid_spec=pltpu.PrefetchScalarGridSpec(
            num_scalar_prefetch=1,
            grid=(1,),
            in_specs=[whole(keep.shape), whole(got.shape)],
            out_specs=[whole(shape) for shape in shapes],
        ),
        out_shape=[jax.ShapeDtypeStruct(shape, F32) for shape in shapes],
        compiler_params=params(16),
        cost_estimate=cost(),
        name="unpack_small",
    )(sc, keep, got)


def plus(*parts):
    total = parts[0].astype(F32)
    for part in parts[1:]:
        total = total + part.astype(F32)
    return total.astype(BF16)


def swap(values, axis, size, flip):
    return lax.ppermute(values, axis, [(i, i ^ flip) for i in range(size)])


def halved(values, step):
    half = values.shape[0] // 2
    return plus(values[:half], swap(values[half:], *step))


def doubled(values, step):
    return jnp.concatenate([values, swap(values, *step)], 0)


def spread_bits(value, places):
    count = len(places)
    total = 0
    for t, bit in enumerate(places):
        total = total | (((value >> bit) & 1) << (count - 1 - t))
    return total


def after(value, *others):
    return lax.optimization_barrier((value,) + others)[0]


def build(seq_size, grp_size):
    count = seq_size * grp_size
    chips = seq_size // 2
    core = ("seq", seq_size, 1)
    chip_bits = list(range(chips.bit_length() - 1))
    grp_bits = list(range(grp_size.bit_length() - 1))
    chip_steps = [("seq", seq_size, 2 << bit) for bit in chip_bits]
    grp_steps = [("grp", grp_size, 1 << bit) for bit in grp_bits]
    grp_places = [len(chip_bits) + bit for bit in grp_bits]
    plans = [grp_steps + chip_steps, grp_steps[::-1] + chip_steps]
    places = [grp_places + chip_bits, grp_places[::-1] + chip_bits]
    orders = [[spread_bits(j, spots) for j in range(count // 2)] for spots in places]

    def shards(
        inputs,
        lengths,
        attn_gain,
        w_query,
        w_key,
        w_value,
        w_out,
        ffn_gain,
        w_gate,
        w_up,
        w_down,
        cotangent,
    ):
        rows = inputs.shape[1]
        mine = lax.axis_index("seq")
        group = lax.axis_index("grp")
        number = group * chips + lax.shift_right_logical(mine, 1)
        sc = jnp.stack(
            [mine, lengths[0]] + [spread_bits(number, spots) for spots in places] + [group]
        ).astype(jnp.int32)
        cos_np, sin_np = rope_tables(rows * seq_size)
        cos = jnp.asarray(cos_np)
        sin = jnp.asarray(sin_np)
        x = inputs[0].T
        cot = cotangent[0].T
        wk = w_key.T
        wv = w_value.T
        wd = w_down.T

        up = [(i, i + 2) for i in range(seq_size - 2)]
        down = [(i + 2, i) for i in range(seq_size - 2)]
        normed, query, own = first(sc, x, attn_gain, w_query, wk, wv, cos, sin)
        pairs = []
        state = None
        block = own
        for rank in range(chips):
            mate = swap(block if state is None else after(block, state[0]), *core)
            pairs.append((block, mate))
            if rank + 1 < chips:
                block = lax.ppermute(block, "seq", up)
            state = forward(sc, query, *pairs[-1], state, rank)
        m, l, acc = state
        outputs, d_mixed, lse, delta, d_resid, *halves = middle(
            sc, acc, m, l, x, cot, ffn_gain, w_out, w_gate, w_up, wd, orders
        )
        sends = halves[1::2]
        big = halves[::2]

        stages = [lambda parts: [plus(part, swap(send, *core)) for part, send in zip(parts, sends)]]
        for pair in zip(*plans):
            stages.append(lambda parts, pair=pair: [halved(p, s) for p, s in zip(parts, pair)])
        gathers = [
            lambda parts, pair=pair: [doubled(p, s) for p, s in zip(parts, pair)]
            for pair in list(zip(*plans))[::-1]
        ]
        stages = stages + gathers[: len(chip_steps) - 1]
        late = gathers[len(chip_steps) - 1 :]
        when = [1, 4, 6] + list(range(7, 2 * seq_size))
        dq = None
        passed = None
        calls = 0
        for rank in reversed(range(chips)):
            grads = [None, None]
            for which in (1, 0):
                if calls in when and stages:
                    big = stages.pop(0)(big)
                    dq = after(dq, *big)
                dq, grads[which] = backward(
                    sc, query, d_mixed, lse, delta, pairs[rank][which], dq, rank, which
                )
                calls += 1
            terms = [grads[0], swap(grads[1], *core)]
            if passed is not None:
                terms.append(lax.ppermute(passed, "seq", down))
            passed = plus(*terms)
        while stages:
            big = stages.pop(0)(big)
        dq = after(dq, *big)

        d_inputs, small, small_send = last(
            sc, dq, passed, normed, x, d_resid, attn_gain, w_query, wk, wv, cos, sin, 2 * grp_size
        )
        for stage in late[:-1]:
            big = stage(big)
        small = plus(small, swap(small_send, *core))
        for step in grp_steps[::-1]:
            small = halved(small, step)
        big = late[-1]([after(part, small) for part in big])
        for step in chip_steps:
            small = plus(small, swap(small, *step))
        for step in grp_steps:
            small = doubled(small, step)
        d_query, d_key, d_value, d_attn_gain = unpack_small(sc, small, swap(small, *core))
        d_gate, d_up, d_down, d_out, d_ffn_gain = unpack_big(
            sc, big[0], swap(big[0], *core), big[1], swap(big[1], *core), orders
        )
        return (
            outputs.T[None],
            d_inputs.T[None],
            d_attn_gain,
            d_query,
            d_key.T,
            d_value.T,
            d_out,
            d_ffn_gain.reshape(D),
            d_gate,
            d_up,
            d_down.T,
        )

    return shards


def solution(mesh):
    tokens = P("grp", "seq", None)
    return jax.shard_map(
        build(mesh.shape["seq"], mesh.shape["grp"]),
        mesh=mesh,
        in_specs=(tokens, P("grp")) + (P(),) * 9 + (tokens,),
        out_specs=(tokens, tokens) + (P(),) * 9,
        check_vma=False,
    )
```

```python
import functools
import math

import jax
import jax.numpy as jnp
import numpy as np
from jax import lax
from jax.experimental import pallas as pl
from jax.experimental.pallas import tpu as pltpu
from jax.sharding import PartitionSpec as P

D = 576
KV_HEADS = 3
HEAD_DIM = 64
REP = 3
HEADS = KV_HEADS * REP
KVD = 192
FF = 1536
CHUNK = 512
STACK = 2048
PART = 384
HALF = HEAD_DIM // 2

epsilon = 1e-05
rope_base = 100000.0
neg_big = -1e30
log2e = math.log2(math.e)
ln2 = math.log(2.0)

F32 = jnp.float32
BF16 = jnp.bfloat16


def mm(left, right, left_dim, right_dim):
    return lax.dot_general(
        left, right, (((left_dim,), (right_dim,)), ((), ())), preferred_element_type=F32
    )


def params(mebibytes):
    return pltpu.CompilerParams(vmem_limit_bytes=mebibytes * 2**20)


def whole(shape):
    return pl.BlockSpec(shape, lambda *_: (0,) * len(shape))


def cost():
    return pl.CostEstimate(flops=10**8, bytes_accessed=2**17, transcendentals=0)


def rope_tables(length):
    steps = np.arange(HALF, dtype=np.float32)
    freqs = (1.0 / np.float32(rope_base) ** (steps * np.float32(2.0) / np.float32(HEAD_DIM))).astype(
        np.float32
    )
    angles = np.arange(length, dtype=np.float32)[None, :] * freqs[:, None]
    return np.cos(angles).astype(np.float32), np.sin(angles).astype(np.float32)


def rotated(rows, cos, sin, scale, sign):
    parts = []
    for start in range(0, rows.shape[0], HEAD_DIM):
        one = rows[start : start + HALF]
        two = rows[start + HALF : start + HEAD_DIM]
        parts.append((one * cos - sign * (two * sin)) * scale)
        parts.append((two * cos + sign * (one * sin)) * scale)
    return jnp.concatenate(parts, 0)


def column(vector):
    return jnp.broadcast_to(vector[None], (8, vector.shape[0])).T[:, :1]


def first_kernel(sc, x_ref, gain_ref, wq_ref, wk_ref, wv_ref, cos_ref, sin_ref, n_ref, q_ref, k_ref, v_ref):
    x = x_ref[...].astype(F32)
    scale = lax.rsqrt(jnp.mean(x * x, axis=0, keepdims=True) + epsilon)
    normed = (x * scale * column(gain_ref[...])).astype(BF16)
    n_ref[...] = normed
    cos = cos_ref[...]
    sin = sin_ref[...]
    key = mm(wk_ref[...], normed, 1, 0)
    k_ref[...] = rotated(key, cos, sin, 1.0, 1.0).astype(BF16)
    v_ref[...] = mm(wv_ref[...], normed, 1, 0).astype(BF16)
    query = mm(wq_ref[...].T, normed, 1, 0)
    q_ref[...] = rotated(query, cos, sin, HEAD_DIM**-0.5 * log2e, 1.0).astype(BF16)


def first(sc, x, gain, wq, wk, wv, cos, sin):
    rows = x.shape[1]
    return pl.pallas_call(
        first_kernel,
        grid_spec=pltpu.PrefetchScalarGridSpec(
            num_scalar_prefetch=1,
            grid=(1,),
            in_specs=[
                whole(x.shape),
                whole(gain.shape),
                whole(wq.shape),
                whole(wk.shape),
                whole(wv.shape),
                pl.BlockSpec((HALF, rows), lambda i, sc: (0, sc[0])),
                pl.BlockSpec((HALF, rows), lambda i, sc: (0, sc[0])),
            ],
            out_specs=[whole((D, rows))] * 2 + [whole((KVD, rows))] * 2,
        ),
        out_shape=[
            jax.ShapeDtypeStruct((D, rows), BF16),
            jax.ShapeDtypeStruct((D, rows), BF16),
            jax.ShapeDtypeStruct((KVD, rows), BF16),
            jax.ShapeDtypeStruct((KVD, rows), BF16),
        ],
        compiler_params=params(56),
        cost_estimate=cost(),
        name="first",
    )(sc, x, gain, wq, wk, wv, cos, sin)


def block_facts(sc, rank, which, rows):
    mine = sc[0]
    block = mine - 2 * rank if which == 0 else (mine ^ 1) - 2 * rank
    length = sc[1]
    start = block * rows
    active = (block >= 0) & (block <= mine) & (start < length)
    partial = (block == mine) | (start + rows > length)
    pos = mine * rows + lax.broadcasted_iota(jnp.int32, (1, rows), 1)
    bound = jnp.minimum(pos, length - 1) - start
    return active, partial, bound


def masked_scores(scores, bound):
    rows = lax.broadcasted_iota(jnp.int32, scores.shape, 0)
    return jnp.where(rows <= bound, scores, neg_big)


def forward_block(hidden_keys, bound, kv_ref, q_ref, m_ref, l_ref, acc_ref):
    rows = q_ref.shape[1]
    keys = kv_ref[:KVD, :].T
    ones = jnp.ones((8, rows), BF16)

    def score(head):
        kv = head // REP
        scores = mm(
            keys[:, kv * HEAD_DIM : (kv + 1) * HEAD_DIM],
            q_ref[head * HEAD_DIM : (head + 1) * HEAD_DIM, :],
            1,
            0,
        )
        if hidden_keys:
            scores = masked_scores(scores, bound)
        return scores, jnp.max(scores, axis=0, keepdims=True)

    def weigh(head, scores, top):
        kv = head // REP
        old = m_ref[head : head + 1, :]
        new = jnp.maximum(old, top)
        weights = jnp.exp2(scores - new).astype(BF16)
        values = jnp.concatenate(
            [kv_ref[KVD + kv * HEAD_DIM : KVD + (kv + 1) * HEAD_DIM, :], ones], 0
        )
        return new, jnp.exp2(old - new), mm(values, weights, 1, 0)

    def store(head, new, fade, out):
        rows_of = slice(head * HEAD_DIM, (head + 1) * HEAD_DIM)
        m_ref[head : head + 1, :] = new
        l_ref[head : head + 1, :] = l_ref[head : head + 1, :] * fade + out[HEAD_DIM : HEAD_DIM + 1]
        acc_ref[rows_of, :] = acc_ref[rows_of, :] * fade + out[:HEAD_DIM]

    ahead = score(0)
    held = None
    for head in range(HEADS):
        current = ahead
        if head + 1 < HEADS:
            ahead = score(head + 1)
        result = weigh(head, *current)
        if held is not None:
            store(*held)
        held = (head,) + result
    store(*held)


def forward_kernel(sc, q_ref, ak_ref, av_ref, bk_ref, bv_ref, *refs, rank, fresh):
    rows = q_ref.shape[1]
    which = pl.program_id(0)
    m_ref, l_ref, acc_ref, kv_ref = refs[-4:]

    @pl.when(which == 0)
    def _():
        if fresh:
            m_ref[...] = jnp.full_like(m_ref, neg_big)
            l_ref[...] = jnp.zeros_like(l_ref)
            acc_ref[...] = jnp.zeros_like(acc_ref)
        else:
            m_ref[...] = refs[0][...]
            l_ref[...] = refs[1][...]
            acc_ref[...] = refs[2][...]
        kv_ref[:KVD, :] = ak_ref[...]
        kv_ref[KVD:, :] = av_ref[...]

    @pl.when(which == 1)
    def _():
        kv_ref[:KVD, :] = bk_ref[...]
        kv_ref[KVD:, :] = bv_ref[...]

    first_facts = block_facts(sc, rank, 0, rows)
    second_facts = block_facts(sc, rank, 1, rows)
    active, partial, bound = [
        jnp.where(which == 0, one, two) for one, two in zip(first_facts, second_facts)
    ]

    @pl.when(active & jnp.logical_not(partial))
    def _():
        forward_block(False, bound, kv_ref, q_ref, m_ref, l_ref, acc_ref)

    @pl.when(active & partial)
    def _():
        forward_block(True, bound, kv_ref, q_ref, m_ref, l_ref, acc_ref)


def forward(sc, q, a, b, state, rank):
    rows = q.shape[1]
    state = () if state is None else tuple(state)
    return pl.pallas_call(
        functools.partial(forward_kernel, rank=rank, fresh=not state),
        grid_spec=pltpu.PrefetchScalarGridSpec(
            num_scalar_prefetch=1,
            grid=(2,),
            in_specs=[whole(part.shape) for part in (q, *a, *b, *state)],
            out_specs=[whole((16, rows)), whole((16, rows)), whole((D, rows))],
            scratch_shapes=[pltpu.VMEM((2 * KVD, rows), BF16)],
        ),
        out_shape=[
            jax.ShapeDtypeStruct((16, rows), F32),
            jax.ShapeDtypeStruct((16, rows), F32),
            jax.ShapeDtypeStruct((D, rows), F32),
        ],
        compiler_params=params(20),
        cost_estimate=cost(),
        name=f"forward_{rank}",
    )(sc, q, *a, *b, *state)


def backward_block(hidden_keys, bound, k_ref, v_ref, q_ref, do_ref, lse_ref, delta_ref, dq_ref, out_ref):
    keys = k_ref[...].T
    values = v_ref[...].T

    def start(head):
        kv = head // REP
        lanes = slice(kv * HEAD_DIM, (kv + 1) * HEAD_DIM)
        rows_of = slice(head * HEAD_DIM, (head + 1) * HEAD_DIM)
        scores = mm(keys[:, lanes], q_ref[rows_of, :], 1, 0)
        if hidden_keys:
            scores = masked_scores(scores, bound)
        return scores, mm(values[:, lanes], do_ref[rows_of, :], 1, 0)

    ahead = start(0)
    for head in range(HEADS):
        kv = head // REP
        rows_of = slice(head * HEAD_DIM, (head + 1) * HEAD_DIM)
        scores, d_probs = ahead
        if head + 1 < HEADS:
            ahead = start(head + 1)
        probs = jnp.exp2(scores - lse_ref[head : head + 1, :])
        d_scores = (probs * (d_probs - delta_ref[head : head + 1, :])).astype(BF16)
        value_term = mm(probs.astype(BF16), do_ref[rows_of, :], 1, 1)
        key_term = mm(d_scores, q_ref[rows_of, :], 1, 1)
        first_rep = head % REP == 0
        d_value = value_term if first_rep else d_value + value_term
        d_key = key_term if first_rep else d_key + key_term
        dq_ref[rows_of, :] = dq_ref[rows_of, :] + mm(
            k_ref[kv * HEAD_DIM : (kv + 1) * HEAD_DIM, :], d_scores, 1, 0
        )
        if head % REP == REP - 1:
            out_ref[kv] = jnp.concatenate([d_key, d_value], 1).astype(BF16)


def backward_kernel(sc, q_ref, do_ref, lse_ref, delta_ref, k_ref, v_ref, *refs, rank, which):
    dq_ref, out_ref = refs[-2:]
    dq_ref[...] = refs[0][...] if len(refs) == 3 else jnp.zeros_like(dq_ref)
    active, partial, bound = block_facts(sc, rank, which, q_ref.shape[1])
    rest = (k_ref, v_ref, q_ref, do_ref, lse_ref, delta_ref, dq_ref, out_ref)

    @pl.when(active & jnp.logical_not(partial))
    def _():
        backward_block(False, bound, *rest)

    @pl.when(active & partial)
    def _():
        backward_block(True, bound, *rest)

    @pl.when(jnp.logical_not(active))
    def _():
        out_ref[...] = jnp.zeros_like(out_ref)


def backward(sc, q, d_out, lse, delta, kv, dq, rank, which):
    rows = q.shape[1]
    args = (q, d_out, lse, delta, *kv) + (() if dq is None else (dq,))
    grads = (KV_HEADS, rows, 2 * HEAD_DIM)
    return pl.pallas_call(
        functools.partial(backward_kernel, rank=rank, which=which),
        grid_spec=pltpu.PrefetchScalarGridSpec(
            num_scalar_prefetch=1,
            grid=(1,),
            in_specs=[whole(part.shape) for part in args],
            out_specs=[whole((D, rows)), whole(grads)],
        ),
        out_shape=[
            jax.ShapeDtypeStruct((D, rows), F32),
            jax.ShapeDtypeStruct(grads, BF16),
        ],
        compiler_params=params(20),
        cost_estimate=cost(),
        name=f"backward_{rank}_{which}",
    )(sc, *args)


def place(sc, orders, spot, pair):
    return jnp.where((sc[0] & 1) == 0, orders[0][pair], orders[1][pair]) ^ spot


def store_pieces(sc, orders, spot, keep_ref, send_ref, piece_of):
    low = (sc[0] & 1) == 0
    for pair in range(keep_ref.shape[0]):
        even = piece_of(2 * pair)
        odd = piece_of(2 * pair + 1)
        keep_ref[place(sc, orders, spot[0], pair)] = jnp.where(low, even, odd)
        send_ref[place(sc, orders[::-1], spot[1], pair)] = jnp.where(low, odd, even)


def load_pair(sc, orders, spot, keep_ref, got_ref, pair):
    low = (sc[0] & 1) == 0
    one = keep_ref[place(sc, orders, spot[0], pair)]
    two = got_ref[place(sc, orders[::-1], spot[1], pair)]
    return jnp.where(low, one, two), jnp.where(low, two, one)


def middle_kernel(
    sc,
    acc_ref,
    m_ref,
    l_ref,
    x_ref,
    cot_ref,
    gain_ref,
    wo_ref,
    wg_ref,
    wu_ref,
    wd_ref,
    y_ref,
    do_ref,
    lse_ref,
    delta_ref,
    dh_ref,
    keep_ref,
    send_ref,
    mixed_ref,
    stack_ref,
    hid_ref,
    dg_ref,
    du_ref,
    *,
    orders,
):
    for head in range(HEADS):
        rows_of = slice(head * HEAD_DIM, (head + 1) * HEAD_DIM)
        mixed_ref[rows_of, :] = acc_ref[rows_of, :] * (1.0 / l_ref[head : head + 1, :])
    lse_ref[:HEADS, :] = m_ref[:HEADS, :] + jnp.log2(l_ref[:HEADS, :])
    gain = column(gain_ref[...])
    cot_t = cot_ref[...]
    cot = cot_t.T
    mixed_low = mixed_ref[...].astype(BF16)
    h = x_ref[...].astype(F32) + mm(wo_ref[...].T, mixed_low, 1, 0)
    scale = lax.rsqrt(jnp.mean(h * h, axis=0, keepdims=True) + epsilon)
    normed_t = (h * scale * gain).astype(BF16)
    normed = normed_t.T

    def start(chunk):
        cols = slice(chunk * CHUNK, (chunk + 1) * CHUNK)
        return (
            mm(normed, wg_ref[:, cols], 1, 0),
            mm(normed, wu_ref[:, cols], 1, 0),
            mm(cot, wd_ref[:, cols], 1, 0),
        )

    chunks = FF // CHUNK
    ahead = start(0)
    for chunk in range(chunks):
        gate, up, d_hidden = ahead
        if chunk + 1 < chunks:
            ahead = start(chunk + 1)
        cols = slice(chunk * CHUNK, (chunk + 1) * CHUNK)
        sig = 1.0 / (1.0 + jnp.exp2(gate * -log2e))
        silu = gate * sig
        hidden = (silu * up).astype(BF16)
        d_gate = (d_hidden * up * (sig * (1.0 + gate * (1.0 - sig)))).astype(BF16)
        d_up = (d_hidden * silu).astype(BF16)
        hid_ref[:, cols] = hidden
        dg_ref[:, cols] = d_gate
        du_ref[:, cols] = d_up
        stack_ref[:D, cols] = mm(normed_t, d_gate, 1, 0).astype(BF16)
        stack_ref[D : 2 * D, cols] = mm(normed_t, d_up, 1, 0).astype(BF16)
        stack_ref[2 * D : 3 * D, cols] = mm(cot_t, hidden, 1, 0).astype(BF16)
    y_ref[...] = (h + mm(wd_ref[...], hid_ref[...], 1, 1)).astype(BF16)
    dn = mm(wg_ref[...], dg_ref[...], 1, 1) + mm(wu_ref[...], du_ref[...], 1, 1)
    unit = h * scale
    gain_sum = jnp.sum(dn * unit, axis=1, keepdims=True)
    scaled = dn * gain
    dh = cot_t.astype(F32) + scale * (
        scaled - unit * jnp.mean(scaled * unit, axis=0, keepdims=True)
    )
    dh_ref[...] = dh
    dh_low = dh.astype(BF16)
    mixed = mixed_ref[...]
    d_mixed = mm(wo_ref[...], dh_low, 1, 0).astype(BF16)
    do_ref[...] = d_mixed
    for head in range(HEADS):
        rows_of = slice(head * HEAD_DIM, (head + 1) * HEAD_DIM)
        delta_ref[head : head + 1, :] = jnp.sum(
            d_mixed[rows_of].astype(F32) * mixed[rows_of], axis=0, keepdims=True
        )
    d_wo = mm(mixed_low, dh_low, 1, 1).astype(BF16)
    gain_row = jnp.broadcast_to(gain_sum, (D, 128)).T[:16].astype(BF16)
    quarter = D // 4
    base = 3 * D
    for k in range(4):
        cols = slice(k * PART, (k + 1) * PART)
        part = d_wo[k * quarter : (k + 1) * quarter]
        stack_ref[base : base + quarter, cols] = part[:, :PART]
        stack_ref[base + quarter : base + 2 * quarter, cols] = jnp.concatenate(
            [part[:, PART:], jnp.zeros((quarter, 2 * PART - D), BF16)], 1
        )
        stack_ref[base + 2 * quarter :, cols] = jnp.zeros((STACK - base - 2 * quarter, PART), BF16)
    stack_ref[base + 2 * quarter : base + 2 * quarter + 16, :D] = gain_row
    rows = keep_ref.shape[1]
    store_pieces(
        sc,
        orders,
        (sc[2], sc[3]),
        keep_ref,
        send_ref,
        lambda p: stack_ref[p * rows : (p + 1) * rows, :],
    )


def middle(sc, acc, m, l, x, cot, gain, wo, wg, wu, wd, orders):
    rows = x.shape[1]
    pairs = len(orders[0])
    half = (pairs, STACK // (2 * pairs), FF)
    args = (acc, m, l, x, cot, gain, wo, wg, wu, wd)
    outs = [
        ((D, rows), BF16),
        ((D, rows), BF16),
        ((16, rows), F32),
        ((16, rows), F32),
        ((D, rows), F32),
        (half, BF16),
        (half, BF16),
    ]
    return pl.pallas_call(
        functools.partial(middle_kernel, orders=orders),
        grid_spec=pltpu.PrefetchScalarGridSpec(
            num_scalar_prefetch=1,
            grid=(1,),
            in_specs=[whole(part.shape) for part in args],
            out_specs=[whole(shape) for shape, _ in outs],
            scratch_shapes=[
                pltpu.VMEM((D, rows), F32),
                pltpu.VMEM((STACK, FF), BF16),
                pltpu.VMEM((rows, FF), BF16),
                pltpu.VMEM((rows, FF), BF16),
                pltpu.VMEM((rows, FF), BF16),
            ],
        ),
        out_shape=[jax.ShapeDtypeStruct(*out) for out in outs],
        compiler_params=params(48),
        cost_estimate=cost(),
        name="middle",
    )(sc, *args)


def last_kernel(
    sc,
    dq_ref,
    dkv_ref,
    n_ref,
    x_ref,
    dh_ref,
    gain_ref,
    wq_ref,
    wk_ref,
    wv_ref,
    cos_ref,
    sin_ref,
    dx_ref,
    keep_ref,
    send_ref,
    *,
    orders,
):
    cos = cos_ref[...]
    sin = sin_ref[...]
    rows = x_ref.shape[1]
    d_query = rotated(dq_ref[...], cos, sin, HEAD_DIM**-0.5, -1.0).astype(BF16)
    turned = [dkv_ref[kv].astype(F32).T for kv in range(KV_HEADS)]
    d_key = rotated(
        jnp.concatenate([part[:HEAD_DIM] for part in turned], 0), cos, sin, ln2, -1.0
    ).astype(BF16)
    d_value = jnp.concatenate([part[HEAD_DIM:] for part in turned], 0).astype(BF16)
    dn = (
        mm(wq_ref[...], d_query, 1, 0)
        + mm(wk_ref[...], d_key, 0, 0)
        + mm(wv_ref[...], d_value, 0, 0)
    )
    x = x_ref[...].astype(F32)
    scale = lax.rsqrt(jnp.mean(x * x, axis=0, keepdims=True) + epsilon)
    unit = x * scale
    scaled = dn * column(gain_ref[...])
    dx_ref[...] = (
        dh_ref[...] + scale * (scaled - unit * jnp.mean(scaled * unit, axis=0, keepdims=True))
    ).astype(BF16)
    pad = 64
    joined = jnp.concatenate([d_query, jnp.zeros((pad, rows), BF16), d_key, d_value], 0)
    grad = mm(n_ref[...], joined, 1, 1)
    gain_sum = jnp.sum(dn * unit, axis=1, keepdims=True)
    spot = D // 128
    lane = lax.broadcasted_iota(jnp.int32, (D, 128), 1)
    mixed = jnp.where(
        lane < D - spot * 128, grad[:, spot * 128 : (spot + 1) * 128], gain_sum
    )
    tiles = [
        (mixed if i == spot else grad[:, i * 128 : (i + 1) * 128]).astype(BF16) for i in range(8)
    ]
    piece_rows = keep_ref.shape[1]

    def piece_of(piece):
        top = (piece // 8) * piece_rows
        count = max(min(piece_rows, D - top), 0)
        empty = jnp.zeros((piece_rows - count, 128), BF16)
        if count == 0:
            return empty
        part = tiles[piece % 8][top : top + count]
        return jnp.concatenate([part, empty], 0) if count < piece_rows else part

    store_pieces(sc, orders, (sc[4], sc[5]), keep_ref, send_ref, piece_of)


def last(sc, dq, dkv, n, x, dh, gain, wq, wk, wv, cos, sin, orders):
    pieces = 2 * len(orders[0])
    rows = x.shape[1]
    piece_rows = -(-D // max(pieces // 8, 1))
    half = (pieces // 2, -(-piece_rows // 16) * 16, 128)
    table = pl.BlockSpec((HALF, rows), lambda i, sc: (0, sc[0]))
    return pl.pallas_call(
        functools.partial(last_kernel, orders=orders),
        grid_spec=pltpu.PrefetchScalarGridSpec(
            num_scalar_prefetch=1,
            grid=(1,),
            in_specs=[whole(part.shape) for part in (dq, dkv, n, x, dh, gain, wq, wk, wv)]
            + [table, table],
            out_specs=[whole((D, rows)), whole(half), whole(half)],
        ),
        out_shape=[
            jax.ShapeDtypeStruct((D, rows), BF16),
            jax.ShapeDtypeStruct(half, BF16),
            jax.ShapeDtypeStruct(half, BF16),
        ],
        compiler_params=params(24),
        cost_estimate=cost(),
        name="last",
    )(sc, dq, dkv, n, x, dh, gain, wq, wk, wv, cos, sin)


def unpack_big_kernel(sc, keep_ref, got_ref, gate_ref, up_ref, down_ref, wo_ref, gain_ref, *, orders):
    step = pl.program_id(0)
    quarter = D // 4
    refs = (gate_ref, up_ref, down_ref)
    pairs, rows, _ = keep_ref.shape
    rest = []
    for pair in range(pairs):
        for side, part in enumerate(load_pair(sc, orders, (sc[2], sc[3]), keep_ref, got_ref, pair)):
            part = part.astype(F32)
            top = (2 * pair + side) * rows
            if top < 3 * D:
                refs[top // D][top % D : top % D + rows, :] = part
            else:
                rest.append(part)
    rest = jnp.concatenate(rest, 0)
    wo_ref[:, :PART] = rest[:quarter]
    wo_ref[:, PART:] = rest[quarter : 2 * quarter, : D - PART]
    row = rest[2 * quarter : 2 * quarter + 1]

    @pl.when(step == 0)
    def _():
        gain_ref[:, :PART] = row

    @pl.when(step == 1)
    def _():
        gain_ref[:, PART:] = row[:, : D - PART]


def unpack_big(sc, keep, got, orders):
    shapes = [(D, FF), (D, FF), (D, FF), (D, D), (1, D)]
    cols = pl.BlockSpec((D, PART), lambda i, sc: (0, i))
    part = pl.BlockSpec(keep.shape[:2] + (PART,), lambda i, sc: (0, 0, i))
    return pl.pallas_call(
        functools.partial(unpack_big_kernel, orders=orders),
        grid_spec=pltpu.PrefetchScalarGridSpec(
            num_scalar_prefetch=1,
            grid=(FF // PART,),
            in_specs=[part, part],
            out_specs=[
                cols,
                cols,
                cols,
                pl.BlockSpec((D // 4, D), lambda i, sc: (i, 0)),
                whole((1, D)),
            ],
        ),
        out_shape=[jax.ShapeDtypeStruct(shape, F32) for shape in shapes],
        compiler_params=params(32),
        cost_estimate=cost(),
        name="unpack_big",
    )(sc, keep, got)


def unpack_small_kernel(sc, keep_ref, got_ref, q_ref, k_ref, v_ref, gain_ref, *, orders):
    pairs, rows, _ = keep_ref.shape
    columns = [[] for _ in range(8)]
    for pair in range(pairs):
        for side, part in enumerate(load_pair(sc, orders, (sc[4], sc[5]), keep_ref, got_ref, pair)):
            piece = 2 * pair + side
            count = min(rows, D - (piece // 8) * rows)
            if count > 0:
                columns[piece % 8].append(part[:count].astype(F32))
    full = [jnp.concatenate(parts, 0) if len(parts) > 1 else parts[0] for parts in columns]
    spot = D // 128
    for i in range(spot):
        q_ref[:, i * 128 : (i + 1) * 128] = full[i]
    q_ref[:, spot * 128 :] = full[spot][:, : D - spot * 128]
    gain_ref[...] = full[spot].T[D - spot * 128]
    key_value = jnp.concatenate(full[spot + 1 :], 1).T
    k_ref[...] = key_value[:KVD]
    v_ref[...] = key_value[KVD:]


def unpack_small(sc, keep, got, orders):
    shapes = [(D, D), (KVD, D), (KVD, D), (D,)]
    return pl.pallas_call(
        functools.partial(unpack_small_kernel, orders=orders),
        grid_spec=pltpu.PrefetchScalarGridSpec(
            num_scalar_prefetch=1,
            grid=(1,),
            in_specs=[whole(keep.shape), whole(got.shape)],
            out_specs=[whole(shape) for shape in shapes],
        ),
        out_shape=[jax.ShapeDtypeStruct(shape, F32) for shape in shapes],
        compiler_params=params(16),
        cost_estimate=cost(),
        name="unpack_small",
    )(sc, keep, got)


def plus(*parts):
    total = parts[0].astype(F32)
    for part in parts[1:]:
        total = total + part.astype(F32)
    return total.astype(BF16)


def swap(values, step):
    grp_size, seq_size = lax.axis_size("grp"), lax.axis_size("seq")
    moves = [(i, i ^ step[i & 1]) for i in range(grp_size * seq_size)]
    spot = [(i % seq_size) * grp_size + i // seq_size for i in range(grp_size * seq_size)]
    return lax.ppermute(values, ("seq", "grp"), [(spot[i], spot[j]) for i, j in moves])


def halved(values, step, gate=None):
    half = values.shape[0] // 2
    return plus(values[:half], after(swap(values[half:], step), gate))


def doubled(values, step, gate=None):
    return jnp.concatenate([values, after(swap(values, step), gate)], 0)


def spread_bits(value, places):
    count = len(places)
    total = 0
    for t, bit in enumerate(places):
        total = total | (((value >> bit) & 1) << (count - 1 - t))
    return total


def after(value, other):
    return value if other is None else lax.optimization_barrier((value, other))[0]


def build(seq_size, grp_size):
    count = seq_size * grp_size
    chips = seq_size // 2
    core = (1, 1)
    seq_bits = seq_size.bit_length() - 1
    chip_bits = list(range(1, seq_bits))
    grp_bits = list(range(seq_bits, count.bit_length() - 1))
    routes = [grp_bits + chip_bits, grp_bits[::-1] + chip_bits[::-1]]
    big_steps = [(1 << one, 1 << two) for one, two in zip(*routes)]
    grp_steps = big_steps[: len(grp_bits)]
    chip_steps = big_steps[len(grp_bits) :]
    big_places = [[bit - 1 for bit in route] for route in routes]
    small_places = [[bit - seq_bits for bit in route[: len(grp_bits)]] for route in routes]
    big_orders = [[spread_bits(j, spots) for j in range(count // 2)] for spots in big_places]
    small_orders = [[spread_bits(j, spots) for j in range(grp_size)] for spots in small_places]

    def shards(
        inputs,
        lengths,
        attn_gain,
        w_query,
        w_key,
        w_value,
        w_out,
        ffn_gain,
        w_gate,
        w_up,
        w_down,
        cotangent,
    ):
        rows = inputs.shape[1]
        mine = lax.axis_index("seq")
        group = lax.axis_index("grp")
        number = group * chips + lax.shift_right_logical(mine, 1)
        low = (mine & 1) == 0
        scalars = [mine, lengths[0]]
        for value, (one, two) in ((number, big_places), (group, small_places)):
            first_spot = spread_bits(value, one)
            second_spot = spread_bits(value, two)
            scalars.append(jnp.where(low, first_spot, second_spot))
            scalars.append(jnp.where(low, second_spot, first_spot))
        sc = jnp.stack(scalars).astype(jnp.int32)
        cos_np, sin_np = rope_tables(rows * seq_size)
        cos = jnp.asarray(cos_np)
        sin = jnp.asarray(sin_np)
        x = inputs[0].T
        cot = cotangent[0].T
        wk = w_key.T
        wv = w_value.T
        wd = w_down.T

        up = [(i, i + 2) for i in range(seq_size - 2)]
        down = [(i + 2, i) for i in range(seq_size - 2)]
        normed, query, *block = first(sc, x, attn_gain, w_query, wk, wv, cos, sin)
        pairs = []
        state = None
        for rank in range(chips):
            gate = None if state is None else state[0]
            mate = [swap(after(part, gate), core) for part in block]
            pairs.append((block, mate))
            if rank + 1 < chips:
                block = [lax.ppermute(part, "seq", up) for part in block]
            state = forward(sc, query, *pairs[-1], state, rank)
        m, l, acc = state
        outputs, d_mixed, lse, delta, d_resid, big, send = middle(
            sc, acc, m, l, x, cot, ffn_gain, w_out, w_gate, w_up, wd, big_orders
        )
        stages = [lambda part, gate: plus(part, after(swap(send, core), gate))] + [
            functools.partial(halved, step=step) for step in big_steps
        ]
        when = [1, 4, 6] + list(range(7, 2 * seq_size))
        dq = None
        passed = None
        calls = 0
        for rank in reversed(range(chips)):
            grads = [None, None]
            for which in (1, 0):
                if calls in when and stages:
                    big = stages.pop(0)(big, gate=dq)
                    dq = after(dq, big)
                dq, grads[which] = backward(
                    sc, query, d_mixed, lse, delta, pairs[rank][which], dq, rank, which
                )
                calls += 1
            terms = [grads[0], swap(grads[1], core)]
            if passed is not None:
                terms.append(lax.ppermute(passed, "seq", down))
            passed = plus(*terms)
            dq = after(dq, passed)
        for stage in stages:
            big = stage(big, gate=dq)
        dq = after(dq, big)

        d_inputs, small, small_send = last(
            sc, dq, passed, normed, x, d_resid, attn_gain, w_query, wk, wv, cos, sin, small_orders
        )
        marks = [small_send, plus(small, swap(small_send, core))]
        for step in grp_steps:
            marks.append(halved(marks[-1], step))
        small = marks[-1]
        for step in chip_steps:
            small = plus(small, swap(small, step))
        for i, step in enumerate(big_steps[:0:-1]):
            big = doubled(big, step, marks[min(i, len(marks) - 2)])
        big = doubled(after(big, marks[-1]), big_steps[0], small)
        for step in grp_steps[::-1]:
            small = doubled(small, step)
        d_query, d_key, d_value, d_attn_gain = unpack_small(
            sc, small, swap(small, core), small_orders
        )
        d_gate, d_up, d_down, d_out, d_ffn_gain = unpack_big(
            sc, big, swap(big, core), big_orders
        )
        return (
            outputs.T[None],
            d_inputs.T[None],
            d_attn_gain,
            d_query,
            d_key.T,
            d_value.T,
            d_out,
            d_ffn_gain.reshape(D),
            d_gate,
            d_up,
            d_down.T,
        )

    return shards


def solution(mesh):
    tokens = P("grp", "seq", None)
    return jax.shard_map(
        build(mesh.shape["seq"], mesh.shape["grp"]),
        mesh=mesh,
        in_specs=(tokens, P("grp")) + (P(),) * 9 + (tokens,),
        out_specs=(tokens, tokens) + (P(),) * 9,
        check_vma=False,
    )
```

```python
import functools
import math

import jax
import jax.numpy as jnp
import numpy as np
from jax import lax
from jax.experimental import pallas as pl
from jax.experimental.pallas import tpu as pltpu
from jax.sharding import PartitionSpec as P

D = 576
KV_HEADS = 3
HEAD_DIM = 64
REP = 3
HEADS = KV_HEADS * REP
KVD = 192
FF = 1536
CHUNK = 512
STACK = 2048
PART = 384
HALF = HEAD_DIM // 2

epsilon = 1e-05
rope_base = 100000.0
neg_big = -1e30
log2e = math.log2(math.e)
ln2 = math.log(2.0)

F32 = jnp.float32
BF16 = jnp.bfloat16


def mm(left, right, left_dim, right_dim):
    return lax.dot_general(
        left, right, (((left_dim,), (right_dim,)), ((), ())), preferred_element_type=F32
    )


def params(mebibytes):
    return pltpu.CompilerParams(vmem_limit_bytes=mebibytes * 2**20)


def whole(shape):
    return pl.BlockSpec(shape, lambda *_: (0,) * len(shape))


def call(kernel, name, limit, sc, args, outs, scratch=(), aliases=None):
    return pl.pallas_call(
        kernel,
        in_specs=[pl.BlockSpec(memory_space=pltpu.SMEM)]
        + [pl.BlockSpec(memory_space=pltpu.VMEM)] * len(args),
        out_specs=[pl.BlockSpec(memory_space=pltpu.VMEM)] * len(outs),
        out_shape=[jax.ShapeDtypeStruct(*out) for out in outs],
        scratch_shapes=list(scratch),
        input_output_aliases=aliases or {},
        compiler_params=params(limit),
        cost_estimate=cost(),
        name=name,
    )(sc, *args)


def cost():
    return pl.CostEstimate(flops=10**8, bytes_accessed=2**17, transcendentals=0)


def rope_tables(length):
    steps = np.arange(HALF, dtype=np.float32)
    freqs = (1.0 / np.float32(rope_base) ** (steps * np.float32(2.0) / np.float32(HEAD_DIM))).astype(
        np.float32
    )
    angles = np.arange(length, dtype=np.float32)[None, :] * freqs[:, None]
    return np.cos(angles).astype(np.float32), np.sin(angles).astype(np.float32)


def rotated(rows, cos, sin, scale, sign):
    parts = []
    for start in range(0, rows.shape[0], HEAD_DIM):
        one = rows[start : start + HALF]
        two = rows[start + HALF : start + HEAD_DIM]
        parts.append((one * cos - sign * (two * sin)) * scale)
        parts.append((two * cos + sign * (one * sin)) * scale)
    return jnp.concatenate(parts, 0)


def column(vector):
    return jnp.broadcast_to(vector[None], (8, vector.shape[0])).T[:, :1]


def first_kernel(sc, x_ref, gain_ref, wq_ref, wk_ref, wv_ref, cos_ref, sin_ref, n_ref, q_ref, k_ref, v_ref):
    x = x_ref[...].astype(F32)
    scale = lax.rsqrt(jnp.mean(x * x, axis=0, keepdims=True) + epsilon)
    normed = (x * scale * column(gain_ref[...])).astype(BF16)
    n_ref[...] = normed
    cos = cos_ref[...]
    sin = sin_ref[...]
    key = mm(wk_ref[...], normed, 1, 0)
    k_ref[...] = rotated(key, cos, sin, 1.0, 1.0).astype(BF16)
    v_ref[...] = mm(wv_ref[...], normed, 1, 0).astype(BF16)
    query = mm(wq_ref[...].T, normed, 1, 0)
    q_ref[...] = rotated(query, cos, sin, HEAD_DIM**-0.5 * log2e, 1.0).astype(BF16)


def first(sc, x, gain, wq, wk, wv, cos, sin):
    rows = x.shape[1]
    return pl.pallas_call(
        first_kernel,
        grid_spec=pltpu.PrefetchScalarGridSpec(
            num_scalar_prefetch=1,
            grid=(1,),
            in_specs=[
                whole(x.shape),
                whole(gain.shape),
                whole(wq.shape),
                whole(wk.shape),
                whole(wv.shape),
                pl.BlockSpec((HALF, rows), lambda i, sc: (0, sc[0])),
                pl.BlockSpec((HALF, rows), lambda i, sc: (0, sc[0])),
            ],
            out_specs=[whole((D, rows))] * 2 + [whole((KVD, rows))] * 2,
        ),
        out_shape=[
            jax.ShapeDtypeStruct((D, rows), BF16),
            jax.ShapeDtypeStruct((D, rows), BF16),
            jax.ShapeDtypeStruct((KVD, rows), BF16),
            jax.ShapeDtypeStruct((KVD, rows), BF16),
        ],
        compiler_params=params(56),
        cost_estimate=cost(),
        name="first",
    )(sc, x, gain, wq, wk, wv, cos, sin)


def block_facts(sc, rank, which, rows):
    mine = sc[0]
    block = mine - 2 * rank if which == 0 else (mine ^ 1) - 2 * rank
    length = sc[1]
    start = block * rows
    active = (block >= 0) & (block <= mine) & (start < length)
    partial = (block == mine) | (start + rows > length)
    pos = mine * rows + lax.broadcasted_iota(jnp.int32, (1, rows), 1)
    bound = jnp.minimum(pos, length - 1) - start
    return active, partial, bound


def masked_scores(scores, bound):
    rows = lax.broadcasted_iota(jnp.int32, scores.shape, 0)
    return jnp.where(rows <= bound, scores, neg_big)


def forward_block(hidden_keys, bound, k_ref, v_ref, q_ref, m_ref, l_ref, acc_ref):
    rows = q_ref.shape[1]
    keys = k_ref[...].T
    ones = jnp.ones((8, rows), BF16)

    def score(head):
        kv = head // REP
        scores = mm(
            keys[:, kv * HEAD_DIM : (kv + 1) * HEAD_DIM],
            q_ref[head * HEAD_DIM : (head + 1) * HEAD_DIM, :],
            1,
            0,
        )
        if hidden_keys:
            scores = masked_scores(scores, bound)
        return scores, jnp.max(scores, axis=0, keepdims=True)

    def weigh(head, scores, top):
        kv = head // REP
        old = m_ref[head : head + 1, :]
        new = jnp.maximum(old, top)
        weights = jnp.exp2(scores - new).astype(BF16)
        values = jnp.concatenate(
            [v_ref[kv * HEAD_DIM : (kv + 1) * HEAD_DIM, :], ones], 0
        )
        return new, jnp.exp2(old - new), mm(values, weights, 1, 0)

    def store(head, new, fade, out):
        rows_of = slice(head * HEAD_DIM, (head + 1) * HEAD_DIM)
        m_ref[head : head + 1, :] = new
        l_ref[head : head + 1, :] = l_ref[head : head + 1, :] * fade + out[HEAD_DIM : HEAD_DIM + 1]
        acc_ref[rows_of, :] = acc_ref[rows_of, :] * fade + out[:HEAD_DIM]

    ahead = score(0)
    held = None
    for head in range(HEADS):
        current = ahead
        if head + 1 < HEADS:
            ahead = score(head + 1)
        result = weigh(head, *current)
        if held is not None:
            store(*held)
        held = (head,) + result
    store(*held)


def forward_kernel(sc, q_ref, k_ref, v_ref, *refs, rank, which):
    m_ref, l_ref, acc_ref = refs[-3:]
    if len(refs) == 3:
        m_ref[...] = jnp.full_like(m_ref, neg_big)
        l_ref[...] = jnp.zeros_like(l_ref)
        acc_ref[...] = jnp.zeros_like(acc_ref)
    active, partial, bound = block_facts(sc, rank, which, q_ref.shape[1])

    @pl.when(active & jnp.logical_not(partial))
    def _():
        forward_block(False, bound, k_ref, v_ref, q_ref, m_ref, l_ref, acc_ref)

    @pl.when(active & partial)
    def _():
        forward_block(True, bound, k_ref, v_ref, q_ref, m_ref, l_ref, acc_ref)


def forward(sc, q, block, state, rank, which):
    rows = q.shape[1]
    state = () if state is None else tuple(state)
    kernel = functools.partial(forward_kernel, rank=rank, which=which)
    outs = [((16, rows), F32), ((16, rows), F32), ((D, rows), F32)]
    aliases = {4: 0, 5: 1, 6: 2} if state else None
    return call(
        kernel, f"forward_{rank}_{which}", 12, sc, (q, *block, *state), outs, aliases=aliases
    )


def backward_block(hidden_keys, bound, k_ref, v_ref, q_ref, do_ref, lse_ref, delta_ref, dq_ref, out_ref):
    keys = k_ref[...].T
    values = v_ref[...].T

    def start(head):
        kv = head // REP
        lanes = slice(kv * HEAD_DIM, (kv + 1) * HEAD_DIM)
        rows_of = slice(head * HEAD_DIM, (head + 1) * HEAD_DIM)
        scores = mm(keys[:, lanes], q_ref[rows_of, :], 1, 0)
        if hidden_keys:
            scores = masked_scores(scores, bound)
        return scores, mm(values[:, lanes], do_ref[rows_of, :], 1, 0)

    ahead = start(0)
    for head in range(HEADS):
        kv = head // REP
        rows_of = slice(head * HEAD_DIM, (head + 1) * HEAD_DIM)
        scores, d_probs = ahead
        if head + 1 < HEADS:
            ahead = start(head + 1)
        probs = jnp.exp2(scores - lse_ref[head : head + 1, :])
        d_scores = (probs * (d_probs - delta_ref[head : head + 1, :])).astype(BF16)
        value_term = mm(probs.astype(BF16), do_ref[rows_of, :], 1, 1)
        key_term = mm(d_scores, q_ref[rows_of, :], 1, 1)
        first_rep = head % REP == 0
        d_value = value_term if first_rep else d_value + value_term
        d_key = key_term if first_rep else d_key + key_term
        dq_ref[rows_of, :] = dq_ref[rows_of, :] + mm(
            k_ref[kv * HEAD_DIM : (kv + 1) * HEAD_DIM, :], d_scores, 1, 0
        )
        if head % REP == REP - 1:
            out_ref[kv] = jnp.concatenate([d_key, d_value], 1).astype(BF16)


def backward_kernel(sc, q_ref, do_ref, lse_ref, delta_ref, k_ref, v_ref, *refs, rank, which):
    dq_ref, out_ref = refs[-2:]
    if len(refs) == 2:
        dq_ref[...] = jnp.zeros_like(dq_ref)
    active, partial, bound = block_facts(sc, rank, which, q_ref.shape[1])
    rest = (k_ref, v_ref, q_ref, do_ref, lse_ref, delta_ref, dq_ref, out_ref)

    @pl.when(active & jnp.logical_not(partial))
    def _():
        backward_block(False, bound, *rest)

    @pl.when(active & partial)
    def _():
        backward_block(True, bound, *rest)

    @pl.when(jnp.logical_not(active))
    def _():
        out_ref[...] = jnp.zeros_like(out_ref)


def backward(sc, q, d_out, lse, delta, kv, dq, rank, which):
    rows = q.shape[1]
    args = (q, d_out, lse, delta, *kv) + (() if dq is None else (dq,))
    grads = (KV_HEADS, rows, 2 * HEAD_DIM)
    kernel = functools.partial(backward_kernel, rank=rank, which=which)
    outs = [((D, rows), F32), (grads, BF16)]
    aliases = None if dq is None else {len(args): 0}
    return call(kernel, f"backward_{rank}_{which}", 12, sc, args, outs, aliases=aliases)


def place(sc, orders, spot, pair):
    return jnp.where((sc[0] & 1) == 0, orders[0][pair], orders[1][pair]) ^ spot


def store_pieces(sc, orders, spot, keep_ref, send_ref, piece_of):
    low = (sc[0] & 1) == 0
    for pair in range(keep_ref.shape[0]):
        even = piece_of(2 * pair)
        odd = piece_of(2 * pair + 1)
        keep_ref[place(sc, orders, spot[0], pair)] = jnp.where(low, even, odd)
        send_ref[place(sc, orders[::-1], spot[1], pair)] = jnp.where(low, odd, even)


def load_pair(sc, orders, spot, keep_ref, got_ref, pair):
    low = (sc[0] & 1) == 0
    one = keep_ref[place(sc, orders, spot[0], pair)]
    two = got_ref[place(sc, orders[::-1], spot[1], pair)]
    return jnp.where(low, one, two), jnp.where(low, two, one)


def middle_kernel(
    sc,
    acc_ref,
    m_ref,
    l_ref,
    x_ref,
    cot_ref,
    gain_ref,
    wo_ref,
    wg_ref,
    wu_ref,
    wd_ref,
    y_ref,
    do_ref,
    lse_ref,
    delta_ref,
    dh_ref,
    keep_ref,
    send_ref,
    mixed_ref,
    stack_ref,
    hid_ref,
    dg_ref,
    du_ref,
    *,
    orders,
):
    for head in range(HEADS):
        rows_of = slice(head * HEAD_DIM, (head + 1) * HEAD_DIM)
        mixed_ref[rows_of, :] = acc_ref[rows_of, :] * (1.0 / l_ref[head : head + 1, :])
    lse_ref[:HEADS, :] = m_ref[:HEADS, :] + jnp.log2(l_ref[:HEADS, :])
    gain = column(gain_ref[...])
    cot_t = cot_ref[...]
    cot = cot_t.T
    mixed_low = mixed_ref[...].astype(BF16)
    h = x_ref[...].astype(F32) + mm(wo_ref[...].T, mixed_low, 1, 0)
    scale = lax.rsqrt(jnp.mean(h * h, axis=0, keepdims=True) + epsilon)
    normed_t = (h * scale * gain).astype(BF16)
    normed = normed_t.T

    def start(chunk):
        cols = slice(chunk * CHUNK, (chunk + 1) * CHUNK)
        return (
            mm(normed, wg_ref[:, cols], 1, 0),
            mm(normed, wu_ref[:, cols], 1, 0),
            mm(cot, wd_ref[:, cols], 1, 0),
        )

    chunks = FF // CHUNK
    ahead = start(0)
    for chunk in range(chunks):
        gate, up, d_hidden = ahead
        if chunk + 1 < chunks:
            ahead = start(chunk + 1)
        cols = slice(chunk * CHUNK, (chunk + 1) * CHUNK)
        sig = 1.0 / (1.0 + jnp.exp2(gate * -log2e))
        silu = gate * sig
        hidden = (silu * up).astype(BF16)
        d_gate = (d_hidden * up * (sig * (1.0 + gate * (1.0 - sig)))).astype(BF16)
        d_up = (d_hidden * silu).astype(BF16)
        hid_ref[:, cols] = hidden
        dg_ref[:, cols] = d_gate
        du_ref[:, cols] = d_up
        stack_ref[:D, cols] = mm(normed_t, d_gate, 1, 0).astype(BF16)
        stack_ref[D : 2 * D, cols] = mm(normed_t, d_up, 1, 0).astype(BF16)
        stack_ref[2 * D : 3 * D, cols] = mm(cot_t, hidden, 1, 0).astype(BF16)
    y_ref[...] = (h + mm(wd_ref[...], hid_ref[...], 1, 1)).astype(BF16)
    dn = mm(wg_ref[...], dg_ref[...], 1, 1) + mm(wu_ref[...], du_ref[...], 1, 1)
    unit = h * scale
    gain_sum = jnp.sum(dn * unit, axis=1, keepdims=True)
    scaled = dn * gain
    dh = cot_t.astype(F32) + scale * (
        scaled - unit * jnp.mean(scaled * unit, axis=0, keepdims=True)
    )
    dh_ref[...] = dh
    dh_low = dh.astype(BF16)
    mixed = mixed_ref[...]
    d_mixed = mm(wo_ref[...], dh_low, 1, 0).astype(BF16)
    do_ref[...] = d_mixed
    for head in range(HEADS):
        rows_of = slice(head * HEAD_DIM, (head + 1) * HEAD_DIM)
        delta_ref[head : head + 1, :] = jnp.sum(
            d_mixed[rows_of].astype(F32) * mixed[rows_of], axis=0, keepdims=True
        )
    d_wo = mm(mixed_low, dh_low, 1, 1).astype(BF16)
    gain_row = jnp.broadcast_to(gain_sum, (D, 128)).T[:16].astype(BF16)
    quarter = D // 4
    base = 3 * D
    for k in range(4):
        cols = slice(k * PART, (k + 1) * PART)
        part = d_wo[k * quarter : (k + 1) * quarter]
        stack_ref[base : base + quarter, cols] = part[:, :PART]
        stack_ref[base + quarter : base + 2 * quarter, cols] = jnp.concatenate(
            [part[:, PART:], jnp.zeros((quarter, 2 * PART - D), BF16)], 1
        )
        stack_ref[base + 2 * quarter :, cols] = jnp.zeros((STACK - base - 2 * quarter, PART), BF16)
    stack_ref[base + 2 * quarter : base + 2 * quarter + 16, :D] = gain_row
    rows = keep_ref.shape[1]
    store_pieces(
        sc,
        orders,
        (sc[2], sc[3]),
        keep_ref,
        send_ref,
        lambda p: stack_ref[p * rows : (p + 1) * rows, :],
    )


def middle(sc, acc, m, l, x, cot, gain, wo, wg, wu, wd, orders):
    rows = x.shape[1]
    pairs = len(orders[0])
    half = (pairs, STACK // (2 * pairs), FF)
    args = (acc, m, l, x, cot, gain, wo, wg, wu, wd)
    outs = [
        ((D, rows), BF16),
        ((D, rows), BF16),
        ((16, rows), F32),
        ((16, rows), F32),
        ((D, rows), F32),
        (half, BF16),
        (half, BF16),
    ]
    scratch = [
        pltpu.VMEM((D, rows), F32),
        pltpu.VMEM((STACK, FF), BF16),
        pltpu.VMEM((rows, FF), BF16),
        pltpu.VMEM((rows, FF), BF16),
        pltpu.VMEM((rows, FF), BF16),
    ]
    kernel = functools.partial(middle_kernel, orders=orders)
    return call(kernel, "middle", 34, sc, args, outs, scratch)


def last_kernel(
    sc,
    dq_ref,
    dkv_ref,
    n_ref,
    x_ref,
    dh_ref,
    gain_ref,
    wq_ref,
    wk_ref,
    wv_ref,
    cos_ref,
    sin_ref,
    dx_ref,
    keep_ref,
    send_ref,
    *,
    orders,
):
    cos = cos_ref[...]
    sin = sin_ref[...]
    rows = x_ref.shape[1]
    d_query = rotated(dq_ref[...], cos, sin, HEAD_DIM**-0.5, -1.0).astype(BF16)
    turned = [dkv_ref[kv].astype(F32).T for kv in range(KV_HEADS)]
    d_key = rotated(
        jnp.concatenate([part[:HEAD_DIM] for part in turned], 0), cos, sin, ln2, -1.0
    ).astype(BF16)
    d_value = jnp.concatenate([part[HEAD_DIM:] for part in turned], 0).astype(BF16)
    dn = (
        mm(wq_ref[...], d_query, 1, 0)
        + mm(wk_ref[...], d_key, 0, 0)
        + mm(wv_ref[...], d_value, 0, 0)
    )
    x = x_ref[...].astype(F32)
    scale = lax.rsqrt(jnp.mean(x * x, axis=0, keepdims=True) + epsilon)
    unit = x * scale
    scaled = dn * column(gain_ref[...])
    dx_ref[...] = (
        dh_ref[...] + scale * (scaled - unit * jnp.mean(scaled * unit, axis=0, keepdims=True))
    ).astype(BF16)
    pad = 64
    joined = jnp.concatenate([d_query, jnp.zeros((pad, rows), BF16), d_key, d_value], 0)
    grad = mm(n_ref[...], joined, 1, 1)
    gain_sum = jnp.sum(dn * unit, axis=1, keepdims=True)
    spot = D // 128
    lane = lax.broadcasted_iota(jnp.int32, (D, 128), 1)
    mixed = jnp.where(
        lane < D - spot * 128, grad[:, spot * 128 : (spot + 1) * 128], gain_sum
    )
    tiles = [
        (mixed if i == spot else grad[:, i * 128 : (i + 1) * 128]).astype(BF16) for i in range(8)
    ]
    piece_rows = keep_ref.shape[1]

    def piece_of(piece):
        top = (piece // 8) * piece_rows
        count = max(min(piece_rows, D - top), 0)
        empty = jnp.zeros((piece_rows - count, 128), BF16)
        if count == 0:
            return empty
        part = tiles[piece % 8][top : top + count]
        return jnp.concatenate([part, empty], 0) if count < piece_rows else part

    store_pieces(sc, orders, (sc[4], sc[5]), keep_ref, send_ref, piece_of)


def last(sc, dq, dkv, n, x, dh, gain, wq, wk, wv, cos, sin, orders):
    pieces = 2 * len(orders[0])
    rows = x.shape[1]
    piece_rows = -(-D // max(pieces // 8, 1))
    half = (pieces // 2, -(-piece_rows // 16) * 16, 128)
    table = pl.BlockSpec((HALF, rows), lambda i, sc: (0, sc[0]))
    return pl.pallas_call(
        functools.partial(last_kernel, orders=orders),
        grid_spec=pltpu.PrefetchScalarGridSpec(
            num_scalar_prefetch=1,
            grid=(1,),
            in_specs=[whole(part.shape) for part in (dq, dkv, n, x, dh, gain, wq, wk, wv)]
            + [table, table],
            out_specs=[whole((D, rows)), whole(half), whole(half)],
        ),
        out_shape=[
            jax.ShapeDtypeStruct((D, rows), BF16),
            jax.ShapeDtypeStruct(half, BF16),
            jax.ShapeDtypeStruct(half, BF16),
        ],
        compiler_params=params(24),
        cost_estimate=cost(),
        name="last",
    )(sc, dq, dkv, n, x, dh, gain, wq, wk, wv, cos, sin)


def unpack_big_kernel(sc, keep_ref, got_ref, gate_ref, up_ref, down_ref, wo_ref, gain_ref, *, orders):
    step = pl.program_id(0)
    quarter = D // 4
    refs = (gate_ref, up_ref, down_ref)
    pairs, rows, _ = keep_ref.shape
    rest = []
    for pair in range(pairs):
        for side, part in enumerate(load_pair(sc, orders, (sc[2], sc[3]), keep_ref, got_ref, pair)):
            part = part.astype(F32)
            top = (2 * pair + side) * rows
            if top < 3 * D:
                refs[top // D][top % D : top % D + rows, :] = part
            else:
                rest.append(part)
    rest = jnp.concatenate(rest, 0)
    wo_ref[:, :PART] = rest[:quarter]
    wo_ref[:, PART:] = rest[quarter : 2 * quarter, : D - PART]
    row = rest[2 * quarter : 2 * quarter + 1]

    @pl.when(step == 0)
    def _():
        gain_ref[:, :PART] = row

    @pl.when(step == 1)
    def _():
        gain_ref[:, PART:] = row[:, : D - PART]


def unpack_big(sc, keep, got, orders):
    shapes = [(D, FF), (D, FF), (D, FF), (D, D), (1, D)]
    cols = pl.BlockSpec((D, PART), lambda i, sc: (0, i))
    part = pl.BlockSpec(keep.shape[:2] + (PART,), lambda i, sc: (0, 0, i))
    return pl.pallas_call(
        functools.partial(unpack_big_kernel, orders=orders),
        grid_spec=pltpu.PrefetchScalarGridSpec(
            num_scalar_prefetch=1,
            grid=(FF // PART,),
            in_specs=[part, part],
            out_specs=[
                cols,
                cols,
                cols,
                pl.BlockSpec((D // 4, D), lambda i, sc: (i, 0)),
                whole((1, D)),
            ],
        ),
        out_shape=[jax.ShapeDtypeStruct(shape, F32) for shape in shapes],
        compiler_params=params(32),
        cost_estimate=cost(),
        name="unpack_big",
    )(sc, keep, got)


def unpack_small_kernel(sc, keep_ref, got_ref, q_ref, k_ref, v_ref, gain_ref, *, orders):
    pairs, rows, _ = keep_ref.shape
    columns = [[] for _ in range(8)]
    for pair in range(pairs):
        for side, part in enumerate(load_pair(sc, orders, (sc[4], sc[5]), keep_ref, got_ref, pair)):
            piece = 2 * pair + side
            count = min(rows, D - (piece // 8) * rows)
            if count > 0:
                columns[piece % 8].append(part[:count].astype(F32))
    full = [jnp.concatenate(parts, 0) if len(parts) > 1 else parts[0] for parts in columns]
    spot = D // 128
    for i in range(spot):
        q_ref[:, i * 128 : (i + 1) * 128] = full[i]
    q_ref[:, spot * 128 :] = full[spot][:, : D - spot * 128]
    gain_ref[...] = full[spot].T[D - spot * 128]
    key_value = jnp.concatenate(full[spot + 1 :], 1).T
    k_ref[...] = key_value[:KVD]
    v_ref[...] = key_value[KVD:]


def unpack_small(sc, keep, got, orders):
    shapes = [(D, D), (KVD, D), (KVD, D), (D,)]
    kernel = functools.partial(unpack_small_kernel, orders=orders)
    return call(kernel, "unpack_small", 12, sc, (keep, got), [(shape, F32) for shape in shapes])


def plus(*parts):
    total = parts[0].astype(F32)
    for part in parts[1:]:
        total = total + part.astype(F32)
    return total.astype(BF16)


def swap(values, step):
    grp_size, seq_size = lax.axis_size("grp"), lax.axis_size("seq")
    moves = [(i, i ^ step[i & 1]) for i in range(grp_size * seq_size)]
    spot = [(i % seq_size) * grp_size + i // seq_size for i in range(grp_size * seq_size)]
    return lax.ppermute(values, ("seq", "grp"), [(spot[i], spot[j]) for i, j in moves])


def halved(values, step, gate=None):
    half = values.shape[0] // 2
    return plus(values[:half], after(swap(values[half:], step), gate))


def doubled(values, step, gate=None):
    return jnp.concatenate([values, after(swap(values, step), gate)], 0)


def spread_bits(value, places):
    count = len(places)
    total = 0
    for t, bit in enumerate(places):
        total = total | (((value >> bit) & 1) << (count - 1 - t))
    return total


def after(value, other):
    return value if other is None else lax.optimization_barrier((value, other))[0]


def build(seq_size, grp_size):
    count = seq_size * grp_size
    chips = seq_size // 2
    core = (1, 1)
    seq_bits = seq_size.bit_length() - 1
    chip_bits = list(range(1, seq_bits))
    grp_bits = list(range(seq_bits, count.bit_length() - 1))
    routes = [grp_bits + chip_bits, grp_bits[::-1] + chip_bits[::-1]]
    big_steps = [(1 << one, 1 << two) for one, two in zip(*routes)]
    grp_steps = big_steps[: len(grp_bits)]
    chip_steps = big_steps[len(grp_bits) :]
    big_places = [[bit - 1 for bit in route] for route in routes]
    small_places = [[bit - seq_bits for bit in route[: len(grp_bits)]] for route in routes]
    big_orders = [[spread_bits(j, spots) for j in range(count // 2)] for spots in big_places]
    small_orders = [[spread_bits(j, spots) for j in range(grp_size)] for spots in small_places]

    def shards(
        inputs,
        lengths,
        attn_gain,
        w_query,
        w_key,
        w_value,
        w_out,
        ffn_gain,
        w_gate,
        w_up,
        w_down,
        cotangent,
    ):
        rows = inputs.shape[1]
        mine = lax.axis_index("seq")
        group = lax.axis_index("grp")
        number = group * chips + lax.shift_right_logical(mine, 1)
        low = (mine & 1) == 0
        scalars = [mine, lengths[0]]
        for value, (one, two) in ((number, big_places), (group, small_places)):
            first_spot = spread_bits(value, one)
            second_spot = spread_bits(value, two)
            scalars.append(jnp.where(low, first_spot, second_spot))
            scalars.append(jnp.where(low, second_spot, first_spot))
        sc = jnp.stack(scalars).astype(jnp.int32)
        cos_np, sin_np = rope_tables(rows * seq_size)
        cos = jnp.asarray(cos_np)
        sin = jnp.asarray(sin_np)
        x = inputs[0].T
        cot = cotangent[0].T
        wk = w_key.T
        wv = w_value.T
        wd = w_down.T

        up = [(i, i + 2) for i in range(seq_size - 2)]
        down = [(i + 2, i) for i in range(seq_size - 2)]
        normed, query, *block = first(sc, x, attn_gain, w_query, wk, wv, cos, sin)
        pairs = []
        state = None
        for rank in range(chips):
            gate = None if state is None else state[0]
            mate = [swap(after(part, gate), core) for part in block]
            pairs.append((block, mate))
            if rank + 1 < chips:
                block = [lax.ppermute(part, "seq", up) for part in block]
            for which in (0, 1):
                state = forward(sc, query, pairs[-1][which], state, rank, which)
        m, l, acc = state
        outputs, d_mixed, lse, delta, d_resid, big, send = middle(
            sc, acc, m, l, x, cot, ffn_gain, w_out, w_gate, w_up, wd, big_orders
        )
        stages = [lambda part, gate: plus(part, after(swap(send, core), gate))] + [
            functools.partial(halved, step=step) for step in big_steps
        ]
        when = [1, 4, 6] + list(range(7, 2 * seq_size))
        dq = None
        passed = None
        calls = 0
        for rank in reversed(range(chips)):
            grads = [None, None]
            for which in (1, 0):
                if calls in when and stages:
                    big = stages.pop(0)(big, gate=dq)
                    dq = after(dq, big)
                dq, grads[which] = backward(
                    sc, query, d_mixed, lse, delta, pairs[rank][which], dq, rank, which
                )
                calls += 1
            terms = [grads[0], swap(grads[1], core)]
            if passed is not None:
                terms.append(lax.ppermute(passed, "seq", down))
            passed = plus(*terms)
            dq = after(dq, passed)
        for stage in stages:
            big = stage(big, gate=dq)
        dq = after(dq, big)

        d_inputs, small, small_send = last(
            sc, dq, passed, normed, x, d_resid, attn_gain, w_query, wk, wv, cos, sin, small_orders
        )
        marks = [plus(small, swap(small_send, core))]
        for step in grp_steps:
            marks.append(halved(marks[-1], step))
        small = marks[-1]
        for step in chip_steps:
            small = plus(small, swap(small, step))
        for i, step in enumerate(big_steps[:0:-1]):
            big = doubled(big, step, marks[min(i, len(marks) - 1)])
        big = doubled(big, big_steps[0], small)
        d_gate, d_up, d_down, d_out, d_ffn_gain = unpack_big(
            sc, big, swap(big, core), big_orders
        )
        for step in grp_steps[:0:-1]:
            small = doubled(small, step)
        small = doubled(small, grp_steps[0], d_ffn_gain)
        d_query, d_key, d_value, d_attn_gain = unpack_small(
            sc, small, swap(small, core), small_orders
        )
        return (
            outputs.T[None],
            d_inputs.T[None],
            d_attn_gain,
            d_query,
            d_key.T,
            d_value.T,
            d_out,
            d_ffn_gain.reshape(D),
            d_gate,
            d_up,
            d_down.T,
        )

    return shards


def solution(mesh):
    tokens = P("grp", "seq", None)
    return jax.shard_map(
        build(mesh.shape["seq"], mesh.shape["grp"]),
        mesh=mesh,
        in_specs=(tokens, P("grp")) + (P(),) * 9 + (tokens,),
        out_specs=(tokens, tokens) + (P(),) * 9,
        check_vma=False,
    )
```

```python
import functools
import math

import jax
import jax.numpy as jnp
import numpy as np
from jax import lax
from jax.experimental import pallas as pl
from jax.experimental.pallas import tpu as pltpu
from jax.sharding import PartitionSpec as P

D = 576
KV_HEADS = 3
HEAD_DIM = 64
REP = 3
HEADS = KV_HEADS * REP
KVD = 192
FF = 1536
CHUNK = 512
STACK = 2048
PART = 384
HALF = HEAD_DIM // 2

epsilon = 1e-05
rope_base = 100000.0
neg_big = -1e30
log2e = math.log2(math.e)
ln2 = math.log(2.0)

F32 = jnp.float32
BF16 = jnp.bfloat16


def mm(left, right, left_dim, right_dim):
    return lax.dot_general(
        left, right, (((left_dim,), (right_dim,)), ((), ())), preferred_element_type=F32
    )


def params(mebibytes):
    return pltpu.CompilerParams(vmem_limit_bytes=mebibytes * 2**20)


def whole(shape):
    return pl.BlockSpec(shape, lambda *_: (0,) * len(shape))


def call(kernel, name, limit, sc, args, outs, scratch=(), aliases=None):
    return pl.pallas_call(
        kernel,
        in_specs=[pl.BlockSpec(memory_space=pltpu.SMEM)]
        + [pl.BlockSpec(memory_space=pltpu.VMEM)] * len(args),
        out_specs=[pl.BlockSpec(memory_space=pltpu.VMEM)] * len(outs),
        out_shape=[jax.ShapeDtypeStruct(*out) for out in outs],
        scratch_shapes=list(scratch),
        input_output_aliases=aliases or {},
        compiler_params=params(limit),
        cost_estimate=cost(),
        name=name,
    )(sc, *args)


def cost():
    return pl.CostEstimate(flops=10**8, bytes_accessed=2**17, transcendentals=0)


def rope_tables(length):
    steps = np.arange(HALF, dtype=np.float32)
    freqs = (1.0 / np.float32(rope_base) ** (steps * np.float32(2.0) / np.float32(HEAD_DIM))).astype(
        np.float32
    )
    angles = np.arange(length, dtype=np.float32)[None, :] * freqs[:, None]
    return np.cos(angles).astype(np.float32), np.sin(angles).astype(np.float32)


def rotated(rows, cos, sin, scale, sign):
    parts = []
    for start in range(0, rows.shape[0], HEAD_DIM):
        one = rows[start : start + HALF]
        two = rows[start + HALF : start + HEAD_DIM]
        parts.append((one * cos - sign * (two * sin)) * scale)
        parts.append((two * cos + sign * (one * sin)) * scale)
    return jnp.concatenate(parts, 0)


def column(vector):
    return jnp.broadcast_to(vector[None], (8, vector.shape[0])).T[:, :1]


def keys_kernel(sc, x_ref, gain_ref, wk_ref, wv_ref, cos_ref, sin_ref, n_ref, kv_ref):
    x = x_ref[...].astype(F32)
    scale = lax.rsqrt(jnp.mean(x * x, axis=0, keepdims=True) + epsilon)
    normed = (x * scale * column(gain_ref[...])).astype(BF16)
    n_ref[...] = normed
    key = mm(wk_ref[...], normed, 1, 0)
    kv_ref[:KVD, :] = rotated(key, cos_ref[...], sin_ref[...], 1.0, 1.0).astype(BF16)
    kv_ref[KVD:, :] = mm(wv_ref[...], normed, 1, 0).astype(BF16)


def query_kernel(sc, n_ref, wq_ref, cos_ref, sin_ref, q_ref):
    query = mm(wq_ref[...].T, n_ref[...], 1, 0)
    q_ref[...] = rotated(
        query, cos_ref[...], sin_ref[...], HEAD_DIM**-0.5 * log2e, 1.0
    ).astype(BF16)


def with_tables(kernel, name, sc, args, cos, sin, outs):
    rows = args[0].shape[1]
    table = pl.BlockSpec((HALF, rows), lambda i, sc: (0, sc[0]))
    return pl.pallas_call(
        kernel,
        grid_spec=pltpu.PrefetchScalarGridSpec(
            num_scalar_prefetch=1,
            grid=(1,),
            in_specs=[whole(part.shape) for part in args] + [table, table],
            out_specs=[whole(shape) for shape in outs],
        ),
        out_shape=[jax.ShapeDtypeStruct(shape, BF16) for shape in outs],
        compiler_params=params(56),
        cost_estimate=cost(),
        name=name,
    )(sc, *args, cos, sin)


def block_facts(sc, rank, which, rows):
    mine = sc[0]
    block = mine - 2 * rank if which == 0 else (mine ^ 1) - 2 * rank
    length = sc[1]
    start = block * rows
    active = (block >= 0) & (block <= mine) & (start < length)
    partial = (block == mine) | (start + rows > length)
    pos = mine * rows + lax.broadcasted_iota(jnp.int32, (1, rows), 1)
    bound = jnp.minimum(pos, length - 1) - start
    return active, partial, bound


def masked_scores(scores, bound):
    rows = lax.broadcasted_iota(jnp.int32, scores.shape, 0)
    return jnp.where(rows <= bound, scores, neg_big)


def forward_block(hidden_keys, bound, k_ref, v_ref, q_ref, m_ref, l_ref, acc_ref):
    rows = q_ref.shape[1]
    keys = k_ref[...].T
    ones = jnp.ones((8, rows), BF16)

    def score(head):
        kv = head // REP
        scores = mm(
            keys[:, kv * HEAD_DIM : (kv + 1) * HEAD_DIM],
            q_ref[head * HEAD_DIM : (head + 1) * HEAD_DIM, :],
            1,
            0,
        )
        if hidden_keys:
            scores = masked_scores(scores, bound)
        return scores, jnp.max(scores, axis=0, keepdims=True)

    def weigh(head, scores, top):
        kv = head // REP
        old = m_ref[head : head + 1, :]
        new = jnp.maximum(old, top)
        weights = jnp.exp2(scores - new).astype(BF16)
        values = jnp.concatenate(
            [v_ref[kv * HEAD_DIM : (kv + 1) * HEAD_DIM, :], ones], 0
        )
        return new, jnp.exp2(old - new), mm(values, weights, 1, 0)

    def store(head, new, fade, out):
        rows_of = slice(head * HEAD_DIM, (head + 1) * HEAD_DIM)
        m_ref[head : head + 1, :] = new
        l_ref[head : head + 1, :] = l_ref[head : head + 1, :] * fade + out[HEAD_DIM : HEAD_DIM + 1]
        acc_ref[rows_of, :] = acc_ref[rows_of, :] * fade + out[:HEAD_DIM]

    ahead = score(0)
    held = None
    for head in range(HEADS):
        current = ahead
        if head + 1 < HEADS:
            ahead = score(head + 1)
        result = weigh(head, *current)
        if held is not None:
            store(*held)
        held = (head,) + result
    store(*held)


def forward_kernel(sc, q_ref, kv_ref, *refs, rank, which):
    k_ref, v_ref = kv_ref.at[:KVD], kv_ref.at[KVD:]
    m_ref, l_ref, acc_ref = refs[-3:]
    if len(refs) == 3:
        m_ref[...] = jnp.full_like(m_ref, neg_big)
        l_ref[...] = jnp.zeros_like(l_ref)
        acc_ref[...] = jnp.zeros_like(acc_ref)
    active, partial, bound = block_facts(sc, rank, which, q_ref.shape[1])

    @pl.when(active & jnp.logical_not(partial))
    def _():
        forward_block(False, bound, k_ref, v_ref, q_ref, m_ref, l_ref, acc_ref)

    @pl.when(active & partial)
    def _():
        forward_block(True, bound, k_ref, v_ref, q_ref, m_ref, l_ref, acc_ref)


def forward(sc, q, block, state, rank, which):
    rows = q.shape[1]
    state = () if state is None else tuple(state)
    kernel = functools.partial(forward_kernel, rank=rank, which=which)
    outs = [((16, rows), F32), ((16, rows), F32), ((D, rows), F32)]
    aliases = {3: 0, 4: 1, 5: 2} if state else None
    return call(
        kernel, f"forward_{rank}_{which}", 12, sc, (q, block, *state), outs, aliases=aliases
    )


def backward_block(
    hidden_keys, bound, k_ref, v_ref, q_ref, do_ref, lse_ref, delta_ref, dq_ref, out_ref, causal=False
):
    rows = q_ref.shape[1]
    keys = k_ref[...].T
    values = v_ref[...].T
    half = rows // 2
    spans = [(slice(0, half), half), (slice(half, rows), rows)] if causal else [(slice(0, rows), rows)]
    units = [(head, span) for head in range(HEADS) for span in range(len(spans))]

    def start(head, span):
        columns, count = spans[span]
        kv = head // REP
        lanes = slice(kv * HEAD_DIM, (kv + 1) * HEAD_DIM)
        rows_of = slice(head * HEAD_DIM, (head + 1) * HEAD_DIM)
        scores = mm(keys[:count, lanes], q_ref[rows_of, columns], 1, 0)
        if hidden_keys:
            scores = masked_scores(scores, bound[:, columns])
        return scores, mm(values[:count, lanes], do_ref[rows_of, columns], 1, 0)

    ahead = start(*units[0])
    sums = {}
    for i, (head, span) in enumerate(units):
        columns, count = spans[span]
        kv = head // REP
        rows_of = slice(head * HEAD_DIM, (head + 1) * HEAD_DIM)
        scores, d_probs = ahead
        if i + 1 < len(units):
            ahead = start(*units[i + 1])
        probs = jnp.exp2(scores - lse_ref[head : head + 1, columns])
        d_scores = (probs * (d_probs - delta_ref[head : head + 1, columns])).astype(BF16)
        value_term = mm(probs.astype(BF16), do_ref[rows_of, columns], 1, 1)
        key_term = mm(d_scores, q_ref[rows_of, columns], 1, 1)
        if span in sums:
            sums[span] = (sums[span][0] + key_term, sums[span][1] + value_term)
        else:
            sums[span] = (key_term, value_term)
        dq_ref[rows_of, columns] = dq_ref[rows_of, columns] + mm(
            k_ref[kv * HEAD_DIM : (kv + 1) * HEAD_DIM, :count], d_scores, 1, 0
        )
        if head % REP == REP - 1 and span == len(spans) - 1:
            full = jnp.concatenate(sums[span], 1)
            if causal:
                out_ref[kv, :half] = (full[:half] + jnp.concatenate(sums[0], 1)).astype(BF16)
                out_ref[kv, half:] = full[half:].astype(BF16)
            else:
                out_ref[kv] = full.astype(BF16)
            sums = {}


def backward_kernel(sc, q_ref, do_ref, lse_ref, delta_ref, kv_ref, *refs, rank, which):
    k_ref, v_ref = kv_ref.at[:KVD], kv_ref.at[KVD:]
    dq_ref, out_ref = refs[-2:]
    if len(refs) == 2:
        dq_ref[...] = jnp.zeros_like(dq_ref)
    active, partial, bound = block_facts(sc, rank, which, q_ref.shape[1])
    rest = (k_ref, v_ref, q_ref, do_ref, lse_ref, delta_ref, dq_ref, out_ref)

    if rank == 0 and which == 0:

        @pl.when(active)
        def _():
            backward_block(True, bound, *rest, causal=True)

    else:

        @pl.when(active & jnp.logical_not(partial))
        def _():
            backward_block(False, bound, *rest)

        @pl.when(active & partial)
        def _():
            backward_block(True, bound, *rest)

    @pl.when(jnp.logical_not(active))
    def _():
        out_ref[...] = jnp.zeros_like(out_ref)


def backward(sc, q, d_out, lse, delta, kv, dq, rank, which):
    rows = q.shape[1]
    args = (q, d_out, lse, delta, kv) + (() if dq is None else (dq,))
    grads = (KV_HEADS, rows, 2 * HEAD_DIM)
    kernel = functools.partial(backward_kernel, rank=rank, which=which)
    outs = [((D, rows), F32), (grads, BF16)]
    aliases = None if dq is None else {len(args): 0}
    return call(kernel, f"backward_{rank}_{which}", 12, sc, args, outs, aliases=aliases)


def place(sc, orders, spot, pair):
    return jnp.where((sc[0] & 1) == 0, orders[0][pair], orders[1][pair]) ^ spot


def store_pieces(sc, orders, spot, keep_ref, send_ref, piece_of):
    low = (sc[0] & 1) == 0
    for pair in range(keep_ref.shape[0]):
        even = piece_of(2 * pair)
        odd = piece_of(2 * pair + 1)
        keep_ref[place(sc, orders, spot[0], pair)] = jnp.where(low, even, odd)
        send_ref[place(sc, orders[::-1], spot[1], pair)] = jnp.where(low, odd, even)


def load_pair(sc, orders, spot, keep_ref, got_ref, pair):
    low = (sc[0] & 1) == 0

    def load(refs, where):
        if not isinstance(refs, tuple):
            return refs[where]
        half = refs[0].shape[0]
        inside = where & (half - 1)
        return jnp.where(where < half, refs[0][inside], refs[1][inside])

    one = load(keep_ref, place(sc, orders, spot[0], pair))
    two = load(got_ref, place(sc, orders[::-1], spot[1], pair))
    return jnp.where(low, one, two), jnp.where(low, two, one)


def middle_kernel(
    sc,
    acc_ref,
    m_ref,
    l_ref,
    x_ref,
    cot_ref,
    gain_ref,
    wo_ref,
    wg_ref,
    wu_ref,
    wd_ref,
    y_ref,
    do_ref,
    lse_ref,
    delta_ref,
    dh_ref,
    keep_ref,
    send_ref,
    mixed_ref,
    stack_ref,
    hid_ref,
    dg_ref,
    du_ref,
    *,
    orders,
):
    for head in range(HEADS):
        rows_of = slice(head * HEAD_DIM, (head + 1) * HEAD_DIM)
        mixed_ref[rows_of, :] = acc_ref[rows_of, :] * (1.0 / l_ref[head : head + 1, :])
    lse_ref[:HEADS, :] = m_ref[:HEADS, :] + jnp.log2(l_ref[:HEADS, :])
    gain = column(gain_ref[...])
    cot_t = cot_ref[...]
    cot = cot_t.T
    mixed_low = mixed_ref[...].astype(BF16)
    h = x_ref[...].astype(F32) + mm(wo_ref[...].T, mixed_low, 1, 0)
    scale = lax.rsqrt(jnp.mean(h * h, axis=0, keepdims=True) + epsilon)
    normed_t = (h * scale * gain).astype(BF16)
    normed = normed_t.T

    def start(chunk):
        cols = slice(chunk * CHUNK, (chunk + 1) * CHUNK)
        return (
            mm(normed, wg_ref[:, cols], 1, 0),
            mm(normed, wu_ref[:, cols], 1, 0),
            mm(cot, wd_ref[:, cols], 1, 0),
        )

    chunks = FF // CHUNK
    ahead = start(0)
    for chunk in range(chunks):
        gate, up, d_hidden = ahead
        if chunk + 1 < chunks:
            ahead = start(chunk + 1)
        cols = slice(chunk * CHUNK, (chunk + 1) * CHUNK)
        sig = 1.0 / (1.0 + jnp.exp2(gate * -log2e))
        silu = gate * sig
        hidden = (silu * up).astype(BF16)
        d_gate = (d_hidden * up * (sig * (1.0 + gate * (1.0 - sig)))).astype(BF16)
        d_up = (d_hidden * silu).astype(BF16)
        hid_ref[:, cols] = hidden
        dg_ref[:, cols] = d_gate
        du_ref[:, cols] = d_up
        stack_ref[:D, cols] = mm(normed_t, d_gate, 1, 0).astype(BF16)
        stack_ref[D : 2 * D, cols] = mm(normed_t, d_up, 1, 0).astype(BF16)
        stack_ref[2 * D : 3 * D, cols] = mm(cot_t, hidden, 1, 0).astype(BF16)
    y_ref[...] = (h + mm(wd_ref[...], hid_ref[...], 1, 1)).astype(BF16)
    dn = mm(wg_ref[...], dg_ref[...], 1, 1) + mm(wu_ref[...], du_ref[...], 1, 1)
    unit = h * scale
    gain_sum = jnp.sum(dn * unit, axis=1, keepdims=True)
    scaled = dn * gain
    dh = cot_t.astype(F32) + scale * (
        scaled - unit * jnp.mean(scaled * unit, axis=0, keepdims=True)
    )
    dh_ref[...] = dh
    dh_low = dh.astype(BF16)
    mixed = mixed_ref[...]
    d_mixed = mm(wo_ref[...], dh_low, 1, 0).astype(BF16)
    do_ref[...] = d_mixed
    for head in range(HEADS):
        rows_of = slice(head * HEAD_DIM, (head + 1) * HEAD_DIM)
        delta_ref[head : head + 1, :] = jnp.sum(
            d_mixed[rows_of].astype(F32) * mixed[rows_of], axis=0, keepdims=True
        )
    d_wo = mm(mixed_low, dh_low, 1, 1).astype(BF16)
    gain_row = jnp.broadcast_to(gain_sum, (D, 128)).T[:16].astype(BF16)
    quarter = D // 4
    base = 3 * D
    for k in range(4):
        cols = slice(k * PART, (k + 1) * PART)
        part = d_wo[k * quarter : (k + 1) * quarter]
        stack_ref[base : base + quarter, cols] = part[:, :PART]
        stack_ref[base + quarter : base + 2 * quarter, cols] = jnp.concatenate(
            [part[:, PART:], jnp.zeros((quarter, 2 * PART - D), BF16)], 1
        )
        stack_ref[base + 2 * quarter :, cols] = jnp.zeros((STACK - base - 2 * quarter, PART), BF16)
    stack_ref[base + 2 * quarter : base + 2 * quarter + 16, :D] = gain_row
    rows = keep_ref.shape[1]
    store_pieces(
        sc,
        orders,
        (sc[2], sc[3]),
        keep_ref,
        send_ref,
        lambda p: stack_ref[p * rows : (p + 1) * rows, :],
    )


def middle(sc, acc, m, l, x, cot, gain, wo, wg, wu, wd, orders):
    rows = x.shape[1]
    pairs = len(orders[0])
    half = (pairs, STACK // (2 * pairs), FF)
    args = (acc, m, l, x, cot, gain, wo, wg, wu, wd)
    outs = [
        ((D, rows), BF16),
        ((D, rows), BF16),
        ((16, rows), F32),
        ((16, rows), F32),
        ((D, rows), F32),
        (half, BF16),
        (half, BF16),
    ]
    scratch = [
        pltpu.VMEM((D, rows), F32),
        pltpu.VMEM((STACK, FF), BF16),
        pltpu.VMEM((rows, FF), BF16),
        pltpu.VMEM((rows, FF), BF16),
        pltpu.VMEM((rows, FF), BF16),
    ]
    kernel = functools.partial(middle_kernel, orders=orders)
    return call(kernel, "middle", 34, sc, args, outs, scratch)


def last_kernel(
    sc,
    dq_ref,
    dkv_ref,
    n_ref,
    x_ref,
    dh_ref,
    gain_ref,
    wq_ref,
    wk_ref,
    wv_ref,
    cos_ref,
    sin_ref,
    dx_ref,
    keep_ref,
    send_ref,
    *,
    orders,
):
    cos = cos_ref[...]
    sin = sin_ref[...]
    rows = x_ref.shape[1]
    d_query = rotated(dq_ref[...], cos, sin, HEAD_DIM**-0.5, -1.0).astype(BF16)
    turned = [dkv_ref[kv].astype(F32).T for kv in range(KV_HEADS)]
    d_key = rotated(
        jnp.concatenate([part[:HEAD_DIM] for part in turned], 0), cos, sin, ln2, -1.0
    ).astype(BF16)
    d_value = jnp.concatenate([part[HEAD_DIM:] for part in turned], 0).astype(BF16)
    dn = (
        mm(wq_ref[...], d_query, 1, 0)
        + mm(wk_ref[...], d_key, 0, 0)
        + mm(wv_ref[...], d_value, 0, 0)
    )
    x = x_ref[...].astype(F32)
    scale = lax.rsqrt(jnp.mean(x * x, axis=0, keepdims=True) + epsilon)
    unit = x * scale
    scaled = dn * column(gain_ref[...])
    dx_ref[...] = (
        dh_ref[...] + scale * (scaled - unit * jnp.mean(scaled * unit, axis=0, keepdims=True))
    ).astype(BF16)
    pad = 64
    joined = jnp.concatenate([d_query, jnp.zeros((pad, rows), BF16), d_key, d_value], 0)
    grad = mm(n_ref[...], joined, 1, 1)
    gain_sum = jnp.sum(dn * unit, axis=1, keepdims=True)
    spot = D // 128
    lane = lax.broadcasted_iota(jnp.int32, (D, 128), 1)
    mixed = jnp.where(
        lane < D - spot * 128, grad[:, spot * 128 : (spot + 1) * 128], gain_sum
    )
    tiles = [
        (mixed if i == spot else grad[:, i * 128 : (i + 1) * 128]).astype(BF16) for i in range(8)
    ]
    piece_rows = keep_ref.shape[1]

    def piece_of(piece):
        top = (piece // 8) * piece_rows
        count = max(min(piece_rows, D - top), 0)
        empty = jnp.zeros((piece_rows - count, 128), BF16)
        if count == 0:
            return empty
        part = tiles[piece % 8][top : top + count]
        return jnp.concatenate([part, empty], 0) if count < piece_rows else part

    store_pieces(sc, orders, (sc[4], sc[5]), keep_ref, send_ref, piece_of)


def last(sc, dq, dkv, n, x, dh, gain, wq, wk, wv, cos, sin, orders):
    pieces = 2 * len(orders[0])
    rows = x.shape[1]
    piece_rows = -(-D // max(pieces // 8, 1))
    half = (pieces // 2, -(-piece_rows // 16) * 16, 128)
    table = pl.BlockSpec((HALF, rows), lambda i, sc: (0, sc[0]))
    return pl.pallas_call(
        functools.partial(last_kernel, orders=orders),
        grid_spec=pltpu.PrefetchScalarGridSpec(
            num_scalar_prefetch=1,
            grid=(1,),
            in_specs=[whole(part.shape) for part in (dq, dkv, n, x, dh, gain, wq, wk, wv)]
            + [table, table],
            out_specs=[whole((D, rows)), whole(half), whole(half)],
        ),
        out_shape=[
            jax.ShapeDtypeStruct((D, rows), BF16),
            jax.ShapeDtypeStruct(half, BF16),
            jax.ShapeDtypeStruct(half, BF16),
        ],
        compiler_params=params(24),
        cost_estimate=cost(),
        name="last",
    )(sc, dq, dkv, n, x, dh, gain, wq, wk, wv, cos, sin)


def unpack_big_kernel(
    sc, keep_ref, far_ref, got_ref, got_far_ref, gate_ref, up_ref, down_ref, wo_ref, gain_ref, *, orders
):
    step = pl.program_id(0)
    quarter = D // 4
    refs = (gate_ref, up_ref, down_ref)
    pairs, rows = 2 * keep_ref.shape[0], keep_ref.shape[1]
    kept, got = (keep_ref, far_ref), (got_ref, got_far_ref)
    rest = []
    for pair in range(pairs):
        for side, part in enumerate(load_pair(sc, orders, (sc[2], sc[3]), kept, got, pair)):
            part = part.astype(F32)
            top = (2 * pair + side) * rows
            if top < 3 * D:
                refs[top // D][top % D : top % D + rows, :] = part
            else:
                rest.append(part)
    rest = jnp.concatenate(rest, 0)
    wo_ref[:, :PART] = rest[:quarter]
    wo_ref[:, PART:] = rest[quarter : 2 * quarter, : D - PART]
    row = rest[2 * quarter : 2 * quarter + 1]

    @pl.when(step == 0)
    def _():
        gain_ref[:, :PART] = row

    @pl.when(step == 1)
    def _():
        gain_ref[:, PART:] = row[:, : D - PART]


def unpack_big(sc, keep, got, orders):
    shapes = [(D, FF), (D, FF), (D, FF), (D, D), (1, D)]
    cols = pl.BlockSpec((D, PART), lambda i, sc: (0, i))
    part = pl.BlockSpec(keep[0].shape[:2] + (PART,), lambda i, sc: (0, 0, i))
    return pl.pallas_call(
        functools.partial(unpack_big_kernel, orders=orders),
        grid_spec=pltpu.PrefetchScalarGridSpec(
            num_scalar_prefetch=1,
            grid=(FF // PART,),
            in_specs=[part] * 4,
            out_specs=[
                cols,
                cols,
                cols,
                pl.BlockSpec((D // 4, D), lambda i, sc: (i, 0)),
                whole((1, D)),
            ],
        ),
        out_shape=[jax.ShapeDtypeStruct(shape, F32) for shape in shapes],
        compiler_params=params(32),
        cost_estimate=cost(),
        name="unpack_big",
    )(sc, *keep, *got)


def unpack_small_kernel(sc, keep_ref, got_ref, q_ref, k_ref, v_ref, gain_ref, *, orders):
    pairs, rows, _ = keep_ref.shape
    columns = [[] for _ in range(8)]
    for pair in range(pairs):
        for side, part in enumerate(load_pair(sc, orders, (sc[4], sc[5]), keep_ref, got_ref, pair)):
            piece = 2 * pair + side
            count = min(rows, D - (piece // 8) * rows)
            if count > 0:
                columns[piece % 8].append(part[:count].astype(F32))
    full = [jnp.concatenate(parts, 0) if len(parts) > 1 else parts[0] for parts in columns]
    spot = D // 128
    for i in range(spot):
        q_ref[:, i * 128 : (i + 1) * 128] = full[i]
    q_ref[:, spot * 128 :] = full[spot][:, : D - spot * 128]
    gain_ref[...] = full[spot].T[D - spot * 128]
    key_value = jnp.concatenate(full[spot + 1 :], 1).T
    k_ref[...] = key_value[:KVD]
    v_ref[...] = key_value[KVD:]


def unpack_small(sc, keep, got, orders):
    shapes = [(D, D), (KVD, D), (KVD, D), (D,)]
    kernel = functools.partial(unpack_small_kernel, orders=orders)
    return call(kernel, "unpack_small", 12, sc, (keep, got), [(shape, F32) for shape in shapes])


def plus(*parts):
    total = parts[0].astype(F32)
    for part in parts[1:]:
        total = total + part.astype(F32)
    return total.astype(BF16)


def swap(values, step):
    grp_size, seq_size = lax.axis_size("grp"), lax.axis_size("seq")
    moves = [(i, i ^ step[i & 1]) for i in range(grp_size * seq_size)]
    spot = [(i % seq_size) * grp_size + i // seq_size for i in range(grp_size * seq_size)]
    return lax.ppermute(values, ("seq", "grp"), [(spot[i], spot[j]) for i, j in moves])


def halved(values, step, gate=None):
    half = values.shape[0] // 2
    return plus(values[:half], after(swap(values[half:], step), gate))


def doubled(values, step, gate=None):
    return jnp.concatenate([values, after(swap(values, step), gate)], 0)


def spread_bits(value, places):
    count = len(places)
    total = 0
    for t, bit in enumerate(places):
        total = total | (((value >> bit) & 1) << (count - 1 - t))
    return total


def after(value, other):
    return value if other is None else lax.optimization_barrier((value, other))[0]


def build(seq_size, grp_size):
    count = seq_size * grp_size
    chips = seq_size // 2
    core = (1, 1)
    seq_bits = seq_size.bit_length() - 1
    chip_bits = list(range(1, seq_bits))
    grp_bits = list(range(seq_bits, count.bit_length() - 1))
    routes = [grp_bits + chip_bits, grp_bits[::-1] + chip_bits[::-1]]
    big_steps = [(1 << one, 1 << two) for one, two in zip(*routes)]
    grp_moves = [(i, (i * seq_size, i * seq_size)) for i in range(1, grp_size)]
    chip_steps = big_steps[len(grp_bits) :]
    big_places = [[bit - 1 for bit in route] for route in routes]
    big_orders = [[spread_bits(j, spots) for j in range(count // 2)] for spots in big_places]
    small_orders = [list(range(grp_size))] * 2

    def shards(
        inputs,
        lengths,
        attn_gain,
        w_query,
        w_key,
        w_value,
        w_out,
        ffn_gain,
        w_gate,
        w_up,
        w_down,
        cotangent,
    ):
        rows = inputs.shape[1]
        mine = lax.axis_index("seq")
        group = lax.axis_index("grp")
        number = group * chips + lax.shift_right_logical(mine, 1)
        low = (mine & 1) == 0
        one, two = [spread_bits(number, spots) for spots in big_places]
        spots = [jnp.where(low, one, two), jnp.where(low, two, one), group, group]
        sc = jnp.stack([mine, lengths[0]] + spots).astype(jnp.int32)
        cos_np, sin_np = rope_tables(rows * seq_size)
        cos = jnp.asarray(cos_np)
        sin = jnp.asarray(sin_np)
        x = inputs[0].T
        cot = cotangent[0].T
        wk = w_key.T
        wv = w_value.T
        wd = w_down.T

        down = [(i + 2, i) for i in range(seq_size - 2)]
        normed, own = with_tables(
            keys_kernel,
            "keys",
            sc,
            (x, attn_gain, wk, wv),
            cos,
            sin,
            [(D, rows), (2 * KVD, rows)],
        )
        [query] = with_tables(
            query_kernel, "query", sc, (normed, w_query), cos, sin, [(D, rows)]
        )
        up = [(i, i + 2) for i in range(seq_size - 2)]
        pairs = []
        state = None
        block = own
        for rank in range(chips):
            gate = None if state is None else state[0]
            pairs.append((block, swap(after(block, gate), core)))
            if rank + 1 < chips:
                block = lax.ppermute(block, "seq", up)
            for which in (0, 1):
                state = forward(sc, query, pairs[-1][which], state, rank, which)
        m, l, acc = state
        outputs, d_mixed, lse, delta, d_resid, big, send = middle(
            sc, acc, m, l, x, cot, ffn_gain, w_out, w_gate, w_up, wd, big_orders
        )
        stages = [lambda part, gate: plus(part, after(swap(send, core), gate))] + [
            functools.partial(halved, step=step) for step in big_steps
        ]
        when = [1, 4, 6] + list(range(7, 2 * seq_size))
        dq = None
        passed = None
        calls = 0
        for rank in reversed(range(chips)):
            grads = [None, None]
            for which in (1, 0):
                if calls in when and stages:
                    big = stages.pop(0)(big, gate=dq)
                    dq = after(dq, big)
                dq, grads[which] = backward(
                    sc, query, d_mixed, lse, delta, pairs[rank][which], dq, rank, which
                )
                calls += 1
            terms = [grads[0], swap(grads[1], core)]
            if passed is not None:
                terms.append(lax.ppermute(passed, "seq", down))
            passed = plus(*terms)
            dq = after(dq, passed)
        for stage in stages:
            big = stage(big, gate=dq)
        dq = after(dq, big)

        d_inputs, small, small_send = last(
            sc, dq, passed, normed, x, d_resid, attn_gain, w_query, wk, wv, cos, sin, small_orders
        )
        small = plus(small, swap(small_send, core))
        marks = [small]
        small = plus(small[:1], *[swap(small[i : i + 1], step) for i, step in grp_moves])
        marks.append(small)
        for step in chip_steps:
            small = plus(small, swap(small, step))
            marks.append(small)
        for i, step in enumerate(big_steps[:0:-1]):
            big = doubled(big, step, marks[min(i, 2)])
        far = after(swap(big, big_steps[0]), small)
        others = [swap(small, step) for _, step in grp_moves]
        d_gate, d_up, d_down, d_out, d_ffn_gain = unpack_big(
            sc, (big, far), (swap(big, core), swap(far, core)), big_orders
        )
        others = [after(other, d_ffn_gain) for other in others]
        small = jnp.concatenate([small] + others, 0)
        d_query, d_key, d_value, d_attn_gain = unpack_small(
            sc, small, swap(small, core), small_orders
        )
        return (
            outputs.T[None],
            d_inputs.T[None],
            d_attn_gain,
            d_query,
            d_key.T,
            d_value.T,
            d_out,
            d_ffn_gain.reshape(D),
            d_gate,
            d_up,
            d_down.T,
        )

    return shards


def solution(mesh):
    tokens = P("grp", "seq", None)
    return jax.shard_map(
        build(mesh.shape["seq"], mesh.shape["grp"]),
        mesh=mesh,
        in_specs=(tokens, P("grp")) + (P(),) * 9 + (tokens,),
        out_specs=(tokens, tokens) + (P(),) * 9,
        check_vma=False,
    )
```

```python
import functools
import math

import jax
import jax.numpy as jnp
import numpy as np
from jax import lax
from jax.experimental import pallas as pl
from jax.experimental.pallas import tpu as pltpu
from jax.sharding import PartitionSpec as P

D = 576
KV_HEADS = 3
HEAD_DIM = 64
REP = 3
HEADS = KV_HEADS * REP
KVD = 192
FF = 1536
CHUNK = 512
STACK = 2048
PART = 384
HALF = HEAD_DIM // 2

epsilon = 1e-05
rope_base = 100000.0
neg_big = -1e30
log2e = math.log2(math.e)
ln2 = math.log(2.0)

F32 = jnp.float32
BF16 = jnp.bfloat16


def mm(left, right, left_dim, right_dim):
    return lax.dot_general(
        left, right, (((left_dim,), (right_dim,)), ((), ())), preferred_element_type=F32
    )


def params(mebibytes):
    return pltpu.CompilerParams(vmem_limit_bytes=mebibytes * 2**20)


def whole(shape):
    return pl.BlockSpec(shape, lambda *_: (0,) * len(shape))


def call(kernel, name, limit, sc, args, outs, scratch=(), aliases=None):
    return pl.pallas_call(
        kernel,
        in_specs=[pl.BlockSpec(memory_space=pltpu.SMEM)]
        + [pl.BlockSpec(memory_space=pltpu.VMEM)] * len(args),
        out_specs=[pl.BlockSpec(memory_space=pltpu.VMEM)] * len(outs),
        out_shape=[jax.ShapeDtypeStruct(*out) for out in outs],
        scratch_shapes=list(scratch),
        input_output_aliases=aliases or {},
        compiler_params=params(limit),
        cost_estimate=cost(),
        name=name,
    )(sc, *args)


def cost():
    return pl.CostEstimate(flops=10**8, bytes_accessed=2**17, transcendentals=0)


def rope_tables(length):
    steps = np.arange(HALF, dtype=np.float32)
    freqs = (1.0 / np.float32(rope_base) ** (steps * np.float32(2.0) / np.float32(HEAD_DIM))).astype(
        np.float32
    )
    angles = np.arange(length, dtype=np.float32)[None, :] * freqs[:, None]
    return np.cos(angles).astype(np.float32), np.sin(angles).astype(np.float32)


def rotated(rows, cos, sin, scale, sign):
    parts = []
    for start in range(0, rows.shape[0], HEAD_DIM):
        one = rows[start : start + HALF]
        two = rows[start + HALF : start + HEAD_DIM]
        parts.append((one * cos - sign * (two * sin)) * scale)
        parts.append((two * cos + sign * (one * sin)) * scale)
    return jnp.concatenate(parts, 0)


def column(vector):
    return jnp.broadcast_to(vector[None], (8, vector.shape[0])).T[:, :1]


def keys_kernel(sc, x_ref, gain_ref, wk_ref, wv_ref, cos_ref, sin_ref, n_ref, kv_ref):
    x = x_ref[...].astype(F32)
    scale = lax.rsqrt(jnp.mean(x * x, axis=0, keepdims=True) + epsilon)
    normed = (x * scale * column(gain_ref[...])).astype(BF16)
    n_ref[...] = normed
    key = mm(wk_ref[...], normed, 1, 0)
    kv_ref[:KVD, :] = rotated(key, cos_ref[...], sin_ref[...], 1.0, 1.0).astype(BF16)
    kv_ref[KVD:, :] = mm(wv_ref[...], normed, 1, 0).astype(BF16)


def query_kernel(sc, n_ref, wq_ref, cos_ref, sin_ref, q_ref):
    query = mm(wq_ref[...].T, n_ref[...], 1, 0)
    q_ref[...] = rotated(
        query, cos_ref[...], sin_ref[...], HEAD_DIM**-0.5 * log2e, 1.0
    ).astype(BF16)


def with_tables(kernel, name, sc, args, cos, sin, outs):
    rows = args[0].shape[1]
    table = pl.BlockSpec((HALF, rows), lambda i, sc: (0, sc[0]))
    return pl.pallas_call(
        kernel,
        grid_spec=pltpu.PrefetchScalarGridSpec(
            num_scalar_prefetch=1,
            grid=(1,),
            in_specs=[whole(part.shape) for part in args] + [table, table],
            out_specs=[whole(shape) for shape in outs],
        ),
        out_shape=[jax.ShapeDtypeStruct(shape, BF16) for shape in outs],
        compiler_params=params(56),
        cost_estimate=cost(),
        name=name,
    )(sc, *args, cos, sin)


def block_facts(sc, rank, which, rows):
    mine = sc[0]
    block = mine - 2 * rank if which == 0 else (mine ^ 1) - 2 * rank
    length = sc[1]
    start = block * rows
    active = (block >= 0) & (block <= mine) & (start < length)
    partial = (block == mine) | (start + rows > length)
    pos = mine * rows + lax.broadcasted_iota(jnp.int32, (1, rows), 1)
    bound = jnp.minimum(pos, length - 1) - start
    return active, partial, bound


def masked_scores(scores, bound):
    rows = lax.broadcasted_iota(jnp.int32, scores.shape, 0)
    return jnp.where(rows <= bound, scores, neg_big)


def forward_block(hidden_keys, bound, k_ref, v_ref, q_ref, m_ref, l_ref, acc_ref):
    rows = q_ref.shape[1]
    keys = k_ref[...].T
    ones = jnp.ones((8, rows), BF16)

    def score(head):
        kv = head // REP
        scores = mm(
            keys[:, kv * HEAD_DIM : (kv + 1) * HEAD_DIM],
            q_ref[head * HEAD_DIM : (head + 1) * HEAD_DIM, :],
            1,
            0,
        )
        if hidden_keys:
            scores = masked_scores(scores, bound)
        return scores, jnp.max(scores, axis=0, keepdims=True)

    def weigh(head, scores, top):
        kv = head // REP
        old = m_ref[head : head + 1, :]
        new = jnp.maximum(old, top)
        weights = jnp.exp2(scores - new).astype(BF16)
        values = jnp.concatenate(
            [v_ref[kv * HEAD_DIM : (kv + 1) * HEAD_DIM, :], ones], 0
        )
        return new, jnp.exp2(old - new), mm(values, weights, 1, 0)

    def store(head, new, fade, out):
        rows_of = slice(head * HEAD_DIM, (head + 1) * HEAD_DIM)
        m_ref[head : head + 1, :] = new
        l_ref[head : head + 1, :] = l_ref[head : head + 1, :] * fade + out[HEAD_DIM : HEAD_DIM + 1]
        acc_ref[rows_of, :] = acc_ref[rows_of, :] * fade + out[:HEAD_DIM]

    ahead = score(0)
    held = None
    for head in range(HEADS):
        current = ahead
        if head + 1 < HEADS:
            ahead = score(head + 1)
        result = weigh(head, *current)
        if held is not None:
            store(*held)
        held = (head,) + result
    store(*held)


def forward_kernel(sc, q_ref, kv_ref, *refs, rank, which):
    k_ref, v_ref = kv_ref.at[:KVD], kv_ref.at[KVD:]
    m_ref, l_ref, acc_ref = refs[-3:]
    if len(refs) == 3:
        m_ref[...] = jnp.full_like(m_ref, neg_big)
        l_ref[...] = jnp.zeros_like(l_ref)
        acc_ref[...] = jnp.zeros_like(acc_ref)
    active, partial, bound = block_facts(sc, rank, which, q_ref.shape[1])

    @pl.when(active & jnp.logical_not(partial))
    def _():
        forward_block(False, bound, k_ref, v_ref, q_ref, m_ref, l_ref, acc_ref)

    @pl.when(active & partial)
    def _():
        forward_block(True, bound, k_ref, v_ref, q_ref, m_ref, l_ref, acc_ref)


def forward(sc, q, block, state, rank, which):
    rows = q.shape[1]
    state = () if state is None else tuple(state)
    kernel = functools.partial(forward_kernel, rank=rank, which=which)
    outs = [((16, rows), F32), ((16, rows), F32), ((D, rows), F32)]
    aliases = {3: 0, 4: 1, 5: 2} if state else None
    return call(
        kernel, f"forward_{rank}_{which}", 12, sc, (q, block, *state), outs, aliases=aliases
    )


def backward_block(
    hidden_keys, bound, k_ref, v_ref, q_ref, do_ref, lse_ref, delta_ref, dq_ref, out_ref, causal=False
):
    rows = q_ref.shape[1]
    keys = k_ref[...].T
    values = v_ref[...].T
    half = rows // 2
    spans = [(slice(0, half), half), (slice(half, rows), rows)] if causal else [(slice(0, rows), rows)]
    units = [(head, span) for head in range(HEADS) for span in range(len(spans))]

    def start(head, span):
        columns, count = spans[span]
        kv = head // REP
        lanes = slice(kv * HEAD_DIM, (kv + 1) * HEAD_DIM)
        rows_of = slice(head * HEAD_DIM, (head + 1) * HEAD_DIM)
        scores = mm(keys[:count, lanes], q_ref[rows_of, columns], 1, 0)
        if hidden_keys:
            scores = masked_scores(scores, bound[:, columns])
        return scores, mm(values[:count, lanes], do_ref[rows_of, columns], 1, 0)

    ahead = start(*units[0])
    sums = {}
    for i, (head, span) in enumerate(units):
        columns, count = spans[span]
        kv = head // REP
        rows_of = slice(head * HEAD_DIM, (head + 1) * HEAD_DIM)
        scores, d_probs = ahead
        if i + 1 < len(units):
            ahead = start(*units[i + 1])
        probs = jnp.exp2(scores - lse_ref[head : head + 1, columns])
        d_scores = (probs * (d_probs - delta_ref[head : head + 1, columns])).astype(BF16)
        value_term = mm(probs.astype(BF16), do_ref[rows_of, columns], 1, 1)
        key_term = mm(d_scores, q_ref[rows_of, columns], 1, 1)
        if span in sums:
            sums[span] = (sums[span][0] + key_term, sums[span][1] + value_term)
        else:
            sums[span] = (key_term, value_term)
        dq_ref[rows_of, columns] = dq_ref[rows_of, columns] + mm(
            k_ref[kv * HEAD_DIM : (kv + 1) * HEAD_DIM, :count], d_scores, 1, 0
        )
        if head % REP == REP - 1 and span == len(spans) - 1:
            full = jnp.concatenate(sums[span], 1)
            if causal:
                out_ref[kv, :half] = (full[:half] + jnp.concatenate(sums[0], 1)).astype(BF16)
                out_ref[kv, half:] = full[half:].astype(BF16)
            else:
                out_ref[kv] = full.astype(BF16)
            sums = {}


def backward_kernel(sc, q_ref, do_ref, lse_ref, delta_ref, kv_ref, *refs, rank, which):
    k_ref, v_ref = kv_ref.at[:KVD], kv_ref.at[KVD:]
    dq_ref, out_ref = refs[-2:]
    if len(refs) == 2:
        dq_ref[...] = jnp.zeros_like(dq_ref)
    active, partial, bound = block_facts(sc, rank, which, q_ref.shape[1])
    rest = (k_ref, v_ref, q_ref, do_ref, lse_ref, delta_ref, dq_ref, out_ref)

    if rank == 0 and which == 0:

        @pl.when(active)
        def _():
            backward_block(True, bound, *rest, causal=True)

    else:

        @pl.when(active & jnp.logical_not(partial))
        def _():
            backward_block(False, bound, *rest)

        @pl.when(active & partial)
        def _():
            backward_block(True, bound, *rest)

    @pl.when(jnp.logical_not(active))
    def _():
        out_ref[...] = jnp.zeros_like(out_ref)


def backward(sc, q, d_out, lse, delta, kv, dq, rank, which):
    rows = q.shape[1]
    args = (q, d_out, lse, delta, kv) + (() if dq is None else (dq,))
    grads = (KV_HEADS, rows, 2 * HEAD_DIM)
    kernel = functools.partial(backward_kernel, rank=rank, which=which)
    outs = [((D, rows), F32), (grads, BF16)]
    aliases = None if dq is None else {len(args): 0}
    return call(kernel, f"backward_{rank}_{which}", 12, sc, args, outs, aliases=aliases)


def place(sc, orders, spot, pair):
    return jnp.where((sc[0] & 1) == 0, orders[0][pair], orders[1][pair]) ^ spot


def store_pieces(sc, orders, spot, keep_ref, send_ref, piece_of):
    low = (sc[0] & 1) == 0
    for pair in range(keep_ref.shape[0]):
        even = piece_of(2 * pair)
        odd = piece_of(2 * pair + 1)
        keep_ref[place(sc, orders, spot[0], pair)] = jnp.where(low, even, odd)
        send_ref[place(sc, orders[::-1], spot[1], pair)] = jnp.where(low, odd, even)


def load_pair(sc, orders, spot, keep_ref, got_ref, pair):
    low = (sc[0] & 1) == 0

    def load(refs, where):
        if not isinstance(refs, tuple):
            return refs[where]
        half = refs[0].shape[0]
        inside = where & (half - 1)
        return jnp.where(where < half, refs[0][inside], refs[1][inside])

    one = load(keep_ref, place(sc, orders, spot[0], pair))
    two = load(got_ref, place(sc, orders[::-1], spot[1], pair))
    return jnp.where(low, one, two), jnp.where(low, two, one)


def middle_kernel(
    sc,
    acc_ref,
    m_ref,
    l_ref,
    x_ref,
    cot_ref,
    gain_ref,
    wo_ref,
    wg_ref,
    wu_ref,
    wd_ref,
    y_ref,
    do_ref,
    lse_ref,
    delta_ref,
    dh_ref,
    keep_ref,
    send_ref,
    mixed_ref,
    stack_ref,
    hid_ref,
    dg_ref,
    du_ref,
    *,
    orders,
):
    for head in range(HEADS):
        rows_of = slice(head * HEAD_DIM, (head + 1) * HEAD_DIM)
        mixed_ref[rows_of, :] = acc_ref[rows_of, :] * (1.0 / l_ref[head : head + 1, :])
    lse_ref[:HEADS, :] = m_ref[:HEADS, :] + jnp.log2(l_ref[:HEADS, :])
    gain = column(gain_ref[...])
    cot_t = cot_ref[...]
    cot = cot_t.T
    mixed_low = mixed_ref[...].astype(BF16)
    h = x_ref[...].astype(F32) + mm(wo_ref[...].T, mixed_low, 1, 0)
    scale = lax.rsqrt(jnp.mean(h * h, axis=0, keepdims=True) + epsilon)
    normed_t = (h * scale * gain).astype(BF16)
    normed = normed_t.T

    def start(chunk):
        cols = slice(chunk * CHUNK, (chunk + 1) * CHUNK)
        return (
            mm(normed, wg_ref[:, cols], 1, 0),
            mm(normed, wu_ref[:, cols], 1, 0),
            mm(cot, wd_ref[:, cols], 1, 0),
        )

    chunks = FF // CHUNK
    ahead = start(0)
    for chunk in range(chunks):
        gate, up, d_hidden = ahead
        if chunk + 1 < chunks:
            ahead = start(chunk + 1)
        cols = slice(chunk * CHUNK, (chunk + 1) * CHUNK)
        sig = 1.0 / (1.0 + jnp.exp2(gate * -log2e))
        silu = gate * sig
        hidden = (silu * up).astype(BF16)
        d_gate = (d_hidden * up * (sig * (1.0 + gate * (1.0 - sig)))).astype(BF16)
        d_up = (d_hidden * silu).astype(BF16)
        hid_ref[:, cols] = hidden
        dg_ref[:, cols] = d_gate
        du_ref[:, cols] = d_up
        stack_ref[:D, cols] = mm(normed_t, d_gate, 1, 0).astype(BF16)
        stack_ref[D : 2 * D, cols] = mm(normed_t, d_up, 1, 0).astype(BF16)
        stack_ref[2 * D : 3 * D, cols] = mm(cot_t, hidden, 1, 0).astype(BF16)
    y_ref[...] = (h + mm(wd_ref[...], hid_ref[...], 1, 1)).astype(BF16)
    dn = mm(wg_ref[...], dg_ref[...], 1, 1) + mm(wu_ref[...], du_ref[...], 1, 1)
    unit = h * scale
    gain_sum = jnp.sum(dn * unit, axis=1, keepdims=True)
    scaled = dn * gain
    dh = cot_t.astype(F32) + scale * (
        scaled - unit * jnp.mean(scaled * unit, axis=0, keepdims=True)
    )
    dh_ref[...] = dh
    dh_low = dh.astype(BF16)
    mixed = mixed_ref[...]
    d_mixed = mm(wo_ref[...], dh_low, 1, 0).astype(BF16)
    do_ref[...] = d_mixed
    for head in range(HEADS):
        rows_of = slice(head * HEAD_DIM, (head + 1) * HEAD_DIM)
        delta_ref[head : head + 1, :] = jnp.sum(
            d_mixed[rows_of].astype(F32) * mixed[rows_of], axis=0, keepdims=True
        )
    d_wo = mm(mixed_low, dh_low, 1, 1).astype(BF16)
    gain_row = jnp.broadcast_to(gain_sum, (D, 128)).T[:16].astype(BF16)
    quarter = D // 4
    base = 3 * D
    for k in range(4):
        cols = slice(k * PART, (k + 1) * PART)
        part = d_wo[k * quarter : (k + 1) * quarter]
        stack_ref[base : base + quarter, cols] = part[:, :PART]
        stack_ref[base + quarter : base + 2 * quarter, cols] = jnp.concatenate(
            [part[:, PART:], jnp.zeros((quarter, 2 * PART - D), BF16)], 1
        )
        stack_ref[base + 2 * quarter :, cols] = jnp.zeros((STACK - base - 2 * quarter, PART), BF16)
    stack_ref[base + 2 * quarter : base + 2 * quarter + 16, :D] = gain_row
    rows = keep_ref.shape[1]
    store_pieces(
        sc,
        orders,
        (sc[2], sc[3]),
        keep_ref,
        send_ref,
        lambda p: stack_ref[p * rows : (p + 1) * rows, :],
    )


def middle(sc, acc, m, l, x, cot, gain, wo, wg, wu, wd, orders):
    rows = x.shape[1]
    pairs = len(orders[0])
    half = (pairs, STACK // (2 * pairs), FF)
    args = (acc, m, l, x, cot, gain, wo, wg, wu, wd)
    outs = [
        ((D, rows), BF16),
        ((D, rows), BF16),
        ((16, rows), F32),
        ((16, rows), F32),
        ((D, rows), F32),
        (half, BF16),
        (half, BF16),
    ]
    scratch = [
        pltpu.VMEM((D, rows), F32),
        pltpu.VMEM((STACK, FF), BF16),
        pltpu.VMEM((rows, FF), BF16),
        pltpu.VMEM((rows, FF), BF16),
        pltpu.VMEM((rows, FF), BF16),
    ]
    kernel = functools.partial(middle_kernel, orders=orders)
    return call(kernel, "middle", 34, sc, args, outs, scratch)


def last_kernel(
    sc,
    dq_ref,
    dkv_ref,
    n_ref,
    x_ref,
    dh_ref,
    gain_ref,
    wq_ref,
    wk_ref,
    wv_ref,
    cos_ref,
    sin_ref,
    dx_ref,
    keep_ref,
    send_ref,
    *,
    orders,
):
    cos = cos_ref[...]
    sin = sin_ref[...]
    rows = x_ref.shape[1]
    d_query = rotated(dq_ref[...], cos, sin, HEAD_DIM**-0.5, -1.0).astype(BF16)
    turned = [dkv_ref[kv].astype(F32).T for kv in range(KV_HEADS)]
    d_key = rotated(
        jnp.concatenate([part[:HEAD_DIM] for part in turned], 0), cos, sin, ln2, -1.0
    ).astype(BF16)
    d_value = jnp.concatenate([part[HEAD_DIM:] for part in turned], 0).astype(BF16)
    dn = (
        mm(wq_ref[...], d_query, 1, 0)
        + mm(wk_ref[...], d_key, 0, 0)
        + mm(wv_ref[...], d_value, 0, 0)
    )
    x = x_ref[...].astype(F32)
    scale = lax.rsqrt(jnp.mean(x * x, axis=0, keepdims=True) + epsilon)
    unit = x * scale
    scaled = dn * column(gain_ref[...])
    dx_ref[...] = (
        dh_ref[...] + scale * (scaled - unit * jnp.mean(scaled * unit, axis=0, keepdims=True))
    ).astype(BF16)
    pad = 64
    joined = jnp.concatenate([d_query, jnp.zeros((pad, rows), BF16), d_key, d_value], 0)
    grad = mm(n_ref[...], joined, 1, 1)
    gain_sum = jnp.sum(dn * unit, axis=1, keepdims=True)
    spot = D // 128
    lane = lax.broadcasted_iota(jnp.int32, (D, 128), 1)
    mixed = jnp.where(
        lane < D - spot * 128, grad[:, spot * 128 : (spot + 1) * 128], gain_sum
    )
    tiles = [
        (mixed if i == spot else grad[:, i * 128 : (i + 1) * 128]).astype(BF16) for i in range(8)
    ]
    piece_rows = keep_ref.shape[1]

    def piece_of(piece):
        top = (piece // 8) * piece_rows
        count = max(min(piece_rows, D - top), 0)
        empty = jnp.zeros((piece_rows - count, 128), BF16)
        if count == 0:
            return empty
        part = tiles[piece % 8][top : top + count]
        return jnp.concatenate([part, empty], 0) if count < piece_rows else part

    store_pieces(sc, orders, (sc[4], sc[5]), keep_ref, send_ref, piece_of)


def last(sc, dq, dkv, n, x, dh, gain, wq, wk, wv, cos, sin, orders):
    pieces = 2 * len(orders[0])
    rows = x.shape[1]
    piece_rows = -(-D // max(pieces // 8, 1))
    half = (pieces // 2, -(-piece_rows // 16) * 16, 128)
    table = pl.BlockSpec((HALF, rows), lambda i, sc: (0, sc[0]))
    return pl.pallas_call(
        functools.partial(last_kernel, orders=orders),
        grid_spec=pltpu.PrefetchScalarGridSpec(
            num_scalar_prefetch=1,
            grid=(1,),
            in_specs=[whole(part.shape) for part in (dq, dkv, n, x, dh, gain, wq, wk, wv)]
            + [table, table],
            out_specs=[whole((D, rows)), whole(half), whole(half)],
        ),
        out_shape=[
            jax.ShapeDtypeStruct((D, rows), BF16),
            jax.ShapeDtypeStruct(half, BF16),
            jax.ShapeDtypeStruct(half, BF16),
        ],
        compiler_params=params(24),
        cost_estimate=cost(),
        name="last",
    )(sc, dq, dkv, n, x, dh, gain, wq, wk, wv, cos, sin)


def unpack_big_kernel(
    sc, keep_ref, far_ref, got_ref, got_far_ref, gate_ref, up_ref, down_ref, wo_ref, gain_ref, *, orders
):
    step = pl.program_id(0)
    quarter = D // 4
    refs = (gate_ref, up_ref, down_ref)
    pairs, rows = 2 * keep_ref.shape[0], keep_ref.shape[1]
    kept, got = (keep_ref, far_ref), (got_ref, got_far_ref)
    rest = []
    for pair in range(pairs):
        for side, part in enumerate(load_pair(sc, orders, (sc[2], sc[3]), kept, got, pair)):
            part = part.astype(F32)
            top = (2 * pair + side) * rows
            if top < 3 * D:
                refs[top // D][top % D : top % D + rows, :] = part
            else:
                rest.append(part)
    rest = jnp.concatenate(rest, 0)
    wo_ref[:, :PART] = rest[:quarter]
    wo_ref[:, PART:] = rest[quarter : 2 * quarter, : D - PART]
    row = rest[2 * quarter : 2 * quarter + 1]

    @pl.when(step == 0)
    def _():
        gain_ref[:, :PART] = row

    @pl.when(step == 1)
    def _():
        gain_ref[:, PART:] = row[:, : D - PART]


def unpack_big(sc, keep, got, orders):
    shapes = [(D, FF), (D, FF), (D, FF), (D, D), (1, D)]
    cols = pl.BlockSpec((D, PART), lambda i, sc: (0, i))
    part = pl.BlockSpec(keep[0].shape[:2] + (PART,), lambda i, sc: (0, 0, i))
    return pl.pallas_call(
        functools.partial(unpack_big_kernel, orders=orders),
        grid_spec=pltpu.PrefetchScalarGridSpec(
            num_scalar_prefetch=1,
            grid=(FF // PART,),
            in_specs=[part] * 4,
            out_specs=[
                cols,
                cols,
                cols,
                pl.BlockSpec((D // 4, D), lambda i, sc: (i, 0)),
                whole((1, D)),
            ],
        ),
        out_shape=[jax.ShapeDtypeStruct(shape, F32) for shape in shapes],
        compiler_params=params(32),
        cost_estimate=cost(),
        name="unpack_big",
    )(sc, *keep, *got)


def unpack_small_kernel(sc, keep_ref, got_ref, q_ref, k_ref, v_ref, gain_ref, *, orders):
    pairs, rows, _ = keep_ref.shape
    columns = [[] for _ in range(8)]
    for pair in range(pairs):
        for side, part in enumerate(load_pair(sc, orders, (sc[4], sc[5]), keep_ref, got_ref, pair)):
            piece = 2 * pair + side
            count = min(rows, D - (piece // 8) * rows)
            if count > 0:
                columns[piece % 8].append(part[:count].astype(F32))
    full = [jnp.concatenate(parts, 0) if len(parts) > 1 else parts[0] for parts in columns]
    spot = D // 128
    for i in range(spot):
        q_ref[:, i * 128 : (i + 1) * 128] = full[i]
    q_ref[:, spot * 128 :] = full[spot][:, : D - spot * 128]
    gain_ref[...] = full[spot].T[D - spot * 128]
    key_value = jnp.concatenate(full[spot + 1 :], 1).T
    k_ref[...] = key_value[:KVD]
    v_ref[...] = key_value[KVD:]


def unpack_small(sc, keep, got, orders):
    shapes = [(D, D), (KVD, D), (KVD, D), (D,)]
    kernel = functools.partial(unpack_small_kernel, orders=orders)
    return call(kernel, "unpack_small", 12, sc, (keep, got), [(shape, F32) for shape in shapes])


def plus(*parts):
    total = parts[0].astype(F32)
    for part in parts[1:]:
        total = total + part.astype(F32)
    return total.astype(BF16)


def swap(values, step):
    grp_size, seq_size = lax.axis_size("grp"), lax.axis_size("seq")
    moves = [(i, i ^ step[i & 1]) for i in range(grp_size * seq_size)]
    spot = [(i % seq_size) * grp_size + i // seq_size for i in range(grp_size * seq_size)]
    return lax.ppermute(values, ("seq", "grp"), [(spot[i], spot[j]) for i, j in moves])


def exchanged(kept, sent, step, gate=None):
    got = after(swap(sent, step), gate)
    half = kept.shape[0] // 2
    if half == 0:
        return plus(kept, got), None
    return plus(kept[:half], got[:half]), plus(kept[half:], got[half:])


def doubled(values, step, gate=None):
    return jnp.concatenate([values, after(swap(values, step), gate)], 0)


def spread_bits(value, places):
    count = len(places)
    total = 0
    for t, bit in enumerate(places):
        total = total | (((value >> bit) & 1) << (count - 1 - t))
    return total


def after(value, other):
    return value if other is None else lax.optimization_barrier((value, other))[0]


def build(seq_size, grp_size):
    count = seq_size * grp_size
    chips = seq_size // 2
    core = (1, 1)
    seq_bits = seq_size.bit_length() - 1
    chip_bits = list(range(1, seq_bits))
    grp_bits = list(range(seq_bits, count.bit_length() - 1))
    routes = [grp_bits + chip_bits, grp_bits[::-1] + chip_bits[::-1]]
    big_steps = [(1 << one, 1 << two) for one, two in zip(*routes)]
    grp_moves = [(i, (i * seq_size, i * seq_size)) for i in range(1, grp_size)]
    chip_steps = big_steps[len(grp_bits) :]
    big_places = [[bit - 1 for bit in route] for route in routes]
    big_orders = [[spread_bits(j, spots) for j in range(count // 2)] for spots in big_places]
    small_orders = [list(range(grp_size))] * 2

    def shards(
        inputs,
        lengths,
        attn_gain,
        w_query,
        w_key,
        w_value,
        w_out,
        ffn_gain,
        w_gate,
        w_up,
        w_down,
        cotangent,
    ):
        rows = inputs.shape[1]
        mine = lax.axis_index("seq")
        group = lax.axis_index("grp")
        number = group * chips + lax.shift_right_logical(mine, 1)
        low = (mine & 1) == 0
        one, two = [spread_bits(number, spots) for spots in big_places]
        spots = [jnp.where(low, one, two), jnp.where(low, two, one), group, group]
        sc = jnp.stack([mine, lengths[0]] + spots).astype(jnp.int32)
        cos_np, sin_np = rope_tables(rows * seq_size)
        cos = jnp.asarray(cos_np)
        sin = jnp.asarray(sin_np)
        x = inputs[0].T
        cot = cotangent[0].T
        wk = w_key.T
        wv = w_value.T
        wd = w_down.T

        down = [(i + 2, i) for i in range(seq_size - 2)]
        normed, own = with_tables(
            keys_kernel,
            "keys",
            sc,
            (x, attn_gain, wk, wv),
            cos,
            sin,
            [(D, rows), (2 * KVD, rows)],
        )
        [query] = with_tables(
            query_kernel, "query", sc, (normed, w_query), cos, sin, [(D, rows)]
        )
        up = [(i, i + 2) for i in range(seq_size - 2)]
        pairs = []
        state = None
        block = own
        for rank in range(chips):
            gate = None if state is None else state[0]
            pairs.append((block, swap(after(block, gate), core)))
            if rank + 1 < chips:
                block = lax.ppermute(block, "seq", up)
            for which in (0, 1):
                state = forward(sc, query, pairs[-1][which], state, rank, which)
        m, l, acc = state
        outputs, d_mixed, lse, delta, d_resid, big, send = middle(
            sc, acc, m, l, x, cot, ffn_gain, w_out, w_gate, w_up, wd, big_orders
        )
        stages = [functools.partial(exchanged, step=step) for step in [core] + big_steps]
        when = [1, 4, 5, 6] + list(range(7, 2 * seq_size))
        dq = None
        passed = None
        calls = 0
        for rank in reversed(range(chips)):
            grads = [None, None]
            for which in (1, 0):
                if calls in when and stages:
                    big, send = stages.pop(0)(big, send, gate=dq)
                    dq = after(dq, big)
                dq, grads[which] = backward(
                    sc, query, d_mixed, lse, delta, pairs[rank][which], dq, rank, which
                )
                calls += 1
            terms = [grads[0], swap(grads[1], core)]
            if passed is not None:
                terms.append(lax.ppermute(passed, "seq", down))
            passed = plus(*terms)
            dq = after(dq, passed)
        for stage in stages:
            big, send = stage(big, send, gate=dq)
        dq = after(dq, big)

        d_inputs, small, small_send = last(
            sc, dq, passed, normed, x, d_resid, attn_gain, w_query, wk, wv, cos, sin, small_orders
        )
        big = doubled(big, big_steps[-1], small_send)
        small_send = after(small_send, big)
        small = plus(small, swap(small_send, core))
        marks = [small]
        small = plus(small[:1], *[swap(small[i : i + 1], step) for i, step in grp_moves])
        marks.append(small)
        for step in chip_steps:
            small = plus(small, swap(small, step))
            marks.append(small)
        for i, step in enumerate(big_steps[-2:0:-1]):
            big = doubled(big, step, marks[min(i, 1)])
        far = after(swap(big, big_steps[0]), small)
        others = [swap(small, step) for _, step in grp_moves]
        d_gate, d_up, d_down, d_out, d_ffn_gain = unpack_big(
            sc, (big, far), (swap(big, core), swap(far, core)), big_orders
        )
        others = [after(other, d_ffn_gain) for other in others]
        small = jnp.concatenate([small] + others, 0)
        d_query, d_key, d_value, d_attn_gain = unpack_small(
            sc, small, swap(small, core), small_orders
        )
        return (
            outputs.T[None],
            d_inputs.T[None],
            d_attn_gain,
            d_query,
            d_key.T,
            d_value.T,
            d_out,
            d_ffn_gain.reshape(D),
            d_gate,
            d_up,
            d_down.T,
        )

    return shards


def solution(mesh):
    tokens = P("grp", "seq", None)
    return jax.shard_map(
        build(mesh.shape["seq"], mesh.shape["grp"]),
        mesh=mesh,
        in_specs=(tokens, P("grp")) + (P(),) * 9 + (tokens,),
        out_specs=(tokens, tokens) + (P(),) * 9,
        check_vma=False,
    )
```

```python
import functools
import math

import jax
import jax.numpy as jnp
import numpy as np
from jax import lax
from jax.experimental import pallas as pl
from jax.experimental.pallas import tpu as pltpu
from jax.sharding import PartitionSpec as P

D = 576
KV_HEADS = 3
HEAD_DIM = 64
REP = 3
HEADS = KV_HEADS * REP
KVD = 192
FF = 1536
CHUNK = 512
STACK = 2048
PART = 384
HALF = HEAD_DIM // 2

epsilon = 1e-05
rope_base = 100000.0
neg_big = -1e30
log2e = math.log2(math.e)
ln2 = math.log(2.0)

F32 = jnp.float32
BF16 = jnp.bfloat16


def mm(left, right, left_dim, right_dim):
    return lax.dot_general(
        left, right, (((left_dim,), (right_dim,)), ((), ())), preferred_element_type=F32
    )


def params(mebibytes):
    return pltpu.CompilerParams(vmem_limit_bytes=mebibytes * 2**20)


def whole(shape):
    return pl.BlockSpec(shape, lambda *_: (0,) * len(shape))


def call(kernel, name, limit, sc, args, outs, scratch=(), aliases=None):
    return pl.pallas_call(
        kernel,
        in_specs=[pl.BlockSpec(memory_space=pltpu.SMEM)]
        + [pl.BlockSpec(memory_space=pltpu.VMEM)] * len(args),
        out_specs=[pl.BlockSpec(memory_space=pltpu.VMEM)] * len(outs),
        out_shape=[jax.ShapeDtypeStruct(*out) for out in outs],
        scratch_shapes=list(scratch),
        input_output_aliases=aliases or {},
        compiler_params=params(limit),
        cost_estimate=cost(),
        name=name,
    )(sc, *args)


def cost():
    return pl.CostEstimate(flops=10**8, bytes_accessed=2**17, transcendentals=0)


def rope_tables(length):
    steps = np.arange(HALF, dtype=np.float32)
    freqs = (1.0 / np.float32(rope_base) ** (steps * np.float32(2.0) / np.float32(HEAD_DIM))).astype(
        np.float32
    )
    angles = np.arange(length, dtype=np.float32)[None, :] * freqs[:, None]
    return np.cos(angles).astype(np.float32), np.sin(angles).astype(np.float32)


def rotated(rows, cos, sin, scale, sign):
    parts = []
    for start in range(0, rows.shape[0], HEAD_DIM):
        one = rows[start : start + HALF]
        two = rows[start + HALF : start + HEAD_DIM]
        parts.append((one * cos - sign * (two * sin)) * scale)
        parts.append((two * cos + sign * (one * sin)) * scale)
    return jnp.concatenate(parts, 0)


def column(vector):
    return jnp.broadcast_to(vector[None], (8, vector.shape[0])).T[:, :1]


def keys_kernel(sc, x_ref, gain_ref, wk_ref, wv_ref, cos_ref, sin_ref, n_ref, kv_ref):
    x = x_ref[...].astype(F32)
    scale = lax.rsqrt(jnp.mean(x * x, axis=0, keepdims=True) + epsilon)
    normed = (x * scale * column(gain_ref[...])).astype(BF16)
    n_ref[...] = normed
    key = mm(wk_ref[...], normed, 1, 0)
    kv_ref[:KVD, :] = rotated(key, cos_ref[...], sin_ref[...], 1.0, 1.0).astype(BF16)
    kv_ref[KVD:, :] = mm(wv_ref[...], normed, 1, 0).astype(BF16)


def query_kernel(sc, n_ref, wq_ref, cos_ref, sin_ref, q_ref):
    query = mm(wq_ref[...].T, n_ref[...], 1, 0)
    q_ref[...] = rotated(
        query, cos_ref[...], sin_ref[...], HEAD_DIM**-0.5 * log2e, 1.0
    ).astype(BF16)


def with_tables(kernel, name, sc, args, cos, sin, outs):
    rows = args[0].shape[1]
    table = pl.BlockSpec((HALF, rows), lambda i, sc: (0, sc[0]))
    return pl.pallas_call(
        kernel,
        grid_spec=pltpu.PrefetchScalarGridSpec(
            num_scalar_prefetch=1,
            grid=(1,),
            in_specs=[whole(part.shape) for part in args] + [table, table],
            out_specs=[whole(shape) for shape in outs],
        ),
        out_shape=[jax.ShapeDtypeStruct(shape, BF16) for shape in outs],
        compiler_params=params(56),
        cost_estimate=cost(),
        name=name,
    )(sc, *args, cos, sin)


def block_facts(sc, rank, which, rows):
    mine = sc[0]
    block = mine - 2 * rank if which == 0 else (mine ^ 1) - 2 * rank
    length = sc[1]
    start = block * rows
    active = (block >= 0) & (block <= mine) & (start < length)
    partial = (block == mine) | (start + rows > length)
    pos = mine * rows + lax.broadcasted_iota(jnp.int32, (1, rows), 1)
    bound = jnp.minimum(pos, length - 1) - start
    return active, partial, bound


def masked_scores(scores, bound):
    rows = lax.broadcasted_iota(jnp.int32, scores.shape, 0)
    return jnp.where(rows <= bound, scores, neg_big)


def forward_block(hidden_keys, bound, k_ref, v_ref, q_ref, m_ref, l_ref, acc_ref):
    rows = q_ref.shape[1]
    keys = k_ref[...].T
    ones = jnp.ones((8, rows), BF16)

    def score(head):
        kv = head // REP
        scores = mm(
            keys[:, kv * HEAD_DIM : (kv + 1) * HEAD_DIM],
            q_ref[head * HEAD_DIM : (head + 1) * HEAD_DIM, :],
            1,
            0,
        )
        if hidden_keys:
            scores = masked_scores(scores, bound)
        return scores, jnp.max(scores, axis=0, keepdims=True)

    def weigh(head, scores, top):
        kv = head // REP
        old = m_ref[head : head + 1, :]
        new = jnp.maximum(old, top)
        weights = jnp.exp2(scores - new).astype(BF16)
        values = jnp.concatenate(
            [v_ref[kv * HEAD_DIM : (kv + 1) * HEAD_DIM, :], ones], 0
        )
        return new, jnp.exp2(old - new), mm(values, weights, 1, 0)

    def store(head, new, fade, out):
        rows_of = slice(head * HEAD_DIM, (head + 1) * HEAD_DIM)
        m_ref[head : head + 1, :] = new
        l_ref[head : head + 1, :] = l_ref[head : head + 1, :] * fade + out[HEAD_DIM : HEAD_DIM + 1]
        acc_ref[rows_of, :] = acc_ref[rows_of, :] * fade + out[:HEAD_DIM]

    ahead = score(0)
    held = None
    for head in range(HEADS):
        current = ahead
        if head + 1 < HEADS:
            ahead = score(head + 1)
        result = weigh(head, *current)
        if held is not None:
            store(*held)
        held = (head,) + result
    store(*held)


def forward_kernel(sc, q_ref, kv_ref, *refs, rank, which):
    k_ref, v_ref = kv_ref.at[:KVD], kv_ref.at[KVD:]
    m_ref, l_ref, acc_ref = refs[-3:]
    if len(refs) == 3:
        m_ref[...] = jnp.full_like(m_ref, neg_big)
        l_ref[...] = jnp.zeros_like(l_ref)
        acc_ref[...] = jnp.zeros_like(acc_ref)
    active, partial, bound = block_facts(sc, rank, which, q_ref.shape[1])

    @pl.when(active & jnp.logical_not(partial))
    def _():
        forward_block(False, bound, k_ref, v_ref, q_ref, m_ref, l_ref, acc_ref)

    @pl.when(active & partial)
    def _():
        forward_block(True, bound, k_ref, v_ref, q_ref, m_ref, l_ref, acc_ref)


def forward(sc, q, block, state, rank, which):
    rows = q.shape[1]
    state = () if state is None else tuple(state)
    kernel = functools.partial(forward_kernel, rank=rank, which=which)
    outs = [((16, rows), F32), ((16, rows), F32), ((D, rows), F32)]
    aliases = {3: 0, 4: 1, 5: 2} if state else None
    return call(
        kernel, f"forward_{rank}_{which}", 12, sc, (q, block, *state), outs, aliases=aliases
    )


def backward_block(
    hidden_keys, bound, k_ref, v_ref, q_ref, do_ref, lse_ref, delta_ref, dq_ref, out_ref, causal=False
):
    rows = q_ref.shape[1]
    keys = k_ref[...].T
    values = v_ref[...].T
    half = rows // 2
    spans = [(slice(0, half), half), (slice(half, rows), rows)] if causal else [(slice(0, rows), rows)]
    units = [(head, span) for head in range(HEADS) for span in range(len(spans))]

    def start(head, span):
        columns, count = spans[span]
        kv = head // REP
        lanes = slice(kv * HEAD_DIM, (kv + 1) * HEAD_DIM)
        rows_of = slice(head * HEAD_DIM, (head + 1) * HEAD_DIM)
        scores = mm(keys[:count, lanes], q_ref[rows_of, columns], 1, 0)
        if hidden_keys:
            scores = masked_scores(scores, bound[:, columns])
        return scores, mm(values[:count, lanes], do_ref[rows_of, columns], 1, 0)

    ahead = start(*units[0])
    sums = {}
    for i, (head, span) in enumerate(units):
        columns, count = spans[span]
        kv = head // REP
        rows_of = slice(head * HEAD_DIM, (head + 1) * HEAD_DIM)
        scores, d_probs = ahead
        if i + 1 < len(units):
            ahead = start(*units[i + 1])
        probs = jnp.exp2(scores - lse_ref[head : head + 1, columns])
        d_scores = (probs * (d_probs - delta_ref[head : head + 1, columns])).astype(BF16)
        value_term = mm(probs.astype(BF16), do_ref[rows_of, columns], 1, 1)
        key_term = mm(d_scores, q_ref[rows_of, columns], 1, 1)
        if span in sums:
            sums[span] = (sums[span][0] + key_term, sums[span][1] + value_term)
        else:
            sums[span] = (key_term, value_term)
        dq_ref[rows_of, columns] = dq_ref[rows_of, columns] + mm(
            k_ref[kv * HEAD_DIM : (kv + 1) * HEAD_DIM, :count], d_scores, 1, 0
        )
        if head % REP == REP - 1 and span == len(spans) - 1:
            full = jnp.concatenate(sums[span], 1)
            if causal:
                out_ref[kv, :half] = (full[:half] + jnp.concatenate(sums[0], 1)).astype(BF16)
                out_ref[kv, half:] = full[half:].astype(BF16)
            else:
                out_ref[kv] = full.astype(BF16)
            sums = {}


def backward_kernel(sc, q_ref, do_ref, lse_ref, delta_ref, kv_ref, *refs, rank, which):
    k_ref, v_ref = kv_ref.at[:KVD], kv_ref.at[KVD:]
    dq_ref, out_ref = refs[-2:]
    if len(refs) == 2:
        dq_ref[...] = jnp.zeros_like(dq_ref)
    active, partial, bound = block_facts(sc, rank, which, q_ref.shape[1])
    rest = (k_ref, v_ref, q_ref, do_ref, lse_ref, delta_ref, dq_ref, out_ref)

    if rank == 0 and which == 0:

        @pl.when(active)
        def _():
            backward_block(True, bound, *rest, causal=True)

    else:

        @pl.when(active & jnp.logical_not(partial))
        def _():
            backward_block(False, bound, *rest)

        @pl.when(active & partial)
        def _():
            backward_block(True, bound, *rest)

    @pl.when(jnp.logical_not(active))
    def _():
        out_ref[...] = jnp.zeros_like(out_ref)


def backward(sc, q, d_out, lse, delta, kv, dq, rank, which):
    rows = q.shape[1]
    args = (q, d_out, lse, delta, kv) + (() if dq is None else (dq,))
    grads = (KV_HEADS, rows, 2 * HEAD_DIM)
    kernel = functools.partial(backward_kernel, rank=rank, which=which)
    outs = [((D, rows), F32), (grads, BF16)]
    aliases = None if dq is None else {len(args): 0}
    return call(kernel, f"backward_{rank}_{which}", 12, sc, args, outs, aliases=aliases)


def place(sc, orders, spot, pair):
    return jnp.where((sc[0] & 1) == 0, orders[0][pair], orders[1][pair]) ^ spot


def store_pieces(sc, orders, spot, keep_ref, send_ref, piece_of):
    low = (sc[0] & 1) == 0
    for pair in range(keep_ref.shape[0]):
        even = piece_of(2 * pair)
        odd = piece_of(2 * pair + 1)
        keep_ref[place(sc, orders, spot[0], pair)] = jnp.where(low, even, odd)
        send_ref[place(sc, orders[::-1], spot[1], pair)] = jnp.where(low, odd, even)


def load_pair(sc, orders, spot, keep_ref, got_ref, pair):
    low = (sc[0] & 1) == 0

    def load(refs, where):
        if not isinstance(refs, tuple):
            return refs[where]
        half = refs[0].shape[0]
        inside = where & (half - 1)
        return jnp.where(where < half, refs[0][inside], refs[1][inside])

    one = load(keep_ref, place(sc, orders, spot[0], pair))
    two = load(got_ref, place(sc, orders[::-1], spot[1], pair))
    return jnp.where(low, one, two), jnp.where(low, two, one)


def middle_kernel(
    sc,
    acc_ref,
    m_ref,
    l_ref,
    x_ref,
    cot_ref,
    gain_ref,
    wo_ref,
    wg_ref,
    wu_ref,
    wd_ref,
    y_ref,
    do_ref,
    lse_ref,
    delta_ref,
    dh_ref,
    keep_ref,
    send_ref,
    mixed_ref,
    stack_ref,
    hid_ref,
    dg_ref,
    du_ref,
    *,
    orders,
):
    for head in range(HEADS):
        rows_of = slice(head * HEAD_DIM, (head + 1) * HEAD_DIM)
        mixed_ref[rows_of, :] = acc_ref[rows_of, :] * (1.0 / l_ref[head : head + 1, :])
    lse_ref[:HEADS, :] = m_ref[:HEADS, :] + jnp.log2(l_ref[:HEADS, :])
    gain = column(gain_ref[...])
    cot_t = cot_ref[...]
    cot = cot_t.T
    mixed_low = mixed_ref[...].astype(BF16)
    h = x_ref[...].astype(F32) + mm(wo_ref[...].T, mixed_low, 1, 0)
    scale = lax.rsqrt(jnp.mean(h * h, axis=0, keepdims=True) + epsilon)
    normed_t = (h * scale * gain).astype(BF16)
    normed = normed_t.T

    def start(chunk):
        cols = slice(chunk * CHUNK, (chunk + 1) * CHUNK)
        return (
            mm(normed, wg_ref[:, cols], 1, 0),
            mm(normed, wu_ref[:, cols], 1, 0),
            mm(cot, wd_ref[:, cols], 1, 0),
        )

    chunks = FF // CHUNK
    ahead = start(0)
    for chunk in range(chunks):
        gate, up, d_hidden = ahead
        if chunk + 1 < chunks:
            ahead = start(chunk + 1)
        cols = slice(chunk * CHUNK, (chunk + 1) * CHUNK)
        sig = 1.0 / (1.0 + jnp.exp2(gate * -log2e))
        silu = gate * sig
        hidden = (silu * up).astype(BF16)
        d_gate = (d_hidden * up * (sig * (1.0 + gate * (1.0 - sig)))).astype(BF16)
        d_up = (d_hidden * silu).astype(BF16)
        hid_ref[:, cols] = hidden
        dg_ref[:, cols] = d_gate
        du_ref[:, cols] = d_up
        stack_ref[:D, cols] = mm(normed_t, d_gate, 1, 0).astype(BF16)
        stack_ref[D : 2 * D, cols] = mm(normed_t, d_up, 1, 0).astype(BF16)
        stack_ref[2 * D : 3 * D, cols] = mm(cot_t, hidden, 1, 0).astype(BF16)
    y_ref[...] = (h + mm(wd_ref[...], hid_ref[...], 1, 1)).astype(BF16)
    dn = mm(wg_ref[...], dg_ref[...], 1, 1) + mm(wu_ref[...], du_ref[...], 1, 1)
    unit = h * scale
    gain_sum = jnp.sum(dn * unit, axis=1, keepdims=True)
    scaled = dn * gain
    dh = cot_t.astype(F32) + scale * (
        scaled - unit * jnp.mean(scaled * unit, axis=0, keepdims=True)
    )
    dh_ref[...] = dh
    dh_low = dh.astype(BF16)
    mixed = mixed_ref[...]
    d_mixed = mm(wo_ref[...], dh_low, 1, 0).astype(BF16)
    do_ref[...] = d_mixed
    for head in range(HEADS):
        rows_of = slice(head * HEAD_DIM, (head + 1) * HEAD_DIM)
        delta_ref[head : head + 1, :] = jnp.sum(
            d_mixed[rows_of].astype(F32) * mixed[rows_of], axis=0, keepdims=True
        )
    d_wo = mm(mixed_low, dh_low, 1, 1).astype(BF16)
    gain_row = jnp.broadcast_to(gain_sum, (D, 128)).T[:16].astype(BF16)
    quarter = D // 4
    base = 3 * D
    for k in range(4):
        cols = slice(k * PART, (k + 1) * PART)
        part = d_wo[k * quarter : (k + 1) * quarter]
        stack_ref[base : base + quarter, cols] = part[:, :PART]
        stack_ref[base + quarter : base + 2 * quarter, cols] = jnp.concatenate(
            [part[:, PART:], jnp.zeros((quarter, 2 * PART - D), BF16)], 1
        )
        stack_ref[base + 2 * quarter :, cols] = jnp.zeros((STACK - base - 2 * quarter, PART), BF16)
    stack_ref[base + 2 * quarter : base + 2 * quarter + 16, :D] = gain_row
    rows = keep_ref.shape[1]
    store_pieces(
        sc,
        orders,
        (sc[2], sc[3]),
        keep_ref,
        send_ref,
        lambda p: stack_ref[p * rows : (p + 1) * rows, :],
    )


def middle(sc, acc, m, l, x, cot, gain, wo, wg, wu, wd, orders):
    rows = x.shape[1]
    pairs = len(orders[0])
    half = (pairs, STACK // (2 * pairs), FF)
    args = (acc, m, l, x, cot, gain, wo, wg, wu, wd)
    outs = [
        ((D, rows), BF16),
        ((D, rows), BF16),
        ((16, rows), F32),
        ((16, rows), F32),
        ((D, rows), F32),
        (half, BF16),
        (half, BF16),
    ]
    scratch = [
        pltpu.VMEM((D, rows), F32),
        pltpu.VMEM((STACK, FF), BF16),
        pltpu.VMEM((rows, FF), BF16),
        pltpu.VMEM((rows, FF), BF16),
        pltpu.VMEM((rows, FF), BF16),
    ]
    kernel = functools.partial(middle_kernel, orders=orders)
    return call(kernel, "middle", 34, sc, args, outs, scratch)


def last_kernel(
    sc,
    dq_ref,
    dkv_ref,
    n_ref,
    x_ref,
    dh_ref,
    gain_ref,
    wq_ref,
    wk_ref,
    wv_ref,
    cos_ref,
    sin_ref,
    dx_ref,
    keep_ref,
    send_ref,
    *,
    orders,
):
    cos = cos_ref[...]
    sin = sin_ref[...]
    rows = x_ref.shape[1]
    d_query = rotated(dq_ref[...], cos, sin, HEAD_DIM**-0.5, -1.0).astype(BF16)
    turned = [dkv_ref[kv].astype(F32).T for kv in range(KV_HEADS)]
    d_key = rotated(
        jnp.concatenate([part[:HEAD_DIM] for part in turned], 0), cos, sin, ln2, -1.0
    ).astype(BF16)
    d_value = jnp.concatenate([part[HEAD_DIM:] for part in turned], 0).astype(BF16)
    dn = (
        mm(wq_ref[...], d_query, 1, 0)
        + mm(wk_ref[...], d_key, 0, 0)
        + mm(wv_ref[...], d_value, 0, 0)
    )
    x = x_ref[...].astype(F32)
    scale = lax.rsqrt(jnp.mean(x * x, axis=0, keepdims=True) + epsilon)
    unit = x * scale
    scaled = dn * column(gain_ref[...])
    dx_ref[...] = (
        dh_ref[...] + scale * (scaled - unit * jnp.mean(scaled * unit, axis=0, keepdims=True))
    ).astype(BF16)
    pad = 64
    joined = jnp.concatenate([d_query, jnp.zeros((pad, rows), BF16), d_key, d_value], 0)
    grad = mm(n_ref[...], joined, 1, 1)
    gain_sum = jnp.sum(dn * unit, axis=1, keepdims=True)
    spot = D // 128
    lane = lax.broadcasted_iota(jnp.int32, (D, 128), 1)
    mixed = jnp.where(
        lane < D - spot * 128, grad[:, spot * 128 : (spot + 1) * 128], gain_sum
    )
    tiles = [
        (mixed if i == spot else grad[:, i * 128 : (i + 1) * 128]).astype(BF16) for i in range(8)
    ]
    piece_rows = keep_ref.shape[1]

    def piece_of(piece):
        top = (piece // 8) * piece_rows
        count = max(min(piece_rows, D - top), 0)
        empty = jnp.zeros((piece_rows - count, 128), BF16)
        if count == 0:
            return empty
        part = tiles[piece % 8][top : top + count]
        return jnp.concatenate([part, empty], 0) if count < piece_rows else part

    store_pieces(sc, orders, (sc[4], sc[5]), keep_ref, send_ref, piece_of)


def last(sc, dq, dkv, n, x, dh, gain, wq, wk, wv, cos, sin, orders):
    pieces = 2 * len(orders[0])
    rows = x.shape[1]
    piece_rows = -(-D // max(pieces // 8, 1))
    half = (pieces // 2, -(-piece_rows // 16) * 16, 128)
    table = pl.BlockSpec((HALF, rows), lambda i, sc: (0, sc[0]))
    return pl.pallas_call(
        functools.partial(last_kernel, orders=orders),
        grid_spec=pltpu.PrefetchScalarGridSpec(
            num_scalar_prefetch=1,
            grid=(1,),
            in_specs=[whole(part.shape) for part in (dq, dkv, n, x, dh, gain, wq, wk, wv)]
            + [table, table],
            out_specs=[whole((D, rows)), whole(half), whole(half)],
        ),
        out_shape=[
            jax.ShapeDtypeStruct((D, rows), BF16),
            jax.ShapeDtypeStruct(half, BF16),
            jax.ShapeDtypeStruct(half, BF16),
        ],
        compiler_params=params(24),
        cost_estimate=cost(),
        name="last",
    )(sc, dq, dkv, n, x, dh, gain, wq, wk, wv, cos, sin)


def unpack_big_kernel(
    sc, keep_ref, far_ref, got_ref, got_far_ref, gate_ref, up_ref, down_ref, wo_ref, gain_ref, *, orders
):
    step = pl.program_id(0)
    quarter = D // 4
    refs = (gate_ref, up_ref, down_ref)
    pairs, rows = 2 * keep_ref.shape[0], keep_ref.shape[1]
    kept, got = (keep_ref, far_ref), (got_ref, got_far_ref)
    rest = []
    for pair in range(pairs):
        for side, part in enumerate(load_pair(sc, orders, (sc[2], sc[3]), kept, got, pair)):
            part = part.astype(F32)
            top = (2 * pair + side) * rows
            if top < 3 * D:
                refs[top // D][top % D : top % D + rows, :] = part
            else:
                rest.append(part)
    rest = jnp.concatenate(rest, 0)
    wo_ref[:, :PART] = rest[:quarter]
    wo_ref[:, PART:] = rest[quarter : 2 * quarter, : D - PART]
    row = rest[2 * quarter : 2 * quarter + 1]

    @pl.when(step == 0)
    def _():
        gain_ref[:, :PART] = row

    @pl.when(step == 1)
    def _():
        gain_ref[:, PART:] = row[:, : D - PART]


def unpack_big(sc, keep, got, orders):
    shapes = [(D, FF), (D, FF), (D, FF), (D, D), (1, D)]
    cols = pl.BlockSpec((D, PART), lambda i, sc: (0, i))
    part = pl.BlockSpec(keep[0].shape[:2] + (PART,), lambda i, sc: (0, 0, i))
    return pl.pallas_call(
        functools.partial(unpack_big_kernel, orders=orders),
        grid_spec=pltpu.PrefetchScalarGridSpec(
            num_scalar_prefetch=1,
            grid=(FF // PART,),
            in_specs=[part] * 4,
            out_specs=[
                cols,
                cols,
                cols,
                pl.BlockSpec((D // 4, D), lambda i, sc: (i, 0)),
                whole((1, D)),
            ],
        ),
        out_shape=[jax.ShapeDtypeStruct(shape, F32) for shape in shapes],
        compiler_params=params(32),
        cost_estimate=cost(),
        name="unpack_big",
    )(sc, *keep, *got)


def unpack_small_kernel(sc, keep_ref, got_ref, q_ref, k_ref, v_ref, gain_ref, *, orders):
    pairs, rows, _ = keep_ref.shape
    columns = [[] for _ in range(8)]
    for pair in range(pairs):
        for side, part in enumerate(load_pair(sc, orders, (sc[4], sc[5]), keep_ref, got_ref, pair)):
            piece = 2 * pair + side
            count = min(rows, D - (piece // 8) * rows)
            if count > 0:
                columns[piece % 8].append(part[:count].astype(F32))
    full = [jnp.concatenate(parts, 0) if len(parts) > 1 else parts[0] for parts in columns]
    spot = D // 128
    for i in range(spot):
        q_ref[:, i * 128 : (i + 1) * 128] = full[i]
    q_ref[:, spot * 128 :] = full[spot][:, : D - spot * 128]
    gain_ref[...] = full[spot].T[D - spot * 128]
    key_value = jnp.concatenate(full[spot + 1 :], 1).T
    k_ref[...] = key_value[:KVD]
    v_ref[...] = key_value[KVD:]


def unpack_small(sc, keep, got, orders):
    shapes = [(D, D), (KVD, D), (KVD, D), (D,)]
    kernel = functools.partial(unpack_small_kernel, orders=orders)
    return call(kernel, "unpack_small", 12, sc, (keep, got), [(shape, F32) for shape in shapes])


def plus(*parts):
    total = parts[0].astype(F32)
    for part in parts[1:]:
        total = total + part.astype(F32)
    return total.astype(BF16)


def swap(values, step):
    grp_size, seq_size = lax.axis_size("grp"), lax.axis_size("seq")
    moves = [(i, i ^ step[i & 1]) for i in range(grp_size * seq_size)]
    spot = [(i % seq_size) * grp_size + i // seq_size for i in range(grp_size * seq_size)]
    return lax.ppermute(values, ("seq", "grp"), [(spot[i], spot[j]) for i, j in moves])


def exchanged(kept, sent, step, gate=None):
    got = after(swap(sent, step), gate)
    half = kept.shape[0] // 2
    if half == 0:
        return plus(kept, got), None
    return plus(kept[:half], got[:half]), plus(kept[half:], got[half:])


def doubled(values, step, gate=None):
    return jnp.concatenate([values, after(swap(values, step), gate)], 0)


def spread_bits(value, places):
    count = len(places)
    total = 0
    for t, bit in enumerate(places):
        total = total | (((value >> bit) & 1) << (count - 1 - t))
    return total


def after(value, other):
    return value if other is None else lax.optimization_barrier((value, other))[0]


def build(seq_size, grp_size):
    count = seq_size * grp_size
    chips = seq_size // 2
    core = (1, 1)
    seq_bits = seq_size.bit_length() - 1
    chip_bits = list(range(1, seq_bits))
    grp_bits = list(range(seq_bits, count.bit_length() - 1))
    routes = [grp_bits + chip_bits, grp_bits[::-1] + chip_bits[::-1]]
    big_steps = [(1 << one, 1 << two) for one, two in zip(*routes)]
    grp_moves = [(i, (i * seq_size, i * seq_size)) for i in range(1, grp_size)]
    chip_steps = big_steps[len(grp_bits) :]
    big_places = [[bit - 1 for bit in route] for route in routes]
    big_orders = [[spread_bits(j, spots) for j in range(count // 2)] for spots in big_places]
    small_orders = [list(range(grp_size))] * 2

    def shards(
        inputs,
        lengths,
        attn_gain,
        w_query,
        w_key,
        w_value,
        w_out,
        ffn_gain,
        w_gate,
        w_up,
        w_down,
        cotangent,
    ):
        rows = inputs.shape[1]
        mine = lax.axis_index("seq")
        group = lax.axis_index("grp")
        number = group * chips + lax.shift_right_logical(mine, 1)
        low = (mine & 1) == 0
        one, two = [spread_bits(number, spots) for spots in big_places]
        spots = [jnp.where(low, one, two), jnp.where(low, two, one), group, group]
        sc = jnp.stack([mine, lengths[0]] + spots).astype(jnp.int32)
        cos_np, sin_np = rope_tables(rows * seq_size)
        cos = jnp.asarray(cos_np)
        sin = jnp.asarray(sin_np)
        x = inputs[0].T
        cot = cotangent[0].T
        wk = w_key.T
        wv = w_value.T
        wd = w_down.T

        down = [(i + 2, i) for i in range(seq_size - 2)]
        normed, own = with_tables(
            keys_kernel,
            "keys",
            sc,
            (x, attn_gain, wk, wv),
            cos,
            sin,
            [(D, rows), (2 * KVD, rows)],
        )
        [query] = with_tables(
            query_kernel, "query", sc, (normed, w_query), cos, sin, [(D, rows)]
        )
        up = [(i, i + 2) for i in range(seq_size - 2)]
        pairs = []
        state = None
        block = own
        for rank in range(chips):
            gate = None if state is None else state[0]
            pairs.append((block, swap(after(block, gate), core)))
            if rank + 1 < chips:
                block = lax.ppermute(block, "seq", up)
            for which in (0, 1):
                state = forward(sc, query, pairs[-1][which], state, rank, which)
        m, l, acc = state
        outputs, d_mixed, lse, delta, d_resid, big, send = middle(
            sc, acc, m, l, x, cot, ffn_gain, w_out, w_gate, w_up, wd, big_orders
        )
        stages = [functools.partial(exchanged, step=step) for step in [core] + big_steps]
        when = [1, 4, 5, 6] + list(range(7, 2 * seq_size))
        dq = None
        passed = None
        calls = 0
        for rank in reversed(range(chips)):
            grads = [None, None]
            for which in (1, 0):
                if calls in when and stages:
                    big, send = stages.pop(0)(big, send, gate=dq)
                    dq = after(dq, big)
                dq, grads[which] = backward(
                    sc, query, d_mixed, lse, delta, pairs[rank][which], dq, rank, which
                )
                calls += 1
            terms = [grads[0], swap(grads[1], core)]
            if passed is not None:
                terms.append(lax.ppermute(passed, "seq", down))
            passed = plus(*terms)
            dq = after(dq, passed)
        for stage in stages:
            big, send = stage(big, send, gate=dq)
        dq = after(dq, big)

        d_inputs, small, small_send = last(
            sc, dq, passed, normed, x, d_resid, attn_gain, w_query, wk, wv, cos, sin, small_orders
        )
        big = doubled(big, big_steps[-1], small_send)
        small_send = after(small_send, big)
        small = plus(small, swap(small_send, core))
        small = plus(small[:1], *[swap(small[i : i + 1], step) for i, step in grp_moves])
        gate = small
        for step in chip_steps:
            small = plus(small, swap(small, step))
        for step in big_steps[-2:0:-1]:
            big = doubled(big, step, gate)
        far = after(swap(big, big_steps[0]), small)
        others = [swap(small, step) for _, step in grp_moves]
        d_gate, d_up, d_down, d_out, d_ffn_gain = unpack_big(
            sc, (big, far), (swap(big, core), swap(far, core)), big_orders
        )
        others = [after(other, d_ffn_gain) for other in others]
        small = jnp.concatenate([small] + others, 0)
        d_query, d_key, d_value, d_attn_gain = unpack_small(
            sc, small, swap(small, core), small_orders
        )
        return (
            outputs.T[None],
            d_inputs.T[None],
            d_attn_gain,
            d_query,
            d_key.T,
            d_value.T,
            d_out,
            d_ffn_gain.reshape(D),
            d_gate,
            d_up,
            d_down.T,
        )

    return shards


def solution(mesh):
    tokens = P("grp", "seq", None)
    return jax.shard_map(
        build(mesh.shape["seq"], mesh.shape["grp"]),
        mesh=mesh,
        in_specs=(tokens, P("grp")) + (P(),) * 9 + (tokens,),
        out_specs=(tokens, tokens) + (P(),) * 9,
        check_vma=False,
    )
```

```python
import functools
import math

import jax
import jax.numpy as jnp
import numpy as np
from jax import lax
from jax.experimental import pallas as pl
from jax.experimental.pallas import tpu as pltpu
from jax.sharding import PartitionSpec as P

D = 576
KV_HEADS = 3
HEAD_DIM = 64
REP = 3
HEADS = KV_HEADS * REP
KVD = 192
FF = 1536
CHUNK = 512
STACK = 2048
PART = 384
HALF = HEAD_DIM // 2

epsilon = 1e-05
rope_base = 100000.0
neg_big = -1e30
log2e = math.log2(math.e)
ln2 = math.log(2.0)

F32 = jnp.float32
BF16 = jnp.bfloat16


def mm(left, right, left_dim, right_dim):
    return lax.dot_general(
        left, right, (((left_dim,), (right_dim,)), ((), ())), preferred_element_type=F32
    )


def params(mebibytes):
    return pltpu.CompilerParams(vmem_limit_bytes=mebibytes * 2**20)


def whole(shape):
    return pl.BlockSpec(shape, lambda *_: (0,) * len(shape))


def call(kernel, name, limit, sc, args, outs, scratch=(), aliases=None):
    return pl.pallas_call(
        kernel,
        in_specs=[pl.BlockSpec(memory_space=pltpu.SMEM)]
        + [pl.BlockSpec(memory_space=pltpu.VMEM)] * len(args),
        out_specs=[pl.BlockSpec(memory_space=pltpu.VMEM)] * len(outs),
        out_shape=[jax.ShapeDtypeStruct(*out) for out in outs],
        scratch_shapes=list(scratch),
        input_output_aliases=aliases or {},
        compiler_params=params(limit),
        cost_estimate=cost(),
        name=name,
    )(sc, *args)


def cost():
    return pl.CostEstimate(flops=10**8, bytes_accessed=2**17, transcendentals=0)


def rope_tables(length):
    steps = np.arange(HALF, dtype=np.float32)
    freqs = (1.0 / np.float32(rope_base) ** (steps * np.float32(2.0) / np.float32(HEAD_DIM))).astype(
        np.float32
    )
    angles = np.arange(length, dtype=np.float32)[None, :] * freqs[:, None]
    return np.cos(angles).astype(np.float32), np.sin(angles).astype(np.float32)


def rotated(rows, cos, sin, scale, sign):
    parts = []
    for start in range(0, rows.shape[0], HEAD_DIM):
        one = rows[start : start + HALF]
        two = rows[start + HALF : start + HEAD_DIM]
        parts.append((one * cos - sign * (two * sin)) * scale)
        parts.append((two * cos + sign * (one * sin)) * scale)
    return jnp.concatenate(parts, 0)


def column(vector):
    return jnp.broadcast_to(vector[None], (8, vector.shape[0])).T[:, :1]


def keys_kernel(sc, x_ref, gain_ref, wk_ref, wv_ref, cos_ref, sin_ref, n_ref, kv_ref):
    x = x_ref[...].astype(F32)
    scale = lax.rsqrt(jnp.mean(x * x, axis=0, keepdims=True) + epsilon)
    normed = (x * scale * column(gain_ref[...])).astype(BF16)
    n_ref[...] = normed
    key = mm(wk_ref[...], normed, 1, 0)
    kv_ref[:KVD, :] = rotated(key, cos_ref[...], sin_ref[...], 1.0, 1.0).astype(BF16)
    kv_ref[KVD:, :] = mm(wv_ref[...], normed, 1, 0).astype(BF16)


def query_kernel(sc, n_ref, wq_ref, cos_ref, sin_ref, q_ref):
    query = mm(wq_ref[...].T, n_ref[...], 1, 0)
    q_ref[...] = rotated(
        query, cos_ref[...], sin_ref[...], HEAD_DIM**-0.5 * log2e, 1.0
    ).astype(BF16)


def with_tables(kernel, name, sc, args, cos, sin, outs):
    rows = args[0].shape[1]
    table = pl.BlockSpec((HALF, rows), lambda i, sc: (0, sc[0]))
    return pl.pallas_call(
        kernel,
        grid_spec=pltpu.PrefetchScalarGridSpec(
            num_scalar_prefetch=1,
            grid=(1,),
            in_specs=[whole(part.shape) for part in args] + [table, table],
            out_specs=[whole(shape) for shape in outs],
        ),
        out_shape=[jax.ShapeDtypeStruct(shape, BF16) for shape in outs],
        compiler_params=params(56),
        cost_estimate=cost(),
        name=name,
    )(sc, *args, cos, sin)


def block_facts(sc, rank, which, rows):
    mine = sc[0]
    block = mine - 2 * rank if which == 0 else (mine ^ 1) - 2 * rank
    length = sc[1]
    start = block * rows
    active = (block >= 0) & (block <= mine) & (start < length)
    partial = (block == mine) | (start + rows > length)
    pos = mine * rows + lax.broadcasted_iota(jnp.int32, (1, rows), 1)
    bound = jnp.minimum(pos, length - 1) - start
    return active, partial, bound


def masked_scores(scores, bound):
    rows = lax.broadcasted_iota(jnp.int32, scores.shape, 0)
    return jnp.where(rows <= bound, scores, neg_big)


def forward_block(hidden_keys, bound, k_ref, v_ref, q_ref, m_ref, l_ref, acc_ref):
    rows = q_ref.shape[1]
    keys = k_ref[...].T
    ones = jnp.ones((8, rows), BF16)

    def score(head):
        kv = head // REP
        scores = mm(
            keys[:, kv * HEAD_DIM : (kv + 1) * HEAD_DIM],
            q_ref[head * HEAD_DIM : (head + 1) * HEAD_DIM, :],
            1,
            0,
        )
        if hidden_keys:
            scores = masked_scores(scores, bound)
        return scores, jnp.max(scores, axis=0, keepdims=True)

    def weigh(head, scores, top):
        kv = head // REP
        old = m_ref[head : head + 1, :]
        new = jnp.maximum(old, top)
        weights = jnp.exp2(scores - new).astype(BF16)
        values = jnp.concatenate(
            [v_ref[kv * HEAD_DIM : (kv + 1) * HEAD_DIM, :], ones], 0
        )
        return new, jnp.exp2(old - new), mm(values, weights, 1, 0)

    def store(head, new, fade, out):
        rows_of = slice(head * HEAD_DIM, (head + 1) * HEAD_DIM)
        m_ref[head : head + 1, :] = new
        l_ref[head : head + 1, :] = l_ref[head : head + 1, :] * fade + out[HEAD_DIM : HEAD_DIM + 1]
        acc_ref[rows_of, :] = acc_ref[rows_of, :] * fade + out[:HEAD_DIM]

    ahead = score(0)
    held = None
    for head in range(HEADS):
        current = ahead
        if head + 1 < HEADS:
            ahead = score(head + 1)
        result = weigh(head, *current)
        if held is not None:
            store(*held)
        held = (head,) + result
    store(*held)


def forward_kernel(sc, q_ref, kv_ref, *refs, rank, which):
    k_ref, v_ref = kv_ref.at[:KVD], kv_ref.at[KVD:]
    m_ref, l_ref, acc_ref = refs[-3:]
    if len(refs) == 3:
        m_ref[...] = jnp.full_like(m_ref, neg_big)
        l_ref[...] = jnp.zeros_like(l_ref)
        acc_ref[...] = jnp.zeros_like(acc_ref)
    active, partial, bound = block_facts(sc, rank, which, q_ref.shape[1])

    @pl.when(active & jnp.logical_not(partial))
    def _():
        forward_block(False, bound, k_ref, v_ref, q_ref, m_ref, l_ref, acc_ref)

    @pl.when(active & partial)
    def _():
        forward_block(True, bound, k_ref, v_ref, q_ref, m_ref, l_ref, acc_ref)


def forward(sc, q, block, state, rank, which):
    rows = q.shape[1]
    state = () if state is None else tuple(state)
    kernel = functools.partial(forward_kernel, rank=rank, which=which)
    outs = [((16, rows), F32), ((16, rows), F32), ((D, rows), F32)]
    aliases = {3: 0, 4: 1, 5: 2} if state else None
    return call(
        kernel, f"forward_{rank}_{which}", 12, sc, (q, block, *state), outs, aliases=aliases
    )


def backward_block(
    hidden_keys, bound, k_ref, v_ref, q_ref, do_ref, lse_ref, delta_ref, dq_ref, out_ref, causal=False
):
    rows = q_ref.shape[1]
    keys = k_ref[...].T
    values = v_ref[...].T
    half = rows // 2
    spans = [(slice(0, half), half), (slice(half, rows), rows)] if causal else [(slice(0, rows), rows)]
    units = [(head, span) for head in range(HEADS) for span in range(len(spans))]

    def start(head, span):
        columns, count = spans[span]
        kv = head // REP
        lanes = slice(kv * HEAD_DIM, (kv + 1) * HEAD_DIM)
        rows_of = slice(head * HEAD_DIM, (head + 1) * HEAD_DIM)
        scores = mm(keys[:count, lanes], q_ref[rows_of, columns], 1, 0)
        if hidden_keys:
            scores = masked_scores(scores, bound[:, columns])
        return scores, mm(values[:count, lanes], do_ref[rows_of, columns], 1, 0)

    ahead = [start(*unit) for unit in units[:2]]
    sums = {}
    for i, (head, span) in enumerate(units):
        columns, count = spans[span]
        kv = head // REP
        rows_of = slice(head * HEAD_DIM, (head + 1) * HEAD_DIM)
        scores, d_probs = ahead.pop(0)
        if i + 2 < len(units):
            ahead.append(start(*units[i + 2]))
        probs = jnp.exp2(scores - lse_ref[head : head + 1, columns])
        d_scores = (probs * (d_probs - delta_ref[head : head + 1, columns])).astype(BF16)
        value_term = mm(probs.astype(BF16), do_ref[rows_of, columns], 1, 1)
        key_term = mm(d_scores, q_ref[rows_of, columns], 1, 1)
        if span in sums:
            sums[span] = (sums[span][0] + key_term, sums[span][1] + value_term)
        else:
            sums[span] = (key_term, value_term)
        dq_ref[rows_of, columns] = dq_ref[rows_of, columns] + mm(
            k_ref[kv * HEAD_DIM : (kv + 1) * HEAD_DIM, :count], d_scores, 1, 0
        )
        if head % REP == REP - 1 and span == len(spans) - 1:
            full = jnp.concatenate(sums[span], 1)
            if causal:
                out_ref[kv, :half] = (full[:half] + jnp.concatenate(sums[0], 1)).astype(BF16)
                out_ref[kv, half:] = full[half:].astype(BF16)
            else:
                out_ref[kv] = full.astype(BF16)
            sums = {}


def backward_kernel(sc, q_ref, do_ref, lse_ref, delta_ref, kv_ref, *refs, rank, which):
    k_ref, v_ref = kv_ref.at[:KVD], kv_ref.at[KVD:]
    dq_ref, out_ref = refs[-2:]
    if len(refs) == 2:
        dq_ref[...] = jnp.zeros_like(dq_ref)
    active, partial, bound = block_facts(sc, rank, which, q_ref.shape[1])
    rest = (k_ref, v_ref, q_ref, do_ref, lse_ref, delta_ref, dq_ref, out_ref)

    if rank == 0 and which == 0:

        @pl.when(active)
        def _():
            backward_block(True, bound, *rest, causal=True)

    else:

        @pl.when(active & jnp.logical_not(partial))
        def _():
            backward_block(False, bound, *rest)

        @pl.when(active & partial)
        def _():
            backward_block(True, bound, *rest)

    @pl.when(jnp.logical_not(active))
    def _():
        out_ref[...] = jnp.zeros_like(out_ref)


def backward(sc, q, d_out, lse, delta, kv, dq, rank, which):
    rows = q.shape[1]
    args = (q, d_out, lse, delta, kv) + (() if dq is None else (dq,))
    grads = (KV_HEADS, rows, 2 * HEAD_DIM)
    kernel = functools.partial(backward_kernel, rank=rank, which=which)
    outs = [((D, rows), F32), (grads, BF16)]
    aliases = None if dq is None else {len(args): 0}
    return call(kernel, f"backward_{rank}_{which}", 12, sc, args, outs, aliases=aliases)


def place(sc, orders, spot, pair):
    return jnp.where((sc[0] & 1) == 0, orders[0][pair], orders[1][pair]) ^ spot


def store_pieces(sc, orders, spot, keep_ref, send_ref, piece_of):
    low = (sc[0] & 1) == 0
    for pair in range(keep_ref.shape[0]):
        even = piece_of(2 * pair)
        odd = piece_of(2 * pair + 1)
        keep_ref[place(sc, orders, spot[0], pair)] = jnp.where(low, even, odd)
        send_ref[place(sc, orders[::-1], spot[1], pair)] = jnp.where(low, odd, even)


def load_pair(sc, orders, spot, keep_ref, got_ref, pair):
    low = (sc[0] & 1) == 0

    def load(refs, where):
        if not isinstance(refs, tuple):
            return refs[where]
        half = refs[0].shape[0]
        inside = where & (half - 1)
        return jnp.where(where < half, refs[0][inside], refs[1][inside])

    one = load(keep_ref, place(sc, orders, spot[0], pair))
    two = load(got_ref, place(sc, orders[::-1], spot[1], pair))
    return jnp.where(low, one, two), jnp.where(low, two, one)


def middle_kernel(
    sc,
    acc_ref,
    m_ref,
    l_ref,
    x_ref,
    cot_ref,
    gain_ref,
    wo_ref,
    wg_ref,
    wu_ref,
    wd_ref,
    y_ref,
    do_ref,
    lse_ref,
    delta_ref,
    dh_ref,
    keep_ref,
    send_ref,
    mixed_ref,
    stack_ref,
    hid_ref,
    dg_ref,
    du_ref,
    *,
    orders,
):
    for head in range(HEADS):
        rows_of = slice(head * HEAD_DIM, (head + 1) * HEAD_DIM)
        mixed_ref[rows_of, :] = acc_ref[rows_of, :] * (1.0 / l_ref[head : head + 1, :])
    lse_ref[:HEADS, :] = m_ref[:HEADS, :] + jnp.log2(l_ref[:HEADS, :])
    gain = column(gain_ref[...])
    cot_t = cot_ref[...]
    cot = cot_t.T
    mixed_low = mixed_ref[...].astype(BF16)
    h = x_ref[...].astype(F32) + mm(wo_ref[...].T, mixed_low, 1, 0)
    scale = lax.rsqrt(jnp.mean(h * h, axis=0, keepdims=True) + epsilon)
    normed_t = (h * scale * gain).astype(BF16)
    normed = normed_t.T

    def start(chunk):
        cols = slice(chunk * CHUNK, (chunk + 1) * CHUNK)
        return (
            mm(normed, wg_ref[:, cols], 1, 0),
            mm(normed, wu_ref[:, cols], 1, 0),
            mm(cot, wd_ref[:, cols], 1, 0),
        )

    chunks = FF // CHUNK
    ahead = start(0)
    for chunk in range(chunks):
        gate, up, d_hidden = ahead
        if chunk + 1 < chunks:
            ahead = start(chunk + 1)
        cols = slice(chunk * CHUNK, (chunk + 1) * CHUNK)
        sig = 1.0 / (1.0 + jnp.exp2(gate * -log2e))
        silu = gate * sig
        hidden = (silu * up).astype(BF16)
        d_gate = (d_hidden * up * (sig * (1.0 + gate * (1.0 - sig)))).astype(BF16)
        d_up = (d_hidden * silu).astype(BF16)
        hid_ref[:, cols] = hidden
        dg_ref[:, cols] = d_gate
        du_ref[:, cols] = d_up
        stack_ref[:D, cols] = mm(normed_t, d_gate, 1, 0).astype(BF16)
        stack_ref[D : 2 * D, cols] = mm(normed_t, d_up, 1, 0).astype(BF16)
        stack_ref[2 * D : 3 * D, cols] = mm(cot_t, hidden, 1, 0).astype(BF16)
    y_ref[...] = (h + mm(wd_ref[...], hid_ref[...], 1, 1)).astype(BF16)
    dn = mm(wg_ref[...], dg_ref[...], 1, 1) + mm(wu_ref[...], du_ref[...], 1, 1)
    unit = h * scale
    gain_sum = jnp.sum(dn * unit, axis=1, keepdims=True)
    scaled = dn * gain
    dh = cot_t.astype(F32) + scale * (
        scaled - unit * jnp.mean(scaled * unit, axis=0, keepdims=True)
    )
    dh_ref[...] = dh
    dh_low = dh.astype(BF16)
    mixed = mixed_ref[...]
    d_mixed = mm(wo_ref[...], dh_low, 1, 0).astype(BF16)
    do_ref[...] = d_mixed
    for head in range(HEADS):
        rows_of = slice(head * HEAD_DIM, (head + 1) * HEAD_DIM)
        delta_ref[head : head + 1, :] = jnp.sum(
            d_mixed[rows_of].astype(F32) * mixed[rows_of], axis=0, keepdims=True
        )
    d_wo = mm(mixed_low, dh_low, 1, 1).astype(BF16)
    gain_row = jnp.broadcast_to(gain_sum, (D, 128)).T[:16].astype(BF16)
    quarter = D // 4
    base = 3 * D
    for k in range(4):
        cols = slice(k * PART, (k + 1) * PART)
        part = d_wo[k * quarter : (k + 1) * quarter]
        stack_ref[base : base + quarter, cols] = part[:, :PART]
        stack_ref[base + quarter : base + 2 * quarter, cols] = jnp.concatenate(
            [part[:, PART:], jnp.zeros((quarter, 2 * PART - D), BF16)], 1
        )
        stack_ref[base + 2 * quarter :, cols] = jnp.zeros((STACK - base - 2 * quarter, PART), BF16)
    stack_ref[base + 2 * quarter : base + 2 * quarter + 16, :D] = gain_row
    rows = keep_ref.shape[1]
    store_pieces(
        sc,
        orders,
        (sc[2], sc[3]),
        keep_ref,
        send_ref,
        lambda p: stack_ref[p * rows : (p + 1) * rows, :],
    )


def middle(sc, acc, m, l, x, cot, gain, wo, wg, wu, wd, orders):
    rows = x.shape[1]
    pairs = len(orders[0])
    half = (pairs, STACK // (2 * pairs), FF)
    args = (acc, m, l, x, cot, gain, wo, wg, wu, wd)
    outs = [
        ((D, rows), BF16),
        ((D, rows), BF16),
        ((16, rows), F32),
        ((16, rows), F32),
        ((D, rows), F32),
        (half, BF16),
        (half, BF16),
    ]
    scratch = [
        pltpu.VMEM((D, rows), F32),
        pltpu.VMEM((STACK, FF), BF16),
        pltpu.VMEM((rows, FF), BF16),
        pltpu.VMEM((rows, FF), BF16),
        pltpu.VMEM((rows, FF), BF16),
    ]
    kernel = functools.partial(middle_kernel, orders=orders)
    return call(kernel, "middle", 34, sc, args, outs, scratch)


def last_kernel(
    sc,
    dq_ref,
    dkv_ref,
    n_ref,
    x_ref,
    dh_ref,
    gain_ref,
    wq_ref,
    wk_ref,
    wv_ref,
    cos_ref,
    sin_ref,
    dx_ref,
    keep_ref,
    send_ref,
    *,
    orders,
):
    cos = cos_ref[...]
    sin = sin_ref[...]
    rows = x_ref.shape[1]
    d_query = rotated(dq_ref[...], cos, sin, HEAD_DIM**-0.5, -1.0).astype(BF16)
    turned = [dkv_ref[kv].astype(F32).T for kv in range(KV_HEADS)]
    d_key = rotated(
        jnp.concatenate([part[:HEAD_DIM] for part in turned], 0), cos, sin, ln2, -1.0
    ).astype(BF16)
    d_value = jnp.concatenate([part[HEAD_DIM:] for part in turned], 0).astype(BF16)
    dn = (
        mm(wq_ref[...], d_query, 1, 0)
        + mm(wk_ref[...], d_key, 0, 0)
        + mm(wv_ref[...], d_value, 0, 0)
    )
    x = x_ref[...].astype(F32)
    scale = lax.rsqrt(jnp.mean(x * x, axis=0, keepdims=True) + epsilon)
    unit = x * scale
    scaled = dn * column(gain_ref[...])
    dx_ref[...] = (
        dh_ref[...] + scale * (scaled - unit * jnp.mean(scaled * unit, axis=0, keepdims=True))
    ).astype(BF16)
    pad = 64
    joined = jnp.concatenate([d_query, jnp.zeros((pad, rows), BF16), d_key, d_value], 0)
    grad = mm(n_ref[...], joined, 1, 1)
    gain_sum = jnp.sum(dn * unit, axis=1, keepdims=True)
    spot = D // 128
    lane = lax.broadcasted_iota(jnp.int32, (D, 128), 1)
    mixed = jnp.where(
        lane < D - spot * 128, grad[:, spot * 128 : (spot + 1) * 128], gain_sum
    )
    tiles = [
        (mixed if i == spot else grad[:, i * 128 : (i + 1) * 128]).astype(BF16) for i in range(8)
    ]
    piece_rows = keep_ref.shape[1]

    def piece_of(piece):
        top = (piece // 8) * piece_rows
        count = max(min(piece_rows, D - top), 0)
        empty = jnp.zeros((piece_rows - count, 128), BF16)
        if count == 0:
            return empty
        part = tiles[piece % 8][top : top + count]
        return jnp.concatenate([part, empty], 0) if count < piece_rows else part

    store_pieces(sc, orders, (sc[4], sc[5]), keep_ref, send_ref, piece_of)


def last(sc, dq, dkv, n, x, dh, gain, wq, wk, wv, cos, sin, orders):
    pieces = 2 * len(orders[0])
    rows = x.shape[1]
    piece_rows = -(-D // max(pieces // 8, 1))
    half = (pieces // 2, -(-piece_rows // 16) * 16, 128)
    table = pl.BlockSpec((HALF, rows), lambda i, sc: (0, sc[0]))
    return pl.pallas_call(
        functools.partial(last_kernel, orders=orders),
        grid_spec=pltpu.PrefetchScalarGridSpec(
            num_scalar_prefetch=1,
            grid=(1,),
            in_specs=[whole(part.shape) for part in (dq, dkv, n, x, dh, gain, wq, wk, wv)]
            + [table, table],
            out_specs=[whole((D, rows)), whole(half), whole(half)],
        ),
        out_shape=[
            jax.ShapeDtypeStruct((D, rows), BF16),
            jax.ShapeDtypeStruct(half, BF16),
            jax.ShapeDtypeStruct(half, BF16),
        ],
        compiler_params=params(24),
        cost_estimate=cost(),
        name="last",
    )(sc, dq, dkv, n, x, dh, gain, wq, wk, wv, cos, sin)


def unpack_big_kernel(
    sc, keep_ref, far_ref, got_ref, got_far_ref, gate_ref, up_ref, down_ref, wo_ref, gain_ref, *, orders
):
    step = pl.program_id(0)
    quarter = D // 4
    refs = (gate_ref, up_ref, down_ref)
    pairs, rows = 2 * keep_ref.shape[0], keep_ref.shape[1]
    kept, got = (keep_ref, far_ref), (got_ref, got_far_ref)
    rest = []
    for pair in range(pairs):
        for side, part in enumerate(load_pair(sc, orders, (sc[2], sc[3]), kept, got, pair)):
            part = part.astype(F32)
            top = (2 * pair + side) * rows
            if top < 3 * D:
                refs[top // D][top % D : top % D + rows, :] = part
            else:
                rest.append(part)
    rest = jnp.concatenate(rest, 0)
    wo_ref[:, :PART] = rest[:quarter]
    wo_ref[:, PART:] = rest[quarter : 2 * quarter, : D - PART]
    row = rest[2 * quarter : 2 * quarter + 1]

    @pl.when(step == 0)
    def _():
        gain_ref[:, :PART] = row

    @pl.when(step == 1)
    def _():
        gain_ref[:, PART:] = row[:, : D - PART]


def unpack_big(sc, keep, got, orders):
    shapes = [(D, FF), (D, FF), (D, FF), (D, D), (1, D)]
    cols = pl.BlockSpec((D, PART), lambda i, sc: (0, i))
    part = pl.BlockSpec(keep[0].shape[:2] + (PART,), lambda i, sc: (0, 0, i))
    return pl.pallas_call(
        functools.partial(unpack_big_kernel, orders=orders),
        grid_spec=pltpu.PrefetchScalarGridSpec(
            num_scalar_prefetch=1,
            grid=(FF // PART,),
            in_specs=[part] * 4,
            out_specs=[
                cols,
                cols,
                cols,
                pl.BlockSpec((D // 4, D), lambda i, sc: (i, 0)),
                whole((1, D)),
            ],
        ),
        out_shape=[jax.ShapeDtypeStruct(shape, F32) for shape in shapes],
        compiler_params=params(32),
        cost_estimate=cost(),
        name="unpack_big",
    )(sc, *keep, *got)


def unpack_small_kernel(sc, keep_ref, got_ref, q_ref, k_ref, v_ref, gain_ref, *, orders):
    pairs, rows, _ = keep_ref.shape
    columns = [[] for _ in range(8)]
    for pair in range(pairs):
        for side, part in enumerate(load_pair(sc, orders, (sc[4], sc[5]), keep_ref, got_ref, pair)):
            piece = 2 * pair + side
            count = min(rows, D - (piece // 8) * rows)
            if count > 0:
                columns[piece % 8].append(part[:count].astype(F32))
    full = [jnp.concatenate(parts, 0) if len(parts) > 1 else parts[0] for parts in columns]
    spot = D // 128
    for i in range(spot):
        q_ref[:, i * 128 : (i + 1) * 128] = full[i]
    q_ref[:, spot * 128 :] = full[spot][:, : D - spot * 128]
    gain_ref[...] = full[spot].T[D - spot * 128]
    key_value = jnp.concatenate(full[spot + 1 :], 1).T
    k_ref[...] = key_value[:KVD]
    v_ref[...] = key_value[KVD:]


def unpack_small(sc, keep, got, orders):
    shapes = [(D, D), (KVD, D), (KVD, D), (D,)]
    kernel = functools.partial(unpack_small_kernel, orders=orders)
    return call(kernel, "unpack_small", 12, sc, (keep, got), [(shape, F32) for shape in shapes])


def plus(*parts):
    total = parts[0].astype(F32)
    for part in parts[1:]:
        total = total + part.astype(F32)
    return total.astype(BF16)


def swap(values, step):
    grp_size, seq_size = lax.axis_size("grp"), lax.axis_size("seq")
    moves = [(i, i ^ step[i & 1]) for i in range(grp_size * seq_size)]
    spot = [(i % seq_size) * grp_size + i // seq_size for i in range(grp_size * seq_size)]
    return lax.ppermute(values, ("seq", "grp"), [(spot[i], spot[j]) for i, j in moves])


def exchanged(kept, sent, step, gate=None):
    got = after(swap(sent, step), gate)
    half = kept.shape[0] // 2
    if half == 0:
        return plus(kept, got), None
    return plus(kept[:half], got[:half]), plus(kept[half:], got[half:])


def doubled(values, step, gate=None):
    return jnp.concatenate([values, after(swap(values, step), gate)], 0)


def spread_bits(value, places):
    count = len(places)
    total = 0
    for t, bit in enumerate(places):
        total = total | (((value >> bit) & 1) << (count - 1 - t))
    return total


def after(value, other):
    return value if other is None else lax.optimization_barrier((value, other))[0]


def build(seq_size, grp_size):
    count = seq_size * grp_size
    chips = seq_size // 2
    core = (1, 1)
    seq_bits = seq_size.bit_length() - 1
    chip_bits = list(range(1, seq_bits))
    grp_bits = list(range(seq_bits, count.bit_length() - 1))
    routes = [grp_bits + chip_bits, grp_bits[::-1] + chip_bits[::-1]]
    big_steps = [(1 << one, 1 << two) for one, two in zip(*routes)]
    grp_moves = [(i, (i * seq_size, i * seq_size)) for i in range(1, grp_size)]
    chip_steps = big_steps[len(grp_bits) :]
    big_places = [[bit - 1 for bit in route] for route in routes]
    big_orders = [[spread_bits(j, spots) for j in range(count // 2)] for spots in big_places]
    small_orders = [list(range(grp_size))] * 2

    def shards(
        inputs,
        lengths,
        attn_gain,
        w_query,
        w_key,
        w_value,
        w_out,
        ffn_gain,
        w_gate,
        w_up,
        w_down,
        cotangent,
    ):
        rows = inputs.shape[1]
        mine = lax.axis_index("seq")
        group = lax.axis_index("grp")
        number = group * chips + lax.shift_right_logical(mine, 1)
        low = (mine & 1) == 0
        one, two = [spread_bits(number, spots) for spots in big_places]
        spots = [jnp.where(low, one, two), jnp.where(low, two, one), group, group]
        sc = jnp.stack([mine, lengths[0]] + spots).astype(jnp.int32)
        cos_np, sin_np = rope_tables(rows * seq_size)
        cos = jnp.asarray(cos_np)
        sin = jnp.asarray(sin_np)
        x = inputs[0].T
        cot = cotangent[0].T
        wk = w_key.T
        wv = w_value.T
        wd = w_down.T

        down = [(i + 2, i) for i in range(seq_size - 2)]
        normed, own = with_tables(
            keys_kernel,
            "keys",
            sc,
            (x, attn_gain, wk, wv),
            cos,
            sin,
            [(D, rows), (2 * KVD, rows)],
        )
        [query] = with_tables(
            query_kernel, "query", sc, (normed, w_query), cos, sin, [(D, rows)]
        )
        up = [(i, i + 2) for i in range(seq_size - 2)]
        pairs = []
        state = None
        block = own
        for rank in range(chips):
            gate = None if state is None else state[0]
            pairs.append((block, swap(after(block, gate), core)))
            if rank + 1 < chips:
                block = lax.ppermute(block, "seq", up)
            for which in (0, 1):
                state = forward(sc, query, pairs[-1][which], state, rank, which)
        m, l, acc = state
        outputs, d_mixed, lse, delta, d_resid, big, send = middle(
            sc, acc, m, l, x, cot, ffn_gain, w_out, w_gate, w_up, wd, big_orders
        )
        stages = [functools.partial(exchanged, step=step) for step in [core] + big_steps]
        when = [1, 4, 5, 6] + list(range(7, 2 * seq_size))
        dq = None
        passed = None
        calls = 0
        for rank in reversed(range(chips)):
            grads = [None, None]
            for which in (1, 0):
                if calls in when and stages:
                    big, send = stages.pop(0)(big, send, gate=dq)
                    dq = after(dq, big)
                dq, grads[which] = backward(
                    sc, query, d_mixed, lse, delta, pairs[rank][which], dq, rank, which
                )
                calls += 1
            terms = [grads[0], swap(grads[1], core)]
            if passed is not None:
                terms.append(lax.ppermute(passed, "seq", down))
            passed = plus(*terms)
            dq = after(dq, passed)
        for stage in stages:
            big, send = stage(big, send, gate=dq)
        dq = after(dq, big)

        d_inputs, small, small_send = last(
            sc, dq, passed, normed, x, d_resid, attn_gain, w_query, wk, wv, cos, sin, small_orders
        )
        big = doubled(big, big_steps[-1], small_send)
        small_send = after(small_send, big)
        small = plus(small, swap(small_send, core))
        small = plus(small[:1], *[swap(small[i : i + 1], step) for i, step in grp_moves])
        gate = small
        for step in chip_steps:
            small = plus(small, swap(small, step))
        for step in big_steps[-2:0:-1]:
            big = doubled(big, step, gate)
        far = after(swap(big, big_steps[0]), small)
        others = [swap(small, step) for _, step in grp_moves]
        d_gate, d_up, d_down, d_out, d_ffn_gain = unpack_big(
            sc, (big, far), (swap(big, core), swap(far, core)), big_orders
        )
        others = [after(other, d_ffn_gain) for other in others]
        small = jnp.concatenate([small] + others, 0)
        d_query, d_key, d_value, d_attn_gain = unpack_small(
            sc, small, swap(small, core), small_orders
        )
        return (
            outputs.T[None],
            d_inputs.T[None],
            d_attn_gain,
            d_query,
            d_key.T,
            d_value.T,
            d_out,
            d_ffn_gain.reshape(D),
            d_gate,
            d_up,
            d_down.T,
        )

    return shards


def solution(mesh):
    tokens = P("grp", "seq", None)
    return jax.shard_map(
        build(mesh.shape["seq"], mesh.shape["grp"]),
        mesh=mesh,
        in_specs=(tokens, P("grp")) + (P(),) * 9 + (tokens,),
        out_specs=(tokens, tokens) + (P(),) * 9,
        check_vma=False,
    )
```
